32 devices in a mesh: seq: 8 (over z, core), head: 4 (over y, x).
Axes of the slice: x: 2, y: 2, z: 4, core: 2. Of those that a mesh axis runs over, the one named last changes fastest.
Arguments:
- queries: bfloat16 [3072, 16384], P('seq', 'head'), may hold values from -5 to 5
- keys: bfloat16 [3072, 1024], P('seq', 'head'), may hold values from -5 to 5
- values: bfloat16 [3072, 1024], P('seq', 'head'), may hold values from -6 to 6
- feat_q: bfloat16 [128, 128, 128], P('head'), may hold values from -0.5 to 0.5
- feat_k: bfloat16 [128, 128, 128], P('head'), may hold values from -0.5 to 0.5
Outputs:
- grad_feat_q: float32 [128, 128, 128], P('head')
- grad_feat_k: float32 [128, 128, 128], P('head')
The draws below stay inside these ranges and needn't reach their ends.
All inputs are finite; a program needn't handle non-finite values.
Results may differ from the reference program's by a relative error of at most 0.02.
Values may be sent and summed in bfloat16 or wider, within the bound.
No kernel may reach another device: no remote copies, remote signals or barrier semaphores. Data moves between devices by JAX's collectives and lax.ppermute only.
A program may use at most 128 MiB of HBM per device.

```python
import math
import jax
import jax.numpy as jnp
from jax import lax

HEADS = 128
KV_HEADS = 8
HD = 128
FD = 128
TOK_DEV = 384
TOKENS = 3072


def drawn_inputs(base_key):
    query_seed, key_seed = jax.random.split(jax.random.fold_in(base_key, 1234), 2)
    queries = jax.random.truncated_normal(query_seed, -5.0, 5.0, (TOKENS, HEADS * HD), jnp.float32)
    keys = jax.random.truncated_normal(key_seed, -5.0, 5.0, (TOKENS, KV_HEADS * HD), jnp.float32)
    return (queries, keys)


def draw_queries(key, part):
    return drawn_inputs(key)[0].astype(jnp.bfloat16)


def draw_keys(key, part):
    return drawn_inputs(key)[1].astype(jnp.bfloat16)


def block_scale(stream_key, extent, cuts, low, largest):
    factor_of = 1.0
    for position, parts in cuts:
        steps = jax.random.uniform(jax.random.fold_in(jax.random.fold_in(stream_key, 6), position), (parts,), jnp.float32, low / len(cuts), largest / len(cuts))
        factor_of = factor_of * jnp.repeat(jnp.exp(steps), extent[position] // parts).reshape((-1,) + (1,) * (len(extent) - 1 - position))
    return factor_of


def bell_draw(own_key, dims, scale, limit, shards=(), kind=jnp.bfloat16):
    values = scale * jax.random.normal(own_key, dims, jnp.float32)
    if shards:
        values = values * block_scale(own_key, dims, shards, -0.22, 0.18)
    return jnp.clip(values, -limit, limit).astype(kind)


def setup_inputs(seed: int = 0) -> dict:
    key_of = jax.random.split(jax.random.key(seed), 6)
    return {
        "queries": draw_queries(jax.random.fold_in(key_of[5], 71), 0),
        "keys": draw_keys(jax.random.fold_in(key_of[5], 71), 0),
        "values": bell_draw(key_of[2], (TOKENS, KV_HEADS * HD), 1.0, 6.0, ((0, 8), (1, 4))),
        "feat_q": bell_draw(key_of[3], (HEADS, HD, FD), HD ** -0.5, 0.5, ((0, 4),)),
        "feat_k": bell_draw(key_of[4], (HEADS, HD, FD), HD ** -0.5, 0.5, ((0, 4),)),
    }


HIGHEST_MODE = lax.Precision.HIGHEST
MASKED_SCORE = -1e30


def rounded_wide(entries):
    return lax.optimization_barrier(entries.astype(jnp.bfloat16)).astype(jnp.float32)


def exclusive_sum(stacked):
    totals = jnp.cumsum(stacked, axis=0)
    return jnp.concatenate([jnp.zeros_like(stacked[:1]), totals[:-1]], axis=0)


def teacher_group(query_heads, key_rows, value_rows):
    block_rows = math.gcd(TOKENS, 512)
    score_scale = HD ** -0.5
    pieces = []
    for block_index in range(TOKENS // block_rows):
        finish = (block_index + 1) * block_rows
        query_block = query_heads[:, block_index * block_rows:finish].astype(jnp.float32)
        scores = jnp.einsum("jrd,kd->jrk", query_block, key_rows[:finish].astype(jnp.float32)) * score_scale
        query_pos = block_index * block_rows + jnp.arange(block_rows, dtype=jnp.int32)
        key_pos = jnp.arange(finish, dtype=jnp.int32)
        allowed = (key_pos[None, :] <= query_pos[:, None])[None]
        row_peak = jnp.max(jnp.where(allowed, scores, MASKED_SCORE), axis=-1)
        weights = jnp.exp(jnp.where(allowed, scores - row_peak[..., None], MASKED_SCORE))
        row_total = jnp.sum(weights, axis=-1)
        mixture = jnp.einsum("jrk,kd->jrd", rounded_wide(weights), value_rows[:finish].astype(jnp.float32))
        pieces.append((mixture / row_total[..., None]).astype(jnp.bfloat16))
    return jnp.concatenate(pieces, axis=1)


def student_group(query_heads, key_rows, value_rows, teacher_out, weight_query, weight_key):
    group_size = query_heads.shape[0]
    block_count = TOKENS // TOK_DEV
    query_wide = query_heads.astype(jnp.float32)
    key_wide = key_rows.astype(jnp.float32)
    query_pre = jnp.einsum("jtd,jdf->jtf", query_wide, weight_query.astype(jnp.float32))
    key_pre = jnp.einsum("td,jdf->jtf", key_wide, weight_key.astype(jnp.float32))
    query_feat = rounded_wide(jax.nn.softplus(query_pre))
    key_feat = rounded_wide(jax.nn.softplus(key_pre))

    def split_blocks(entries):
        return entries.reshape(group_size, block_count, TOK_DEV, -1).transpose(1, 0, 2, 3)

    query_blocks = split_blocks(query_feat)
    key_blocks = split_blocks(key_feat)
    value_blocks = value_rows.astype(jnp.float32).reshape(block_count, TOK_DEV, -1)
    teacher_blocks = split_blocks(teacher_out.astype(jnp.float32))
    block_state = jnp.einsum("njbf,nbd->njfd", key_blocks, value_blocks)
    block_norm = jnp.sum(key_blocks, axis=2)
    before_state = exclusive_sum(block_state)
    before_norm = exclusive_sum(block_norm)
    causal = jnp.arange(TOK_DEV)[:, None] >= jnp.arange(TOK_DEV)[None, :]

    def forward_one(items):
        query_part, key_part, value_part, teacher_part, state_part, norm_part = items
        affinity = jnp.where(causal, jnp.einsum("jrf,jsf->jrs", query_part, key_part), 0.0)
        local_mix = jnp.einsum("jrs,sd->jrd", rounded_wide(affinity), value_part)
        numerator = jnp.einsum("jrf,jfd->jrd", query_part, state_part, precision=HIGHEST_MODE) + local_mix
        denominator = jnp.einsum("jrf,jf->jr", query_part, norm_part, precision=HIGHEST_MODE) + jnp.sum(affinity, axis=-1)
        student = numerator / denominator[..., None]
        grad_out = 2.0 * (student - teacher_part) / TOKENS
        grad_numer = grad_out / denominator[..., None]
        grad_denom = -jnp.sum(grad_out * student, axis=-1) / denominator
        back_state = jnp.einsum("jrf,jrd->jfd", query_part, grad_numer, precision=HIGHEST_MODE)
        back_norm = jnp.einsum("jrf,jr->jf", query_part, grad_denom, precision=HIGHEST_MODE)
        return grad_numer, grad_denom, back_state, back_norm

    grad_numer, grad_denom, back_state, back_norm = lax.map(
        forward_one, (query_blocks, key_blocks, value_blocks, teacher_blocks, before_state, before_norm))
    after_state = exclusive_sum(back_state[::-1])[::-1]
    after_norm = exclusive_sum(back_norm[::-1])[::-1]

    def backward_one(items):
        (query_part, key_part, value_part, qpre_part, kpre_part, qin_part, kin_part,
         state_part, norm_part, later_state, later_norm, numer_part, denom_part) = items
        grad_aff = jnp.einsum("jrd,sd->jrs", numer_part, value_part, precision=HIGHEST_MODE) + denom_part[..., None]
        grad_aff = jnp.where(causal, grad_aff, 0.0)
        grad_qfeat = (jnp.einsum("jrd,jfd->jrf", numer_part, state_part, precision=HIGHEST_MODE)
                      + denom_part[..., None] * norm_part[:, None, :]
                      + jnp.einsum("jrs,jsf->jrf", grad_aff, key_part, precision=HIGHEST_MODE))
        grad_kfeat = (jnp.einsum("sd,jfd->jsf", value_part, later_state, precision=HIGHEST_MODE)
                      + later_norm[:, None, :]
                      + jnp.einsum("jrs,jrf->jsf", grad_aff, query_part, precision=HIGHEST_MODE))
        grad_wq = jnp.einsum("jrd,jrf->jdf", qin_part, grad_qfeat * jax.nn.sigmoid(qpre_part), precision=HIGHEST_MODE)
        grad_wk = jnp.einsum("rd,jrf->jdf", kin_part, grad_kfeat * jax.nn.sigmoid(kpre_part), precision=HIGHEST_MODE)
        return grad_wq, grad_wk

    grad_wq, grad_wk = lax.map(backward_one, (
        query_blocks, key_blocks, value_blocks, split_blocks(query_pre), split_blocks(key_pre),
        split_blocks(query_wide), key_wide.reshape(block_count, TOK_DEV, -1),
        before_state, before_norm, after_state, after_norm, grad_numer, grad_denom))
    return jnp.sum(grad_wq, axis=0), jnp.sum(grad_wk, axis=0)


def reference(queries, keys, values, feat_q, feat_k):
    group_size = HEADS // KV_HEADS
    query_groups = queries.reshape(TOKENS, KV_HEADS, group_size, HD).transpose(1, 2, 0, 3)
    key_groups = keys.reshape(TOKENS, KV_HEADS, HD).transpose(1, 0, 2)
    value_groups = values.reshape(TOKENS, KV_HEADS, HD).transpose(1, 0, 2)
    weight_query = feat_q.reshape(KV_HEADS, group_size, HD, FD)
    weight_key = feat_k.reshape(KV_HEADS, group_size, HD, FD)

    def one_group(items):
        query_heads, key_rows, value_rows, query_map, key_map = items
        teacher_out = teacher_group(query_heads, key_rows, value_rows)
        return student_group(query_heads, key_rows, value_rows, teacher_out, query_map, key_map)

    grad_q, grad_k = lax.map(one_group, (query_groups, key_groups, value_groups, weight_query, weight_key))
    return grad_q.reshape(HEADS, HD, FD), grad_k.reshape(HEADS, HD, FD)
```

```python
import functools
import math

import jax
import jax.numpy as jnp
from jax import lax
from jax.experimental import pallas as pl
from jax.experimental.pallas import tpu as pltpu
from jax.sharding import PartitionSpec as P

HEADS = 128
KV_HEADS = 8
CORES = 2
LOG2E = math.log2(math.e)
MASKED_SCORE = -1e30
VMEM_BYTES = 48 * 1024 * 1024
F32 = jnp.float32
BF16 = jnp.bfloat16

NN = (((1,), (0,)), ((), ()))
NT = (((1,), (1,)), ((), ()))
TN = (((0,), (0,)), ((), ()))


def dot(a, b, form):
    return lax.dot_general(a, b, form, preferred_element_type=F32)


def from_partner(block, axis, stride):
    count = lax.axis_size(axis)
    route = []
    for low in range(count):
        high = low | 1 << stride
        if high != low and high < count:
            route += [(low, high), (high, low)]
    return lax.ppermute(block, axis, route)


def tile_of(rows):
    return 256 if rows % 256 == 0 else rows


def with_ones(values):
    return jnp.concatenate((values, jnp.ones_like(values)), axis=1)


def log1p_exp(decay):
    return jnp.where(decay < 0.01, decay - 0.5 * decay * decay, jnp.log(1.0 + decay))


def features(pre):
    decay = jnp.exp(-jnp.abs(pre))
    return (jnp.maximum(pre, 0.0) + log1p_exp(decay)).astype(BF16)


def slope(pre):
    decay = jnp.exp(-jnp.abs(pre))
    inverse = 1.0 / (1.0 + decay)
    return jnp.where(pre >= 0, inverse, decay * inverse)


def causal_mask(rows):
    return lax.broadcasted_iota(jnp.int32, (rows, rows), 0) >= lax.broadcasted_iota(
        jnp.int32, (rows, rows), 1
    )


def local_attention(scale, q_ref, k_ref, v_ref, acc_ref, stat_ref):
    head = pl.program_id(0)
    rows, width = q_ref.shape
    tile = tile_of(rows)
    lane = lax.broadcasted_iota(jnp.int32, (tile, stat_ref.shape[1]), 1)
    mask = causal_mask(tile)
    wide = with_ones(v_ref[...])
    for i in range(rows // tile):
        here = pl.ds(i * tile, tile)
        end = (i + 1) * tile
        scores = dot(q_ref[here, :], k_ref[:end, :], NT) * scale
        last = jnp.where(mask, scores[:, end - tile :], MASKED_SCORE)
        scores = last if i == 0 else jnp.concatenate((scores[:, : end - tile], last), axis=1)
        peak = jnp.max(scores, axis=1, keepdims=True)
        mixed = dot(jnp.exp2(scores - peak).astype(BF16), wide[:end], NN)
        acc_ref[here, :] = mixed[:, :width]
        stat = jnp.where(lane == head, peak, stat_ref[here, :])
        stat_ref[here, :] = jnp.where(lane == head + 64, mixed[:, width : width + 1], stat)


def chunk_attention(
    scale,
    distance,
    place_ref,
    q_ref,
    k_ref,
    v_ref,
    wk_ref,
    acc_in,
    stat_in,
    state_in,
    acc_ref,
    stat_ref,
    state_ref,
):
    head = pl.program_id(0)
    rows, width = q_ref.shape
    tile = tile_of(rows)
    lane = lax.broadcasted_iota(jnp.int32, (tile, stat_ref.shape[1]), 1)

    @pl.when(head == 0)
    def _():
        stat_ref[...] = stat_in[...]

    @pl.when(place_ref[0] < distance)
    def _():
        acc_ref[...] = acc_in[...]
        state_ref[...] = state_in[...]

    @pl.when(place_ref[0] >= distance)
    def _():
        wide = with_ones(v_ref[...])
        for i in range(rows // tile):
            here = pl.ds(i * tile, tile)
            scores = dot(q_ref[here, :], k_ref[...], NT) * scale
            stat = stat_ref[here, :]
            old_peak = jnp.sum(jnp.where(lane == head, stat, 0.0), axis=1, keepdims=True)
            old_sum = jnp.sum(jnp.where(lane == head + 64, stat, 0.0), axis=1, keepdims=True)
            peak = jnp.maximum(jnp.max(scores, axis=1, keepdims=True), old_peak)
            mixed = dot(jnp.exp2(scores - peak).astype(BF16), wide, NN)
            factor = jnp.exp2(old_peak - peak)
            acc_ref[here, :] = acc_in[here, :] * factor + mixed[:, :width]
            stat = jnp.where(lane == head, peak, stat)
            stat_ref[here, :] = jnp.where(
                lane == head + 64, old_sum * factor + mixed[:, width : width + 1], stat
            )
        key_feat = features(dot(k_ref[...], wk_ref[0], NN))
        state_ref[0] = state_in[0] + dot(key_feat, wide, TN)


def student(total_tokens, chunk_count, place_ref, q_ref, k_ref, v_ref, *refs):
    chunk_refs = refs[: 2 * chunk_count]
    wq_ref, wk_ref, acc_ref, stat_ref, state_ref, out_ref, wk_acc = refs[2 * chunk_count :]
    head = pl.program_id(0) + place_ref[1]
    rows, width = q_ref.shape
    tile = tile_of(rows)
    tiles = rows // tile
    lane = lax.broadcasted_iota(jnp.int32, (tile, stat_ref.shape[1]), 1)
    mask = causal_mask(tile)
    state = state_ref[0]
    query_pre, key_pre, key_feat, query_feat, wide, states, grads, backs = ([] for _ in range(8))
    for i in range(tiles):
        here = pl.ds(i * tile, tile)
        query_pre.append(dot(q_ref[here, :], wq_ref[0], NN))
        key_pre.append(dot(k_ref[here, :], wk_ref[0], NN))
        query_feat.append(features(query_pre[i]))
        key_feat.append(features(key_pre[i]))
        wide.append(with_ones(v_ref[here, :]))
        affinity = jnp.where(mask, dot(query_feat[i], key_feat[i], NT), 0.0).astype(BF16)
        states.append(state.astype(BF16))
        mixed = dot(affinity, wide[i], NN) + dot(query_feat[i], states[i], NN)
        inverse = 1.0 / mixed[:, width:]
        result = mixed[:, :width] * inverse
        stat = stat_ref[here, :]
        total = jnp.sum(jnp.where(lane == head + 64, stat, 0.0), axis=1, keepdims=True)
        teacher = (acc_ref[here, :] / total).astype(BF16).astype(F32)
        grad_out = (result - teacher) * (2.0 / total_tokens)
        grad_numer = grad_out * inverse
        grad_denom = jnp.sum(grad_out * result, axis=1, keepdims=True) * inverse * (-1.0 / width)
        grads.append(jnp.concatenate((grad_numer, grad_denom), axis=1).astype(BF16))
        backs.append(dot(query_feat[i], grads[i], TN))
        state = state + dot(key_feat[i], wide[i], TN)
    after = jnp.zeros_like(state)
    grad_wq = jnp.zeros(wq_ref.shape[1:], F32)
    grad_wk = jnp.zeros(wk_ref.shape[1:], F32)
    for i in reversed(range(tiles)):
        here = pl.ds(i * tile, tile)
        grad_aff = jnp.where(mask, dot(grads[i], wide[i], NT), 0.0).astype(BF16)
        grad_qfeat = dot(grads[i], states[i], NT) + dot(grad_aff, key_feat[i], NN)
        grad_kfeat = dot(grad_aff, query_feat[i], TN)
        if i < tiles - 1:
            grad_kfeat = grad_kfeat + dot(wide[i], after.astype(BF16), NT)
        after = after + backs[i]
        grad_wq += dot(q_ref[here, :], (grad_qfeat * slope(query_pre[i])).astype(BF16), TN)
        grad_wk += dot(k_ref[here, :], (grad_kfeat * slope(key_pre[i])).astype(BF16), TN)
    out_ref[0, 0] = grad_wq.astype(out_ref.dtype)
    wk_acc[...] = grad_wk
    after = after.astype(BF16)
    for c in range(chunk_count):

        @pl.when(place_ref[0] >= c + 1)
        def _(c=c):
            keys = chunk_refs[2 * c][...]
            grad_kfeat = dot(with_ones(chunk_refs[2 * c + 1][...]), after, NT)
            change = grad_kfeat * slope(dot(keys, wk_ref[0], NN))
            wk_acc[...] += dot(keys, change.astype(BF16), TN)

    out_ref[0, 1] = wk_acc[...].astype(out_ref.dtype)


def params():
    return pltpu.CompilerParams(
        vmem_limit_bytes=VMEM_BYTES, dimension_semantics=("arbitrary",)
    )


def body(queries, keys, values, feat_q, feat_k):
    row_count = queries.shape[0]
    heads_here, head_dim, feat_count = feat_q.shape
    seq_count = lax.axis_size("seq")
    chips = seq_count // CORES
    seq_place = lax.axis_index("seq")
    core, chip = seq_place % CORES, seq_place // CORES
    head_place = lax.axis_index("head")
    spread = max(1, HEADS // KV_HEADS // heads_here)
    key_value = jnp.stack((keys, values))
    for bit_index in range(spread.bit_length() - 1):
        partner = from_partner(key_value, "head", bit_index)
        upper_half = head_place // (1 << bit_index) % 2 == 1
        key_value = jnp.where(
            upper_half,
            jnp.concatenate((partner, key_value), axis=2),
            jnp.concatenate((key_value, partner), axis=2),
        )
    groups = key_value.shape[2] // head_dim
    half = heads_here // CORES
    core_route = [(i, i ^ 1) for i in range(seq_count)]
    first = core == 0

    def pair_up(low, high, axis):
        mine = jnp.where(first, low, high)
        other = lax.ppermute(jnp.where(first, high, low), "seq", core_route)
        return jnp.where(
            first,
            jnp.concatenate((mine, other), axis=axis),
            jnp.concatenate((other, mine), axis=axis),
        )

    if groups > 1:
        own_groups = groups // CORES
        split = own_groups * head_dim
        kv = pair_up(key_value[:, :, :split], key_value[:, :, split:], 1)
    else:
        own_groups = groups
        kv = pair_up(key_value, key_value, 1)
    kv = jnp.concatenate((kv[0], kv[1]), axis=1)
    q = pair_up(queries[:, : half * head_dim], queries[:, half * head_dim :], 0)
    rows = CORES * row_count
    up_route = [(i, i + CORES) for i in range(seq_count - CORES)]
    chunks = []
    for _ in range(chips - 1):
        chunks.append(lax.ppermute(chunks[-1] if chunks else kv, "seq", up_route))
    wk = lax.dynamic_slice_in_dim(feat_k, core * half, half, 0)
    wq = lax.dynamic_slice_in_dim(feat_q, core * half, half, 0)

    per_group = half // own_groups
    scale = head_dim ** (-0.5) * LOG2E
    q_spec = pl.BlockSpec((rows, head_dim), lambda h, *_: (0, h))
    k_spec = pl.BlockSpec((rows, head_dim), lambda h, *_: (0, h // per_group))
    v_spec = pl.BlockSpec((rows, head_dim), lambda h, *_: (0, own_groups + h // per_group))
    stat_spec = pl.BlockSpec((rows, 128), lambda h, *_: (0, 0))
    w_spec = pl.BlockSpec((1, head_dim, feat_count), lambda h, *_: (h, 0, 0))
    state_spec = pl.BlockSpec((1, feat_count, 2 * head_dim), lambda h, *_: (h, 0, 0))
    acc_type = jax.ShapeDtypeStruct((rows, half * head_dim), F32)
    stat_type = jax.ShapeDtypeStruct((rows, 128), F32)
    state_type = jax.ShapeDtypeStruct((half, feat_count, 2 * head_dim), F32)

    acc, stat = pl.pallas_call(
        functools.partial(local_attention, scale),
        grid=(half,),
        in_specs=[q_spec, k_spec, v_spec],
        out_specs=[q_spec, stat_spec],
        out_shape=[acc_type, stat_type],
        compiler_params=params(),
        name="local_attention",
    )(q, kv, kv)
    state = jnp.zeros(state_type.shape, F32)
    place = jnp.stack((chip, jnp.zeros_like(chip))).astype(jnp.int32)
    for index, chunk in enumerate(chunks):
        acc, stat, state = pl.pallas_call(
            functools.partial(chunk_attention, scale, index + 1),
            grid_spec=pltpu.PrefetchScalarGridSpec(
                num_scalar_prefetch=1,
                grid=(half,),
                in_specs=[q_spec, k_spec, v_spec, w_spec, q_spec, stat_spec, state_spec],
                out_specs=[q_spec, stat_spec, state_spec],
            ),
            out_shape=[acc_type, stat_type, state_type],
            input_output_aliases={5: 0, 6: 1, 7: 2},
            compiler_params=params(),
            name="chunk_attention",
        )(place, q, chunk, chunk, wk, acc, stat, state)

    grads = pl.pallas_call(
        functools.partial(student, row_count * seq_count, len(chunks)),
        grid_spec=pltpu.PrefetchScalarGridSpec(
            num_scalar_prefetch=1,
            grid=(half,),
            in_specs=[q_spec, k_spec, v_spec]
            + [k_spec, v_spec] * len(chunks)
            + [w_spec, w_spec, q_spec, stat_spec, state_spec],
            out_specs=pl.BlockSpec((1, 2, head_dim, feat_count), lambda h, *_: (h, 0, 0, 0)),
            scratch_shapes=[pltpu.VMEM((head_dim, feat_count), F32)],
        ),
        out_shape=jax.ShapeDtypeStruct((half, 2, head_dim, feat_count), BF16),
        compiler_params=params(),
        name="student",
    )(place, q, kv, kv, *[c for chunk in chunks for c in (chunk, chunk)], wq, wk, acc, stat, state)

    flat = grads.reshape(-1, feat_count)
    share = flat.shape[0] // chips

    def shift_route(distance):
        return [(i, (i + CORES * distance) % seq_count) for i in range(seq_count)]

    def part(index):
        return lax.dynamic_slice_in_dim(flat, index % chips * share, share, 0)

    mine = part(chip).astype(F32)
    for distance in range(1, chips):
        mine += lax.ppermute(part(chip + distance), "seq", shift_route(distance)).astype(F32)
    mine = mine.astype(BF16)
    whole = lax.dynamic_update_slice_in_dim(jnp.zeros_like(flat), mine, chip * share, 0)
    for distance in range(1, chips):
        got = lax.ppermute(mine, "seq", shift_route(distance))
        whole = lax.dynamic_update_slice_in_dim(
            whole, got, (chip - distance + chips) % chips * share, 0
        )
    whole = whole.reshape(half, 2, head_dim, feat_count)
    other = lax.ppermute(whole, "seq", core_route)
    both = jnp.where(
        first, jnp.concatenate((whole, other), axis=0), jnp.concatenate((other, whole), axis=0)
    ).astype(F32)
    return both[:, 0], both[:, 1]


def solution(mesh):
    return jax.shard_map(
        body,
        mesh=mesh,
        in_specs=(
            P("seq", "head"),
            P("seq", "head"),
            P("seq", "head"),
            P("head", None, None),
            P("head", None, None),
        ),
        out_specs=(P("head", None, None), P("head", None, None)),
        check_vma=False,
    )
```

```python
import functools
import math

import jax
import jax.numpy as jnp
from jax import lax
from jax.experimental import pallas as pl
from jax.experimental.pallas import tpu as pltpu
from jax.sharding import PartitionSpec as P

HEADS = 128
KV_HEADS = 8
CORES = 2
LANES = 128
BLOCK_HEADS = 4
STUDENT_HEADS = 4
STUDENT_CALLS = 2
LOG2E = math.log2(math.e)
LN2 = math.log(2.0)
MASKED_SCORE = -1e30
VMEM_BYTES = 56 * 1024 * 1024
F32 = jnp.float32
BF16 = jnp.bfloat16

NN = (((1,), (0,)), ((), ()))
NT = (((1,), (1,)), ((), ()))
TN = (((0,), (0,)), ((), ()))


def dot(a, b, form):
    return lax.dot_general(a, b, form, preferred_element_type=F32)


def from_partner(block, axis, stride):
    count = lax.axis_size(axis)
    route = []
    for low in range(count):
        high = low | 1 << stride
        if high != low and high < count:
            route += [(low, high), (high, low)]
    return lax.ppermute(block, axis, route)


def tile_of(rows):
    return 256 if rows % 256 == 0 else rows


def with_ones(values):
    return jnp.concatenate((values, jnp.ones_like(values)), axis=1)


def turned(block):
    return block.astype(F32).T.astype(BF16)


def turned_with_ones(values):
    return jnp.concatenate((turned(values), jnp.ones((16, values.shape[0]), BF16)), axis=0)


def softplus_and_slope(pre):
    scaled = pre * LOG2E
    decay = jnp.exp2(jnp.minimum(scaled, -scaled))
    small = decay * (LOG2E - (0.5 * LOG2E) * decay)
    log_term = jnp.where(decay < 0.01, small, jnp.log2(1.0 + decay))
    level = jnp.maximum(scaled, 0.0) + log_term
    return (level * LN2).astype(BF16), jnp.exp2(scaled - level)


def columns(index, width):
    return slice(index * width, (index + 1) * width)


def causal_mask(rows):
    return lax.broadcasted_iota(jnp.int32, (rows, rows), 0) >= lax.broadcasted_iota(
        jnp.int32, (rows, rows), 1
    )


def attend(scale, units, score_parts, wide, store):
    ahead = score_parts(units[0])
    for place, unit in enumerate(units):
        parts = ahead
        if place + 1 < len(units):
            ahead = score_parts(units[place + 1])
        peak = functools.reduce(
            jnp.maximum, [jnp.max(part, axis=1, keepdims=True) for part in parts]
        )
        peak = peak * scale
        weights = [jnp.exp2(part * scale - peak).astype(BF16) for part in parts]
        weights = weights[0] if len(weights) == 1 else jnp.concatenate(weights, axis=1)
        mixed = dot(weights, wide[: weights.shape[1]], NN)
        width = mixed.shape[1] // 2
        inverse = 1.0 / mixed[:, width:]
        level = peak + jnp.log2(mixed[:, width : width + 1])
        store(unit, mixed[:, :width] * inverse, level)


def local_attention(scale, place_ref, own_ref, other_ref, k_ref, v_ref, q_ref, mix_ref, level_ref):
    rows, width = k_ref.shape
    heads = q_ref.shape[1] // width
    first_head = pl.program_id(0) * heads
    part = own_ref.shape[0]
    core = place_ref[1]
    q_ref[pl.ds(pl.multiple_of(core * part, part), part), :] = own_ref[...]
    q_ref[pl.ds(pl.multiple_of((1 - core) * part, part), part), :] = other_ref[...]
    tile = tile_of(rows)
    lane = lax.broadcasted_iota(jnp.int32, (tile, LANES), 1)
    mask = causal_mask(tile)
    wide = with_ones(v_ref[...])

    def score_parts(unit):
        b, i = unit
        query = q_ref[columns(i, tile), columns(b, width)]
        last = jnp.where(mask, dot(query, k_ref[columns(i, tile), :], NT), MASKED_SCORE)
        return [last] if i == 0 else [dot(query, k_ref[: i * tile, :], NT), last]

    def store(unit, mixture, level):
        b, i = unit
        mix_ref[columns(i, tile), columns(b, width)] = mixture.astype(BF16)
        here = (columns(i, tile), slice(None))
        level_ref[here] = jnp.where(lane == first_head + b, level, level_ref[here])

    units = [(b, i) for b in range(heads) for i in range(rows // tile)]
    attend(scale, units, score_parts, wide, store)


def chunk_attention(
    scale,
    distance,
    place_ref,
    q_ref,
    k_ref,
    v_ref,
    wk_ref,
    state_in,
    mix_ref,
    level_ref,
    slope_ref,
    state_ref,
    turned_ref,
):
    rows, width = k_ref.shape
    heads = q_ref.shape[1] // width
    first_head = pl.program_id(0) * heads

    @pl.when(place_ref[0] < distance)
    def _():
        mix_ref[...] = jnp.zeros_like(mix_ref)
        slope_ref[...] = jnp.zeros_like(slope_ref)
        level_ref[...] = jnp.full_like(level_ref, MASKED_SCORE)
        state_ref[...] = state_in[...]

    @pl.when(place_ref[0] >= distance)
    def _():
        @pl.when(pl.program_id(0) == 0)
        def _():
            turned_ref[...] = turned_with_ones(v_ref[...])

        tile = tile_of(rows)
        lane = lax.broadcasted_iota(jnp.int32, (tile, LANES), 1)
        wide = with_ones(v_ref[...])
        keys = k_ref[...]
        for pair in range(heads // 2):
            weight = jnp.concatenate((wk_ref[2 * pair], wk_ref[2 * pair + 1]), axis=1)
            feat, slope = softplus_and_slope(dot(keys, weight, NN))
            slope_ref[:, columns(pair, 2 * width)] = slope.astype(BF16)
            state_ref[pair] = state_in[pair] + dot(turned_ref[...], feat, NN)

        def score_parts(unit):
            b, i = unit
            return [dot(q_ref[columns(i, tile), columns(b, width)], keys, NT)]

        def store(unit, mixture, level):
            b, i = unit
            mix_ref[columns(i, tile), columns(b, width)] = mixture.astype(BF16)
            here = (columns(i, tile), slice(None))
            level_ref[here] = jnp.where(lane == first_head + b, level, level_ref[here])

        units = [(b, i) for b in range(heads) for i in range(rows // tile)]
        attend(scale, units, score_parts, wide, store)


def student(total_tokens, chunk_count, start_head, place_ref, q_ref, k_ref, v_ref, *refs):
    refs = list(refs)
    chunk_keys = [refs.pop(0) for _ in range(chunk_count)]
    chunk_values = [refs.pop(0) for _ in range(chunk_count)]
    mix_refs = [refs.pop(0) for _ in range(chunk_count + 1)]
    level_refs = [refs.pop(0) for _ in range(chunk_count + 1)]
    slope_refs = [refs.pop(0) for _ in range(chunk_count)]
    wq_ref, wk_ref, state_ref, out_ref, wide_t, keys_t, chunk_t, wk_acc = refs
    rows, width = k_ref.shape
    heads = q_ref.shape[1] // width
    pairs = heads // 2
    step = pl.program_id(0)
    first_head = start_head + step * heads
    tile = tile_of(rows)
    tiles = rows // tile
    lane = lax.broadcasted_iota(jnp.int32, (tile, LANES), 1)
    mask = causal_mask(tile)

    @pl.when(step == 0)
    def _():
        wide_t[...] = turned_with_ones(v_ref[...])
        keys_t[...] = turned(k_ref[...])
        for c in range(chunk_count):

            @pl.when(place_ref[0] >= c + 1)
            def _(c=c):
                chunk_t[c] = turned(chunk_keys[c][...])

    head_list = range(heads)
    tile_list = range(tiles)
    units = [(b, i) for b in head_list for i in tile_list]
    wide = [with_ones(v_ref[columns(i, tile), :]) for i in tile_list]

    key_feat, key_slope, states = {}, {}, {}
    for pair in range(pairs):
        weight = jnp.concatenate((wk_ref[2 * pair], wk_ref[2 * pair + 1]), axis=1)
        running = state_ref[pair]
        for i in tile_list:
            feat, slope = softplus_and_slope(dot(k_ref[columns(i, tile), :], weight, NN))
            key_slope[pair, i] = slope
            for side in range(2):
                here = columns(side, width)
                key_feat[2 * pair + side, i] = feat[:, here]
                norm = jnp.broadcast_to(running[width : width + 1, here], (width, width))
                states[2 * pair + side, i] = jnp.concatenate(
                    (running[:width, here], norm), axis=0
                ).astype(BF16)
            if i + 1 < tiles:
                running = running + dot(wide_t[:, columns(i, tile)], feat, NN)

    query_feat, query_slope = {}, {}
    for b, i in units:
        query = q_ref[columns(i, tile), columns(b, width)]
        query_feat[b, i], query_slope[b, i] = softplus_and_slope(dot(query, wq_ref[b], NN))

    mixed = {}
    for b, i in units:
        affinity = dot(query_feat[b, i], key_feat[b, i], NT)
        affinity = jnp.where(mask, affinity, 0.0).astype(BF16)
        mixed[b, i] = dot(affinity, wide[i], NN) + dot(query_feat[b, i], states[b, i], NT)

    grads, backs = {}, {}
    for b, i in units:
        inverse = 1.0 / mixed[b, i][:, width:]
        result = mixed[b, i][:, :width] * inverse
        rows_here = columns(i, tile)
        levels = [
            jnp.sum(
                jnp.where(lane == first_head + b, ref[rows_here, :], 0.0), axis=1, keepdims=True
            )
            for ref in level_refs
        ]
        peak = functools.reduce(jnp.maximum, levels)
        shares = [jnp.exp2(level - peak) for level in levels]
        total = functools.reduce(jnp.add, shares)
        teacher = functools.reduce(
            jnp.add,
            [
                share * ref[rows_here, columns(b, width)].astype(F32)
                for share, ref in zip(shares, mix_refs)
            ],
        )
        teacher = (teacher * (1.0 / total)).astype(BF16).astype(F32)
        grad_out = (result - teacher) * (2.0 / total_tokens)
        grad_denom = jnp.sum(grad_out * result, axis=1, keepdims=True) * inverse * (-1.0 / width)
        grads[b, i] = jnp.concatenate((grad_out * inverse, grad_denom), axis=1).astype(BF16)
        backs[b, i] = dot(query_feat[b, i], grads[b, i], TN)

    after = {}
    for b in head_list:
        running = backs[b, tiles - 1]
        for i in reversed(range(tiles - 1)):
            after[b, i] = running.astype(BF16)
            running = running + backs[b, i]
        after[b, -1] = running.astype(BF16)

    query_change, key_change = {}, {}
    for b, i in units:
        grad_aff = jnp.where(mask, dot(grads[b, i], wide[i], NT), 0.0).astype(BF16)
        grad_qfeat = dot(grads[b, i], states[b, i], NN) + dot(grad_aff, key_feat[b, i], NN)
        query_change[b, i] = (grad_qfeat * query_slope[b, i]).astype(BF16)
        key_change[b, i] = dot(grad_aff, query_feat[b, i], TN)
    for b in head_list:
        change = jnp.concatenate([query_change[b, i] for i in tile_list], axis=0)
        out_ref[b, 0] = dot(q_ref[:, columns(b, width)], change, TN).astype(out_ref.dtype)
    for pair in range(pairs):
        changes = []
        for i in tile_list:
            both = jnp.concatenate((key_change[2 * pair, i], key_change[2 * pair + 1, i]), axis=1)
            if i + 1 < tiles:
                later = jnp.concatenate((after[2 * pair, i], after[2 * pair + 1, i]), axis=0)
                both = both + dot(wide[i], later, NT)
            changes.append((both * key_slope[pair, i]).astype(BF16))
        wk_acc[pair] = dot(keys_t[...], jnp.concatenate(changes, axis=0), NN)

    whole = [
        jnp.concatenate((after[2 * pair, -1], after[2 * pair + 1, -1]), axis=0)
        for pair in range(pairs)
    ]
    for c in range(chunk_count):

        @pl.when(place_ref[0] >= c + 1)
        def _(c=c):
            values = with_ones(chunk_values[c][...])
            for pair in range(pairs):
                slope = slope_refs[c][:, columns(pair, 2 * width)].astype(F32)
                change = (dot(values, whole[pair], NT) * slope).astype(BF16)
                wk_acc[pair] += dot(chunk_t[c], change, NN)

    for b in head_list:
        out_ref[b, 1] = wk_acc[b // 2][:, columns(b % 2, width)].astype(out_ref.dtype)


def params():
    return pltpu.CompilerParams(
        vmem_limit_bytes=VMEM_BYTES, dimension_semantics=("arbitrary",)
    )


def cost(microseconds):
    return pl.CostEstimate(
        flops=int(microseconds * 1e9), bytes_accessed=int(microseconds * 3e6), transcendentals=0
    )


def body(queries, keys, values, feat_q, feat_k):
    row_count = queries.shape[0]
    heads_here, width, feat_count = feat_q.shape
    seq_count = lax.axis_size("seq")
    chips = seq_count // CORES
    seq_place = lax.axis_index("seq")
    core, chip = seq_place % CORES, seq_place // CORES
    head_place = lax.axis_index("head")
    spread = max(1, HEADS // KV_HEADS // heads_here)
    key_value = jnp.stack((keys, values))
    for bit_index in range(spread.bit_length() - 1):
        partner = from_partner(key_value, "head", bit_index)
        upper_half = head_place // (1 << bit_index) % 2 == 1
        key_value = jnp.where(
            upper_half,
            jnp.concatenate((partner, key_value), axis=2),
            jnp.concatenate((key_value, partner), axis=2),
        )
    groups = key_value.shape[2] // width
    half = heads_here // CORES
    core_route = [(i, i ^ 1) for i in range(seq_count)]
    first = core == 0

    if groups > 1:
        own_groups = groups // CORES
        split = own_groups * width
        low, high = key_value[:, :, :split], key_value[:, :, split:]
        kept, sent = jnp.where(first, low, high), jnp.where(first, high, low)
    else:
        own_groups = groups
        kept = sent = key_value
    got = lax.ppermute(sent, "seq", core_route)
    kv = jnp.where(
        first, jnp.concatenate((kept, got), axis=1), jnp.concatenate((got, kept), axis=1)
    )
    kv = jnp.concatenate((kv[0], kv[1]), axis=1)
    other_q = lax.ppermute(
        lax.dynamic_slice_in_dim(queries, (1 - core) * half * width, half * width, 1),
        "seq",
        core_route,
    )
    rows = CORES * row_count
    chunks = []
    for distance in range(1, chips):
        route = [(i, i + CORES * distance) for i in range(seq_count - CORES * distance)]
        chunks.append(lax.ppermute(kv, "seq", route))

    per_group = half // own_groups
    heads = math.gcd(per_group, BLOCK_HEADS)
    scale = width ** (-0.5) * LOG2E
    steps = half // heads

    def specs(heads, start):
        return dict(
            q=pl.BlockSpec((rows, heads * width), lambda h, *_: (0, start + h)),
            k=pl.BlockSpec((rows, width), lambda h, *_: (0, (start + h) * heads // per_group)),
            v=pl.BlockSpec(
                (rows, width), lambda h, *_: (0, own_groups + (start + h) * heads // per_group)
            ),
            level=pl.BlockSpec((rows, LANES), lambda h, *_: (0, 0)),
            w=pl.BlockSpec(
                (heads, width, feat_count),
                lambda h, place: (place[1] * (half // heads) + start + h, 0, 0),
            ),
            state=pl.BlockSpec(
                (heads // 2, width + 16, 2 * feat_count), lambda h, *_: (start + h, 0, 0)
            ),
        )

    at = specs(heads, 0)
    mix_type = jax.ShapeDtypeStruct((rows, half * width), BF16)
    level_type = jax.ShapeDtypeStruct((rows, LANES), F32)
    state_type = jax.ShapeDtypeStruct((half // 2, width + 16, 2 * feat_count), F32)
    place = jnp.stack((chip, core)).astype(jnp.int32)

    q, mix, level = pl.pallas_call(
        functools.partial(local_attention, scale),
        grid_spec=pltpu.PrefetchScalarGridSpec(
            num_scalar_prefetch=1,
            grid=(steps,),
            in_specs=[
                pl.BlockSpec(
                    (row_count, heads * width), lambda h, place: (0, place[1] * steps + h)
                ),
                pl.BlockSpec((row_count, heads * width), lambda h, *_: (0, h)),
                at["k"],
                at["v"],
            ],
            out_specs=[at["q"], at["q"], at["level"]],
        ),
        out_shape=[mix_type, mix_type, level_type],
        compiler_params=params(),
        cost_estimate=cost(12),
        name="local_attention",
    )(place, queries, other_q, kv, kv)
    state = jnp.zeros(state_type.shape, F32)
    mixes, levels, slopes = [mix], [level], []
    for index, chunk in enumerate(chunks):
        mix, level, slope, state = pl.pallas_call(
            functools.partial(chunk_attention, scale, index + 1),
            grid_spec=pltpu.PrefetchScalarGridSpec(
                num_scalar_prefetch=1,
                grid=(steps,),
                in_specs=[at["q"], at["k"], at["v"], at["w"], at["state"]],
                out_specs=[at["q"], at["level"], at["q"], at["state"]],
                scratch_shapes=[pltpu.VMEM((width + 16, rows), BF16)],
            ),
            out_shape=[mix_type, level_type, mix_type, state_type],
            compiler_params=params(),
            cost_estimate=cost(18),
            name="chunk_attention",
        )(place, q, chunk, chunk, feat_k, state)
        mixes.append(mix)
        levels.append(level)
        slopes.append(slope)

    calls = math.gcd(half // heads, STUDENT_CALLS)
    group_heads = half // calls
    heads = math.gcd(group_heads, STUDENT_HEADS)
    results = []
    for call in range(calls):
        at = specs(heads, call * group_heads // heads)
        grads = pl.pallas_call(
            functools.partial(
                student, row_count * seq_count, len(chunks), call * group_heads
            ),
            grid_spec=pltpu.PrefetchScalarGridSpec(
                num_scalar_prefetch=1,
                grid=(group_heads // heads,),
                in_specs=[at["q"], at["k"], at["v"]]
                + [at["k"]] * len(chunks)
                + [at["v"]] * len(chunks)
                + [at["q"]] * len(mixes)
                + [at["level"]] * len(levels)
                + [at["q"]] * len(slopes)
                + [at["w"], at["w"], at["state"]],
                out_specs=pl.BlockSpec(
                    (heads, 2, width, feat_count), lambda h, *_: (h, 0, 0, 0)
                ),
                scratch_shapes=[
                    pltpu.VMEM((width + 16, rows), BF16),
                    pltpu.VMEM((width, rows), BF16),
                    pltpu.VMEM((max(1, len(chunks)), width, rows), BF16),
                    pltpu.VMEM((heads // 2, width, 2 * feat_count), F32),
                ],
            ),
            out_shape=jax.ShapeDtypeStruct((group_heads, 2, width, feat_count), BF16),
            compiler_params=params(),
            cost_estimate=cost(40 / calls),
            name="student",
        )(place, q, kv, kv, *chunks, *chunks, *mixes, *levels, *slopes, feat_q, feat_k, state)
        results.append(reduced(grads, chip, chips, seq_count, core_route))
    own = jnp.concatenate([pair[0] for pair in results], axis=0)
    other = jnp.concatenate([pair[1] for pair in results], axis=0)
    both = jnp.where(
        first, jnp.concatenate((own, other), axis=0), jnp.concatenate((other, own), axis=0)
    ).astype(F32)
    return both[:, 0], both[:, 1]


def reduced(grads, chip, chips, seq_count, core_route):
    flat = grads.reshape(-1, grads.shape[-1])
    share = flat.shape[0] // chips

    def route(distance):
        return [(i, (i + CORES * distance) % seq_count) for i in range(seq_count)]

    def part(index):
        return lax.dynamic_slice_in_dim(flat, index % chips * share, share, 0)

    mine = part(chip).astype(F32)
    for distance in range(1, chips):
        mine += lax.ppermute(part(chip + distance), "seq", route(distance)).astype(F32)
    mine = mine.astype(BF16)
    whole = lax.dynamic_update_slice_in_dim(jnp.zeros_like(flat), mine, chip * share, 0)
    for distance in range(1, chips):
        got = lax.ppermute(mine, "seq", route(distance))
        whole = lax.dynamic_update_slice_in_dim(
            whole, got, (chip - distance + chips) % chips * share, 0
        )
    whole = whole.reshape(grads.shape)
    return whole, lax.ppermute(whole, "seq", core_route)


def solution(mesh):
    return jax.shard_map(
        body,
        mesh=mesh,
        in_specs=(
            P("seq", "head"),
            P("seq", "head"),
            P("seq", "head"),
            P("head", None, None),
            P("head", None, None),
        ),
        out_specs=(P("head", None, None), P("head", None, None)),
        check_vma=False,
    )
```

```python
import functools
import math

import jax
import jax.numpy as jnp
from jax import lax
from jax.experimental import pallas as pl
from jax.experimental.pallas import tpu as pltpu
from jax.sharding import PartitionSpec as P

HEADS = 128
KV_HEADS = 8
CORES = 2
LANES = 128
BLOCK_HEADS = 4
STUDENT_PARTS = (2, 1, 1)
LOCAL_WINDOW = 2
CHUNK_WINDOW = 2
UNIT_WINDOW = 8
LOG2E = math.log2(math.e)
LN2 = math.log(2.0)
MASKED_SCORE = -1e30
VMEM_BYTES = 56 * 1024 * 1024
F32 = jnp.float32
BF16 = jnp.bfloat16

NN = (((1,), (0,)), ((), ()))
NT = (((1,), (1,)), ((), ()))
TN = (((0,), (0,)), ((), ()))


def dot(a, b, form):
    return lax.dot_general(a, b, form, preferred_element_type=F32)


def from_partner(block, axis, stride):
    count = lax.axis_size(axis)
    route = []
    for low in range(count):
        high = low | 1 << stride
        if high != low and high < count:
            route += [(low, high), (high, low)]
    return lax.ppermute(block, axis, route)


def tile_of(rows):
    return 256 if rows % 256 == 0 else rows


def with_ones(values):
    return jnp.concatenate((values, jnp.ones_like(values)), axis=1)


def turned(block):
    return block.astype(F32).T.astype(BF16)


def turned_with_ones(values):
    return jnp.concatenate((turned(values), jnp.ones((16, values.shape[0]), BF16)), axis=0)


def softplus_and_slope(pre):
    scaled = pre * LOG2E
    decay = jnp.exp2(jnp.minimum(scaled, -scaled))
    small = decay * (LOG2E - (0.5 * LOG2E) * decay)
    log_term = jnp.where(decay < 0.01, small, jnp.log2(1.0 + decay))
    level = jnp.maximum(scaled, 0.0) + log_term
    return (level * LN2).astype(BF16), jnp.exp2(scaled - level)


def columns(index, width):
    return slice(index * width, (index + 1) * width)


def causal_mask(rows):
    return lax.broadcasted_iota(jnp.int32, (rows, rows), 0) >= lax.broadcasted_iota(
        jnp.int32, (rows, rows), 1
    )


def interleave(tasks, window):
    waiting, active = list(tasks), []
    while waiting or active:
        if waiting and len(active) < window:
            active.append(waiting.pop(0))
        for task in active[::-1]:
            if next(task, active) is active:
                active.remove(task)


def mixture_task(scale, score_parts, wide, unit, store):
    parts = score_parts(unit)
    yield
    peak = functools.reduce(jnp.maximum, [jnp.max(part, axis=1, keepdims=True) for part in parts])
    peak = peak * scale
    weights = [jnp.exp2(part * scale - peak).astype(BF16) for part in parts]
    weights = weights[0] if len(weights) == 1 else jnp.concatenate(weights, axis=1)
    mixed = dot(weights, wide[: weights.shape[1]], NN)
    width = mixed.shape[1] // 2
    store(unit, mixed[:, :width] * (1.0 / mixed[:, width:]), peak + jnp.log2(mixed[:, width : width + 1]))


def level_block(columns_of_heads, rows):
    lane = lax.broadcasted_iota(jnp.int32, (rows, LANES), 1)
    block = jnp.zeros((rows, LANES), F32)
    for b, level in enumerate(columns_of_heads):
        block = jnp.where(lane == b, level, block)
    return block


def storing(mix_ref, level_ref, tile, width, heads):
    held = {}

    def store(unit, mixture, level):
        b, i = unit
        mix_ref[columns(i, tile), columns(b, width)] = mixture.astype(BF16)
        held[unit] = level
        if all((other, i) in held for other in range(heads)):
            level_ref[columns(i, tile), :] = level_block(
                [held[other, i] for other in range(heads)], tile
            )

    return store


def local_attention(scale, place_ref, own_ref, other_ref, k_ref, v_ref, q_ref, mix_ref, level_ref):
    rows, width = k_ref.shape
    heads = q_ref.shape[1] // width
    part = own_ref.shape[0]
    core = place_ref[1]
    q_ref[pl.ds(pl.multiple_of(core * part, part), part), :] = own_ref[...]
    q_ref[pl.ds(pl.multiple_of((1 - core) * part, part), part), :] = other_ref[...]
    tile = tile_of(rows)
    mask = causal_mask(tile)
    wide = with_ones(v_ref[...])

    def score_parts(unit):
        b, i = unit
        query = q_ref[columns(i, tile), columns(b, width)]
        last = jnp.where(mask, dot(query, k_ref[columns(i, tile), :], NT), MASKED_SCORE)
        return [last] if i == 0 else [dot(query, k_ref[: i * tile, :], NT), last]

    store = storing(mix_ref, level_ref, tile, width, heads)
    units = [(b, i) for i in range(rows // tile) for b in range(heads)]
    interleave(
        [mixture_task(scale, score_parts, wide, unit, store) for unit in units], LOCAL_WINDOW
    )


def chunk_attention(
    scale,
    distance,
    place_ref,
    q_ref,
    k_ref,
    v_ref,
    wk_ref,
    state_in,
    mix_ref,
    level_ref,
    slope_ref,
    state_ref,
    turned_ref,
):
    rows, width = k_ref.shape
    heads = q_ref.shape[1] // width
    pairs = heads // 2

    @pl.when(place_ref[0] < distance)
    def _():
        mix_ref[...] = jnp.zeros_like(mix_ref)
        slope_ref[...] = jnp.zeros_like(slope_ref)
        level_ref[...] = jnp.full_like(level_ref, MASKED_SCORE)
        state_ref[...] = state_in[...]

    @pl.when(place_ref[0] >= distance)
    def _():
        @pl.when(pl.program_id(0) == 0)
        def _():
            turned_ref[...] = turned_with_ones(v_ref[...])

        tile = tile_of(rows)
        tiles = rows // tile
        wide = with_ones(v_ref[...])
        keys = k_ref[...]
        weights = [
            jnp.concatenate((wk_ref[2 * pair], wk_ref[2 * pair + 1]), axis=1)
            for pair in range(pairs)
        ]
        states = [state_in[pair] for pair in range(pairs)]

        def feature_task(pair, i):
            pre = dot(keys[columns(i, tile)], weights[pair], NN)
            yield
            feat, slope = softplus_and_slope(pre)
            slope_ref[columns(i, tile), columns(pair, 2 * width)] = slope.astype(BF16)
            states[pair] = states[pair] + dot(turned_ref[:, columns(i, tile)], feat, NN)
            if i == tiles - 1:
                state_ref[pair] = states[pair]

        def score_parts(unit):
            b, i = unit
            return [dot(q_ref[columns(i, tile), columns(b, width)], keys, NT)]

        store = storing(mix_ref, level_ref, tile, width, heads)
        tasks = []
        for i in range(tiles):
            for pair in range(pairs):
                tasks.append(feature_task(pair, i))
                for b in (2 * pair, 2 * pair + 1):
                    tasks.append(mixture_task(scale, score_parts, wide, (b, i), store))
        interleave(tasks, CHUNK_WINDOW)


def student(total_tokens, chunk_count, place_ref, q_ref, k_ref, v_ref, *refs):
    refs = list(refs)
    chunk_keys = [refs.pop(0) for _ in range(chunk_count)]
    chunk_values = [refs.pop(0) for _ in range(chunk_count)]
    mix_refs = [refs.pop(0) for _ in range(chunk_count + 1)]
    level_refs = [refs.pop(0) for _ in range(chunk_count + 1)]
    slope_refs = [refs.pop(0) for _ in range(chunk_count)]
    wq_ref, wk_ref, state_ref, out_ref, wide_t, keys_t, chunk_t, wk_acc = refs
    rows, width = k_ref.shape
    heads = q_ref.shape[1] // width
    pairs = heads // 2
    tile = tile_of(rows)
    tiles = rows // tile
    mask = causal_mask(tile)

    @pl.when(pl.program_id(0) == 0)
    def _():
        wide_t[...] = turned_with_ones(v_ref[...])
        keys_t[...] = turned(k_ref[...])
        for c in range(chunk_count):

            @pl.when(place_ref[0] >= c + 1)
            def _(c=c):
                chunk_t[c] = turned(chunk_keys[c][...])

    head_list = range(heads)
    tile_list = range(tiles)
    wide = [with_ones(v_ref[columns(i, tile), :]) for i in tile_list]
    key_feat, key_slope, states, shares = {}, {}, {}, {}

    def key_task(pair):
        weight = jnp.concatenate((wk_ref[2 * pair], wk_ref[2 * pair + 1]), axis=1)
        running = state_ref[pair]
        pre = dot(k_ref[columns(0, tile), :], weight, NN)
        for i in tile_list:
            yield
            later = dot(k_ref[columns(i + 1, tile), :], weight, NN) if i + 1 < tiles else None
            feat, slope = softplus_and_slope(pre)
            pre = later
            key_slope[pair, i] = slope
            for side in range(2):
                here = columns(side, width)
                key_feat[2 * pair + side, i] = feat[:, here]
                norm = jnp.broadcast_to(running[width : width + 1, here], (width, width))
                states[2 * pair + side, i] = jnp.concatenate(
                    (running[:width, here], norm), axis=0
                ).astype(BF16)
            if i + 1 < tiles:
                running = running + dot(wide_t[:, columns(i, tile)], feat, NN)

    def share_task(i):
        levels = [ref[columns(i, tile), :] for ref in level_refs]
        peak = functools.reduce(jnp.maximum, levels)
        parts = [jnp.exp2(level - peak) for level in levels]
        inverse = 1.0 / functools.reduce(jnp.add, parts)
        shares[i] = [part * inverse for part in parts]
        yield

    interleave([key_task(pair) for pair in range(pairs)] + [share_task(i) for i in tile_list], 4)

    backs, query_change, key_change = {}, {}, {}

    def unit_task(b, i):
        here, head = columns(i, tile), columns(b, width)
        pre = dot(q_ref[here, head], wq_ref[b], NN)
        yield
        feat, slope = softplus_and_slope(pre)
        affinity = dot(feat, key_feat[b, i], NT)
        mixed = dot(feat, states[b, i], NT)
        yield
        affinity = jnp.where(mask, affinity, 0.0).astype(BF16)
        mixed = mixed + dot(affinity, wide[i], NN)
        teacher = functools.reduce(
            jnp.add,
            [
                share[:, b : b + 1] * ref[here, head].astype(F32)
                for share, ref in zip(shares[i], mix_refs)
            ],
        )
        teacher = teacher.astype(BF16).astype(F32)
        yield
        inverse = 1.0 / mixed[:, width:]
        result = mixed[:, :width] * inverse
        grad_out = (result - teacher) * (2.0 / total_tokens)
        grad_denom = jnp.sum(grad_out * result, axis=1, keepdims=True) * inverse * (-1.0 / width)
        grads = jnp.concatenate((grad_out * inverse, grad_denom), axis=1).astype(BF16)
        grad_aff = dot(grads, wide[i], NT)
        backs[b, i] = dot(feat, grads, TN)
        grad_qfeat = dot(grads, states[b, i], NN)
        yield
        grad_aff = jnp.where(mask, grad_aff, 0.0).astype(BF16)
        grad_qfeat = grad_qfeat + dot(grad_aff, key_feat[b, i], NN)
        key_change[b, i] = dot(grad_aff, feat, TN)
        yield
        query_change[b, i] = (grad_qfeat * slope).astype(BF16)

    interleave([unit_task(b, i) for b in head_list for i in tile_list], UNIT_WINDOW)

    whole = [None] * pairs

    def query_weight_task(b):
        change = jnp.concatenate([query_change[b, i] for i in tile_list], axis=0)
        out_ref[b, 0] = dot(q_ref[:, columns(b, width)], change, TN).astype(out_ref.dtype)
        yield

    def key_weight_task(pair):
        sides = (2 * pair, 2 * pair + 1)
        running = [backs[b, tiles - 1] for b in sides]
        changes = [None] * tiles
        for i in reversed(tile_list):
            both = jnp.concatenate([key_change[b, i] for b in sides], axis=1)
            if i + 1 < tiles:
                later = jnp.concatenate(running, axis=0).astype(BF16)
                both = both + dot(wide[i], later, NT)
                running = [old + backs[b, i] for old, b in zip(running, sides)]
                yield
            changes[i] = (both * key_slope[pair, i]).astype(BF16)
        whole[pair] = jnp.concatenate(running, axis=0).astype(BF16)
        wk_acc[pair] = dot(keys_t[...], jnp.concatenate(changes, axis=0), NN)

    tasks = []
    for pair in range(pairs):
        tasks += [query_weight_task(2 * pair), query_weight_task(2 * pair + 1)]
        tasks.append(key_weight_task(pair))
    interleave(tasks, 3)

    for c in range(chunk_count):

        @pl.when(place_ref[0] >= c + 1)
        def _(c=c):
            values = with_ones(chunk_values[c][...])
            sums = [None] * pairs

            def chunk_task(pair, i):
                here = columns(i, tile)
                slope = slope_refs[c][here, columns(pair, 2 * width)]
                change = dot(values[here], whole[pair], NT)
                yield
                change = (change * slope.astype(F32)).astype(BF16)
                term = dot(chunk_t[c, :, here], change, NN)
                sums[pair] = term if i == 0 else sums[pair] + term
                if i == tiles - 1:
                    wk_acc[pair] += sums[pair]

            interleave([chunk_task(pair, i) for pair in range(pairs) for i in tile_list], 2)

    for b in head_list:
        out_ref[b, 1] = wk_acc[b // 2][:, columns(b % 2, width)].astype(out_ref.dtype)


def params():
    return pltpu.CompilerParams(
        vmem_limit_bytes=VMEM_BYTES, dimension_semantics=("arbitrary",)
    )


def cost(microseconds):
    return pl.CostEstimate(
        flops=int(microseconds * 1e9), bytes_accessed=int(microseconds * 3e6), transcendentals=0
    )


class Plan:
    def __init__(self, rows, half, groups, width, feats):
        self.rows, self.half, self.groups, self.width, self.feats = rows, half, groups, width, feats
        self.per_group = half // groups
        self.heads = math.gcd(self.per_group, BLOCK_HEADS)
        self.steps = half // self.heads
        self.mix_type = jax.ShapeDtypeStruct((rows, half * width), BF16)
        self.level_type = jax.ShapeDtypeStruct((rows, self.steps * LANES), F32)
        self.state_type = jax.ShapeDtypeStruct((half // 2, width + 16, 2 * feats), F32)

    def specs(self, start=0):
        rows, width, heads, steps = self.rows, self.width, self.heads, self.steps
        groups, per_group = self.groups, self.per_group
        return dict(
            q=pl.BlockSpec((rows, heads * width), lambda h, *_: (0, start + h)),
            k=pl.BlockSpec((rows, width), lambda h, *_: (0, (start + h) * heads // per_group)),
            v=pl.BlockSpec(
                (rows, width), lambda h, *_: (0, groups + (start + h) * heads // per_group)
            ),
            level=pl.BlockSpec((rows, LANES), lambda h, *_: (0, start + h)),
            w=pl.BlockSpec(
                (heads, width, self.feats),
                lambda h, place: (place[1] * steps + start + h, 0, 0),
            ),
            state=pl.BlockSpec(
                (heads // 2, width + 16, 2 * self.feats), lambda h, *_: (start + h, 0, 0)
            ),
        )

    def local(self, place, queries, other_q, kv):
        at, steps = self.specs(), self.steps
        part, block = queries.shape[0], self.heads * self.width
        return pl.pallas_call(
            functools.partial(local_attention, self.width ** (-0.5) * LOG2E),
            grid_spec=pltpu.PrefetchScalarGridSpec(
                num_scalar_prefetch=1,
                grid=(steps,),
                in_specs=[
                    pl.BlockSpec((part, block), lambda h, place: (0, place[1] * steps + h)),
                    pl.BlockSpec((part, block), lambda h, *_: (0, h)),
                    at["k"],
                    at["v"],
                ],
                out_specs=[at["q"], at["q"], at["level"]],
            ),
            out_shape=[self.mix_type, self.mix_type, self.level_type],
            compiler_params=params(),
            cost_estimate=cost(12),
            name="local_attention",
        )(place, queries, other_q, kv, kv)

    def chunk(self, distance, place, q, chunk, feat_k, state):
        at = self.specs()
        return pl.pallas_call(
            functools.partial(chunk_attention, self.width ** (-0.5) * LOG2E, distance),
            grid_spec=pltpu.PrefetchScalarGridSpec(
                num_scalar_prefetch=1,
                grid=(self.steps,),
                in_specs=[at["q"], at["k"], at["v"], at["w"], at["state"]],
                out_specs=[at["q"], at["level"], at["q"], at["state"]],
                scratch_shapes=[pltpu.VMEM((self.width + 16, self.rows), BF16)],
            ),
            out_shape=[self.mix_type, self.level_type, self.mix_type, self.state_type],
            compiler_params=params(),
            cost_estimate=cost(18),
            name="chunk_attention",
        )(place, q, chunk, chunk, feat_k, state)

    def student(
        self, start, steps, chips, place, q, kv, chunks, mixes, levels, slopes, wq, wk, state
    ):
        at = self.specs(start)
        count, width, rows = len(chunks), self.width, self.rows
        grad_shape = (self.heads, 2, width, self.feats)
        return pl.pallas_call(
            functools.partial(student, chips * rows, count),
            grid_spec=pltpu.PrefetchScalarGridSpec(
                num_scalar_prefetch=1,
                grid=(steps,),
                in_specs=[at["q"], at["k"], at["v"]]
                + [at["k"]] * count
                + [at["v"]] * count
                + [at["q"]] * len(mixes)
                + [at["level"]] * len(levels)
                + [at["q"]] * count
                + [at["w"], at["w"], at["state"]],
                out_specs=pl.BlockSpec(grad_shape, lambda h, *_: (h, 0, 0, 0)),
                scratch_shapes=[
                    pltpu.VMEM((width + 16, rows), BF16),
                    pltpu.VMEM((width, rows), BF16),
                    pltpu.VMEM((max(1, count), width, rows), BF16),
                    pltpu.VMEM((self.heads // 2, width, 2 * self.feats), F32),
                ],
            ),
            out_shape=jax.ShapeDtypeStruct((steps * self.heads,) + grad_shape[1:], BF16),
            compiler_params=params(),
            cost_estimate=cost(12 * steps),
            name="student",
        )(place, q, kv, kv, *chunks, *chunks, *mixes, *levels, *slopes, wq, wk, state)


def body(queries, keys, values, feat_q, feat_k):
    row_count = queries.shape[0]
    heads_here, width, feat_count = feat_q.shape
    seq_count = lax.axis_size("seq")
    chips = seq_count // CORES
    seq_place = lax.axis_index("seq")
    core, chip = seq_place % CORES, seq_place // CORES
    head_place = lax.axis_index("head")
    spread = max(1, HEADS // KV_HEADS // heads_here)
    key_value = jnp.stack((keys, values))
    for bit_index in range(spread.bit_length() - 1):
        partner = from_partner(key_value, "head", bit_index)
        upper_half = head_place // (1 << bit_index) % 2 == 1
        key_value = jnp.where(
            upper_half,
            jnp.concatenate((partner, key_value), axis=2),
            jnp.concatenate((key_value, partner), axis=2),
        )
    groups = key_value.shape[2] // width
    half = heads_here // CORES
    core_route = [(i, i ^ 1) for i in range(seq_count)]
    first = core == 0

    if groups > 1:
        own_groups = groups // CORES
        split = own_groups * width
        low, high = key_value[:, :, :split], key_value[:, :, split:]
        kept, sent = jnp.where(first, low, high), jnp.where(first, high, low)
    else:
        own_groups = groups
        kept = sent = key_value
    got = lax.ppermute(sent, "seq", core_route)
    kv = jnp.where(
        first, jnp.concatenate((kept, got), axis=1), jnp.concatenate((got, kept), axis=1)
    )
    kv = jnp.concatenate((kv[0], kv[1]), axis=1)
    other_q = lax.ppermute(
        lax.dynamic_slice_in_dim(queries, (1 - core) * half * width, half * width, 1),
        "seq",
        core_route,
    )
    rows = CORES * row_count
    chunks = []
    for distance in range(1, chips):
        route = [(i, i + CORES * distance) for i in range(seq_count - CORES * distance)]
        chunks.append(lax.ppermute(kv, "seq", route))

    plan = Plan(rows, half, own_groups, width, feat_count)
    place = jnp.stack((chip, core)).astype(jnp.int32)
    q, mix, level = plan.local(place, queries, other_q, kv)
    state = jnp.zeros(plan.state_type.shape, F32)
    mixes, levels, slopes = [mix], [level], []
    for index, chunk in enumerate(chunks):
        mix, level, slope, state = plan.chunk(index + 1, place, q, chunk, feat_k, state)
        mixes.append(mix)
        levels.append(level)
        slopes.append(slope)
    total_parts = sum(STUDENT_PARTS)
    parts = STUDENT_PARTS if plan.steps % total_parts == 0 else (1,)
    unit = plan.steps // sum(parts)
    results, start = [], 0
    for part in parts:
        steps = part * unit
        grads = plan.student(
            start, steps, chips, place, q, kv, chunks, mixes, levels, slopes, feat_q, feat_k, state
        )
        start += steps
        results.append(reduced(grads, chip, chips, seq_count, core_route))
    own = jnp.concatenate([pair[0] for pair in results], axis=0)
    other = jnp.concatenate([pair[1] for pair in results], axis=0)
    both = jnp.where(
        first, jnp.concatenate((own, other), axis=0), jnp.concatenate((other, own), axis=0)
    ).astype(F32)
    return both[:, 0], both[:, 1]


def reduced(grads, chip, chips, seq_count, core_route):
    flat = grads.reshape(-1, grads.shape[-1])
    share = flat.shape[0] // chips

    def route(distance):
        return [(i, (i + CORES * distance) % seq_count) for i in range(seq_count)]

    def part(index):
        return lax.dynamic_slice_in_dim(flat, index % chips * share, share, 0)

    mine = part(chip).astype(F32)
    for distance in range(1, chips):
        mine += lax.ppermute(part(chip + distance), "seq", route(distance)).astype(F32)
    mine = mine.astype(BF16)
    whole = lax.dynamic_update_slice_in_dim(jnp.zeros_like(flat), mine, chip * share, 0)
    for distance in range(1, chips):
        got = lax.ppermute(mine, "seq", route(distance))
        whole = lax.dynamic_update_slice_in_dim(
            whole, got, (chip - distance + chips) % chips * share, 0
        )
    whole = whole.reshape(grads.shape)
    return whole, lax.ppermute(whole, "seq", core_route)


def solution(mesh):
    return jax.shard_map(
        body,
        mesh=mesh,
        in_specs=(
            P("seq", "head"),
            P("seq", "head"),
            P("seq", "head"),
            P("head", None, None),
            P("head", None, None),
        ),
        out_specs=(P("head", None, None), P("head", None, None)),
        check_vma=False,
    )
```

```python
import functools
import math

import jax
import jax.numpy as jnp
from jax import lax
from jax.experimental import pallas as pl
from jax.experimental.pallas import tpu as pltpu
from jax.sharding import PartitionSpec as P

HEADS = 128
KV_HEADS = 8
CORES = 2
SUBLANES = 8
BLOCK_HEADS = 4
STUDENT_PARTS = (2, 1, 1)
LOCAL_WINDOW = 2
CHUNK_WINDOW = 2
UNIT_WINDOW = 8
LOG2E = math.log2(math.e)
LN2 = math.log(2.0)
MASKED_SCORE = -1e30
SAFE_LOW = 2.0**-100
SAFE_HIGH = 2.0**120
VMEM_BYTES = 56 * 1024 * 1024
F32 = jnp.float32
BF16 = jnp.bfloat16

NN = (((1,), (0,)), ((), ()))
NT = (((1,), (1,)), ((), ()))
TN = (((0,), (0,)), ((), ()))


def dot(a, b, form):
    return lax.dot_general(a, b, form, preferred_element_type=F32)


def from_partner(block, axis, stride):
    count = lax.axis_size(axis)
    route = []
    for low in range(count):
        high = low | 1 << stride
        if high != low and high < count:
            route += [(low, high), (high, low)]
    return lax.ppermute(block, axis, route)


def tile_of(rows):
    return 256 if rows % 256 == 0 else rows


def with_ones(values):
    return jnp.concatenate((values, jnp.ones_like(values)), axis=1)


def turned(block):
    return block.astype(F32).T.astype(BF16)


def turned_with_ones(values):
    return jnp.concatenate((turned(values), jnp.ones((16, values.shape[0]), BF16)), axis=0)


def softplus_and_slope(pre):
    scaled = pre * LOG2E
    decay = jnp.exp2(jnp.minimum(scaled, -scaled))
    small = decay * (LOG2E - (0.5 * LOG2E) * decay)
    log_term = jnp.where(decay < 0.01, small, jnp.log2(1.0 + decay))
    level = jnp.maximum(scaled, 0.0) + log_term
    return (level * LN2).astype(BF16), jnp.exp2(scaled - level)


def masked(mask, block, other):
    return block if mask is True else jnp.where(mask, block, other)


def columns(index, width):
    return slice(index * width, (index + 1) * width)


def causal_mask(rows):
    return lax.broadcasted_iota(jnp.int32, (rows, rows), 0) >= lax.broadcasted_iota(
        jnp.int32, (rows, rows), 1
    )


def interleave(tasks, window):
    waiting, active = list(tasks), []
    while waiting or active:
        if waiting and len(active) < window:
            active.append(waiting.pop(0))
        for task in active[::-1]:
            if next(task, active) is active:
                active.remove(task)


def mixture_task(scale, shifted, score_parts, values_t, unit, store):
    parts = score_parts(unit)
    yield
    peak = 0.0
    if shifted:
        peak = scale * functools.reduce(
            jnp.maximum,
            [jnp.max(masked(mask, part, MASKED_SCORE), axis=0, keepdims=True) for part, mask in parts],
        )
    weights = [
        masked(
            mask, jnp.exp2(part * scale - peak if shifted else part * scale), 0.0
        ).astype(BF16)
        for part, mask in parts
    ]
    weights = weights[0] if len(weights) == 1 else jnp.concatenate(weights, axis=0)
    mixed = dot(values_t[:, : weights.shape[0]], weights, NN)
    width = mixed.shape[0] - 16
    total = mixed[width : width + 1]
    store(unit, (mixed[:width] * (1.0 / total)).astype(BF16), total, peak + jnp.log2(total))


def attend(scale, units, score_parts, values_t, mix_ref, level_ref, tile, width, others, window):
    totals = []

    def store(unit, mixture, total, level):
        b, i = unit
        mix_ref[columns(b, width), columns(i, tile)] = mixture
        level_ref[0, b : b + 1, columns(i, tile)] = level
        totals.append(total)

    def tasks(shifted):
        return [
            mixture_task(scale, shifted, score_parts, values_t, unit, store) for unit in units
        ]

    first, spread = tasks(False), []
    for place, task in enumerate(first):
        spread += others[place * len(others) // len(first) : (place + 1) * len(others) // len(first)]
        spread.append(task)
    interleave(spread, window)
    low = jnp.min(functools.reduce(jnp.minimum, totals))
    high = jnp.max(functools.reduce(jnp.maximum, totals))

    @pl.when(jnp.logical_not((low > SAFE_LOW) & (high < SAFE_HIGH)))
    def _():
        interleave(tasks(True), window)


def local_attention(
    scale, place_ref, own_ref, other_ref, k_ref, v_ref, q_ref, mix_ref, level_ref, turned_ref
):
    rows, width = k_ref.shape
    heads = q_ref.shape[1] // width
    part = own_ref.shape[0]
    core = place_ref[1]
    q_ref[pl.ds(pl.multiple_of(core * part, part), part), :] = own_ref[...]
    q_ref[pl.ds(pl.multiple_of((1 - core) * part, part), part), :] = other_ref[...]
    @pl.when(pl.program_id(0) == 0)
    def _():
        turned_ref[...] = turned_with_ones(v_ref[...])

    tile = tile_of(rows)
    mask = lax.broadcasted_iota(jnp.int32, (tile, tile), 0) <= lax.broadcasted_iota(
        jnp.int32, (tile, tile), 1
    )

    def score_parts(unit):
        b, i = unit
        query = q_ref[columns(i, tile), columns(b, width)]
        last = (dot(k_ref[columns(i, tile), :], query, NT), mask)
        return [last] if i == 0 else [(dot(k_ref[: i * tile, :], query, NT), True), last]

    units = [(b, i) for i in range(rows // tile) for b in range(heads)]
    attend(
        scale, units, score_parts, turned_ref, mix_ref, level_ref, tile, width, [], LOCAL_WINDOW
    )


def chunk_attention(
    scale,
    distance,
    place_ref,
    q_ref,
    k_ref,
    v_ref,
    wk_ref,
    state_in,
    mix_ref,
    level_ref,
    slope_ref,
    state_ref,
    turned_ref,
):
    rows, width = k_ref.shape
    heads = q_ref.shape[1] // width
    pairs = heads // 2

    @pl.when(place_ref[0] < distance)
    def _():
        mix_ref[...] = jnp.zeros_like(mix_ref)
        slope_ref[...] = jnp.zeros_like(slope_ref)
        level_ref[...] = jnp.full_like(level_ref, MASKED_SCORE)
        state_ref[...] = state_in[...]

    @pl.when(place_ref[0] >= distance)
    def _():
        @pl.when(pl.program_id(0) == 0)
        def _():
            turned_ref[...] = turned_with_ones(v_ref[...])

        tile = tile_of(rows)
        tiles = rows // tile
        keys = k_ref[...]
        weights = [
            jnp.concatenate((wk_ref[2 * pair], wk_ref[2 * pair + 1]), axis=1)
            for pair in range(pairs)
        ]
        states = [state_in[pair] for pair in range(pairs)]

        def feature_task(pair, i):
            pre = dot(keys[columns(i, tile)], weights[pair], NN)
            yield
            feat, slope = softplus_and_slope(pre)
            slope_ref[columns(i, tile), columns(pair, 2 * width)] = slope.astype(BF16)
            states[pair] = states[pair] + dot(turned_ref[:, columns(i, tile)], feat, NN)
            if i == tiles - 1:
                state_ref[pair] = states[pair]

        def score_parts(unit):
            b, i = unit
            return [(dot(keys, q_ref[columns(i, tile), columns(b, width)], NT), True)]

        units = [(b, i) for i in range(tiles) for b in range(heads)]
        features = [feature_task(pair, i) for i in range(tiles) for pair in range(pairs)]
        attend(
            scale,
            units,
            score_parts,
            turned_ref,
            mix_ref,
            level_ref,
            tile,
            width,
            features,
            CHUNK_WINDOW,
        )


def student(total_tokens, chunk_count, place_ref, q_ref, k_ref, v_ref, *refs):
    refs = list(refs)
    chunk_keys = [refs.pop(0) for _ in range(chunk_count)]
    chunk_values = [refs.pop(0) for _ in range(chunk_count)]
    mix_refs = [refs.pop(0) for _ in range(chunk_count + 1)]
    level_refs = [refs.pop(0) for _ in range(chunk_count + 1)]
    slope_refs = [refs.pop(0) for _ in range(chunk_count)]
    wq_ref, wk_ref, state_ref, out_ref, wide_t, keys_t, chunk_t, wk_acc = refs
    rows, width = k_ref.shape
    heads = q_ref.shape[1] // width
    pairs = heads // 2
    tile = tile_of(rows)
    tiles = rows // tile
    mask = causal_mask(tile)

    @pl.when(pl.program_id(0) == 0)
    def _():
        wide_t[...] = turned_with_ones(v_ref[...])
        keys_t[...] = turned(k_ref[...])
        for c in range(chunk_count):

            @pl.when(place_ref[0] >= c + 1)
            def _(c=c):
                chunk_t[c] = turned(chunk_keys[c][...])

    head_list = range(heads)
    tile_list = range(tiles)
    wide = [with_ones(v_ref[columns(i, tile), :]) for i in tile_list]
    key_feat, key_slope, states, shares = {}, {}, {}, {}

    def key_task(pair):
        weight = jnp.concatenate((wk_ref[2 * pair], wk_ref[2 * pair + 1]), axis=1)
        running = state_ref[pair]
        pre = dot(k_ref[columns(0, tile), :], weight, NN)
        for i in tile_list:
            yield
            later = dot(k_ref[columns(i + 1, tile), :], weight, NN) if i + 1 < tiles else None
            feat, slope = softplus_and_slope(pre)
            pre = later
            key_slope[pair, i] = slope
            for side in range(2):
                here = columns(side, width)
                key_feat[2 * pair + side, i] = feat[:, here]
                norm = jnp.broadcast_to(running[width : width + 1, here], (width, width))
                states[2 * pair + side, i] = jnp.concatenate(
                    (running[:width, here], norm), axis=0
                ).astype(BF16)
            if i + 1 < tiles:
                running = running + dot(wide_t[:, columns(i, tile)], feat, NN)

    def share_task(i):
        levels = [ref[0, :, columns(i, tile)] for ref in level_refs]
        peak = functools.reduce(jnp.maximum, levels)
        parts = [jnp.exp2(level - peak) for level in levels]
        inverse = 1.0 / functools.reduce(jnp.add, parts)
        shares[i] = [part * inverse for part in parts]
        yield

    interleave([key_task(pair) for pair in range(pairs)] + [share_task(i) for i in tile_list], 4)

    backs, query_change, key_change = {}, {}, {}

    def unit_task(b, i):
        here, head = columns(i, tile), columns(b, width)
        pre = dot(q_ref[here, head], wq_ref[b], NN)
        yield
        feat, slope = softplus_and_slope(pre)
        affinity = dot(feat, key_feat[b, i], NT)
        mixed = dot(feat, states[b, i], NT)
        yield
        affinity = jnp.where(mask, affinity, 0.0).astype(BF16)
        mixed = mixed + dot(affinity, wide[i], NN)
        teacher = functools.reduce(
            jnp.add,
            [
                share[b : b + 1] * ref[head, here].astype(F32)
                for share, ref in zip(shares[i], mix_refs)
            ],
        )
        teacher = turned(teacher).astype(F32)
        yield
        inverse = 1.0 / mixed[:, width:]
        result = mixed[:, :width] * inverse
        grad_out = (result - teacher) * (2.0 / total_tokens)
        grad_denom = jnp.sum(grad_out * result, axis=1, keepdims=True) * inverse * (-1.0 / width)
        grads = jnp.concatenate((grad_out * inverse, grad_denom), axis=1).astype(BF16)
        grad_aff = dot(grads, wide[i], NT)
        backs[b, i] = dot(feat, grads, TN)
        grad_qfeat = dot(grads, states[b, i], NN)
        yield
        grad_aff = jnp.where(mask, grad_aff, 0.0).astype(BF16)
        grad_qfeat = grad_qfeat + dot(grad_aff, key_feat[b, i], NN)
        key_change[b, i] = dot(grad_aff, feat, TN)
        yield
        query_change[b, i] = (grad_qfeat * slope).astype(BF16)

    interleave([unit_task(b, i) for b in head_list for i in tile_list], UNIT_WINDOW)

    whole = [None] * pairs

    def query_weight_task(b):
        change = jnp.concatenate([query_change[b, i] for i in tile_list], axis=0)
        out_ref[b, 0] = dot(q_ref[:, columns(b, width)], change, TN).astype(out_ref.dtype)
        yield

    def key_weight_task(pair):
        sides = (2 * pair, 2 * pair + 1)
        running = [backs[b, tiles - 1] for b in sides]
        changes = [None] * tiles
        for i in reversed(tile_list):
            both = jnp.concatenate([key_change[b, i] for b in sides], axis=1)
            if i + 1 < tiles:
                later = jnp.concatenate(running, axis=0).astype(BF16)
                both = both + dot(wide[i], later, NT)
                running = [old + backs[b, i] for old, b in zip(running, sides)]
                yield
            changes[i] = (both * key_slope[pair, i]).astype(BF16)
        whole[pair] = jnp.concatenate(running, axis=0).astype(BF16)
        wk_acc[pair] = dot(keys_t[...], jnp.concatenate(changes, axis=0), NN)

    tasks = []
    for pair in range(pairs):
        tasks += [query_weight_task(2 * pair), query_weight_task(2 * pair + 1)]
        tasks.append(key_weight_task(pair))
    interleave(tasks, 3)

    for c in range(chunk_count):

        @pl.when(place_ref[0] >= c + 1)
        def _(c=c):
            values = with_ones(chunk_values[c][...])
            sums = [None] * pairs

            def chunk_task(pair, i):
                here = columns(i, tile)
                slope = slope_refs[c][here, columns(pair, 2 * width)]
                change = dot(values[here], whole[pair], NT)
                yield
                change = (change * slope.astype(F32)).astype(BF16)
                term = dot(chunk_t[c, :, here], change, NN)
                sums[pair] = term if i == 0 else sums[pair] + term
                if i == tiles - 1:
                    wk_acc[pair] += sums[pair]

            interleave([chunk_task(pair, i) for pair in range(pairs) for i in tile_list], 2)

    for b in head_list:
        out_ref[b, 1] = wk_acc[b // 2][:, columns(b % 2, width)].astype(out_ref.dtype)


def params():
    return pltpu.CompilerParams(
        vmem_limit_bytes=VMEM_BYTES, dimension_semantics=("arbitrary",)
    )


def cost(microseconds):
    return pl.CostEstimate(
        flops=int(microseconds * 1e9), bytes_accessed=int(microseconds * 3e6), transcendentals=0
    )


class Plan:
    def __init__(self, rows, half, groups, width, feats):
        self.rows, self.half, self.groups, self.width, self.feats = rows, half, groups, width, feats
        self.per_group = half // groups
        self.heads = math.gcd(self.per_group, BLOCK_HEADS)
        self.steps = half // self.heads
        self.mix_type = jax.ShapeDtypeStruct((half * width, rows), BF16)
        self.q_type = jax.ShapeDtypeStruct((rows, half * width), BF16)
        self.level_type = jax.ShapeDtypeStruct((self.steps, SUBLANES, rows), F32)
        self.state_type = jax.ShapeDtypeStruct((half // 2, width + 16, 2 * feats), F32)

    def specs(self, start=0):
        rows, width, heads, steps = self.rows, self.width, self.heads, self.steps
        groups, per_group = self.groups, self.per_group
        return dict(
            q=pl.BlockSpec((rows, heads * width), lambda h, *_: (0, start + h)),
            k=pl.BlockSpec((rows, width), lambda h, *_: (0, (start + h) * heads // per_group)),
            v=pl.BlockSpec(
                (rows, width), lambda h, *_: (0, groups + (start + h) * heads // per_group)
            ),
            mix=pl.BlockSpec((heads * width, rows), lambda h, *_: (start + h, 0)),
            level=pl.BlockSpec((1, SUBLANES, rows), lambda h, *_: (start + h, 0, 0)),
            w=pl.BlockSpec(
                (heads, width, self.feats),
                lambda h, place: (place[1] * steps + start + h, 0, 0),
            ),
            state=pl.BlockSpec(
                (heads // 2, width + 16, 2 * self.feats), lambda h, *_: (start + h, 0, 0)
            ),
        )

    def local(self, place, queries, other_q, kv):
        at, steps = self.specs(), self.steps
        part, block = queries.shape[0], self.heads * self.width
        return pl.pallas_call(
            functools.partial(local_attention, self.width ** (-0.5) * LOG2E),
            grid_spec=pltpu.PrefetchScalarGridSpec(
                num_scalar_prefetch=1,
                grid=(steps,),
                in_specs=[
                    pl.BlockSpec((part, block), lambda h, place: (0, place[1] * steps + h)),
                    pl.BlockSpec((part, block), lambda h, *_: (0, h)),
                    at["k"],
                    at["v"],
                ],
                out_specs=[at["q"], at["mix"], at["level"]],
                scratch_shapes=[pltpu.VMEM((self.width + 16, self.rows), BF16)],
            ),
            out_shape=[self.q_type, self.mix_type, self.level_type],
            compiler_params=params(),
            cost_estimate=cost(12),
            name="local_attention",
        )(place, queries, other_q, kv, kv)

    def chunk(self, distance, place, q, chunk, feat_k, state):
        at = self.specs()
        return pl.pallas_call(
            functools.partial(chunk_attention, self.width ** (-0.5) * LOG2E, distance),
            grid_spec=pltpu.PrefetchScalarGridSpec(
                num_scalar_prefetch=1,
                grid=(self.steps,),
                in_specs=[at["q"], at["k"], at["v"], at["w"], at["state"]],
                out_specs=[at["mix"], at["level"], at["q"], at["state"]],
                scratch_shapes=[pltpu.VMEM((self.width + 16, self.rows), BF16)],
            ),
            out_shape=[self.mix_type, self.level_type, self.q_type, self.state_type],
            compiler_params=params(),
            cost_estimate=cost(18),
            name="chunk_attention",
        )(place, q, chunk, chunk, feat_k, state)

    def student(
        self, start, steps, chips, place, q, kv, chunks, mixes, levels, slopes, wq, wk, state
    ):
        at = self.specs(start)
        count, width, rows = len(chunks), self.width, self.rows
        grad_shape = (self.heads, 2, width, self.feats)
        return pl.pallas_call(
            functools.partial(student, chips * rows, count),
            grid_spec=pltpu.PrefetchScalarGridSpec(
                num_scalar_prefetch=1,
                grid=(steps,),
                in_specs=[at["q"], at["k"], at["v"]]
                + [at["k"]] * count
                + [at["v"]] * count
                + [at["mix"]] * len(mixes)
                + [at["level"]] * len(levels)
                + [at["q"]] * count
                + [at["w"], at["w"], at["state"]],
                out_specs=pl.BlockSpec(grad_shape, lambda h, *_: (h, 0, 0, 0)),
                scratch_shapes=[
                    pltpu.VMEM((width + 16, rows), BF16),
                    pltpu.VMEM((width, rows), BF16),
                    pltpu.VMEM((max(1, count), width, rows), BF16),
                    pltpu.VMEM((self.heads // 2, width, 2 * self.feats), F32),
                ],
            ),
            out_shape=jax.ShapeDtypeStruct((steps * self.heads,) + grad_shape[1:], BF16),
            compiler_params=params(),
            cost_estimate=cost(12 * steps),
            name="student",
        )(place, q, kv, kv, *chunks, *chunks, *mixes, *levels, *slopes, wq, wk, state)


def body(queries, keys, values, feat_q, feat_k):
    row_count = queries.shape[0]
    heads_here, width, feat_count = feat_q.shape
    seq_count = lax.axis_size("seq")
    chips = seq_count // CORES
    seq_place = lax.axis_index("seq")
    core, chip = seq_place % CORES, seq_place // CORES
    head_place = lax.axis_index("head")
    spread = max(1, HEADS // KV_HEADS // heads_here)
    key_value = jnp.stack((keys, values))
    for bit_index in range(spread.bit_length() - 1):
        partner = from_partner(key_value, "head", bit_index)
        upper_half = head_place // (1 << bit_index) % 2 == 1
        key_value = jnp.where(
            upper_half,
            jnp.concatenate((partner, key_value), axis=2),
            jnp.concatenate((key_value, partner), axis=2),
        )
    groups = key_value.shape[2] // width
    half = heads_here // CORES
    core_route = [(i, i ^ 1) for i in range(seq_count)]
    first = core == 0

    if groups > 1:
        own_groups = groups // CORES
        split = own_groups * width
        low, high = key_value[:, :, :split], key_value[:, :, split:]
        kept, sent = jnp.where(first, low, high), jnp.where(first, high, low)
    else:
        own_groups = groups
        kept = sent = key_value
    got = lax.ppermute(sent, "seq", core_route)
    kv = jnp.where(
        first, jnp.concatenate((kept, got), axis=1), jnp.concatenate((got, kept), axis=1)
    )
    kv = jnp.concatenate((kv[0], kv[1]), axis=1)
    other_q = lax.ppermute(
        lax.dynamic_slice_in_dim(queries, (1 - core) * half * width, half * width, 1),
        "seq",
        core_route,
    )
    rows = CORES * row_count
    chunks = []
    for distance in range(1, chips):
        route = [(i, i + CORES * distance) for i in range(seq_count - CORES * distance)]
        chunks.append(lax.ppermute(kv, "seq", route))

    plan = Plan(rows, half, own_groups, width, feat_count)
    place = jnp.stack((chip, core)).astype(jnp.int32)
    q, mix, level = plan.local(place, queries, other_q, kv)
    state = jnp.zeros(plan.state_type.shape, F32)
    mixes, levels, slopes = [mix], [level], []
    for index, chunk in enumerate(chunks):
        mix, level, slope, state = plan.chunk(index + 1, place, q, chunk, feat_k, state)
        mixes.append(mix)
        levels.append(level)
        slopes.append(slope)
    total_parts = sum(STUDENT_PARTS)
    parts = STUDENT_PARTS if plan.steps % total_parts == 0 else (1,)
    unit = plan.steps // sum(parts)
    results, start = [], 0
    for part in parts:
        steps = part * unit
        if results:
            place, grads = lax.optimization_barrier((place, grads))
        grads = plan.student(
            start, steps, chips, place, q, kv, chunks, mixes, levels, slopes, feat_q, feat_k, state
        )
        start += steps
        results.append(grads)
    results = [reduced(grads, chip, chips, seq_count, core_route) for grads in results]
    own = jnp.concatenate([pair[0] for pair in results], axis=0)
    other = jnp.concatenate([pair[1] for pair in results], axis=0)
    both = jnp.where(
        first, jnp.concatenate((own, other), axis=0), jnp.concatenate((other, own), axis=0)
    ).astype(F32)
    return both[:, 0], both[:, 1]


def reduced(grads, chip, chips, seq_count, core_route):
    flat = grads.reshape(-1, grads.shape[-1])
    share = flat.shape[0] // chips

    def route(distance):
        return [(i, (i + CORES * distance) % seq_count) for i in range(seq_count)]

    def part(index):
        return lax.dynamic_slice_in_dim(flat, index % chips * share, share, 0)

    mine = part(chip).astype(F32)
    for distance in range(1, chips):
        mine += lax.ppermute(part(chip + distance), "seq", route(distance)).astype(F32)
    mine = mine.astype(BF16)
    whole = lax.dynamic_update_slice_in_dim(jnp.zeros_like(flat), mine, chip * share, 0)
    for distance in range(1, chips):
        got = lax.ppermute(mine, "seq", route(distance))
        whole = lax.dynamic_update_slice_in_dim(
            whole, got, (chip - distance + chips) % chips * share, 0
        )
    whole = whole.reshape(grads.shape)
    return whole, lax.ppermute(whole, "seq", core_route)


def solution(mesh):
    return jax.shard_map(
        body,
        mesh=mesh,
        in_specs=(
            P("seq", "head"),
            P("seq", "head"),
            P("seq", "head"),
            P("head", None, None),
            P("head", None, None),
        ),
        out_specs=(P("head", None, None), P("head", None, None)),
        check_vma=False,
    )
```

```python
import functools
import math

import jax
import jax.numpy as jnp
from jax import lax
from jax.experimental import pallas as pl
from jax.experimental.pallas import tpu as pltpu
from jax.sharding import PartitionSpec as P

HEADS = 128
KV_HEADS = 8
CORES = 2
SUBLANES = 8
BLOCK_HEADS = 4
STUDENT_PARTS = (2, 1, 1)
LOCAL_WINDOW = 2
CHUNK_WINDOW = 2
UNIT_WINDOW = 8
LOG2E = math.log2(math.e)
LN2 = math.log(2.0)
MASKED_SCORE = -1e30
SAFE_LOW = 2.0**-100
SAFE_HIGH = 2.0**120
VMEM_BYTES = 56 * 1024 * 1024
F32 = jnp.float32
BF16 = jnp.bfloat16

NN = (((1,), (0,)), ((), ()))
NT = (((1,), (1,)), ((), ()))
TN = (((0,), (0,)), ((), ()))


def dot(a, b, form):
    return lax.dot_general(a, b, form, preferred_element_type=F32)


def from_partner(block, axis, stride):
    count = lax.axis_size(axis)
    route = []
    for low in range(count):
        high = low | 1 << stride
        if high != low and high < count:
            route += [(low, high), (high, low)]
    return lax.ppermute(block, axis, route)


def tile_of(rows):
    return 256 if rows % 256 == 0 else rows


def with_ones(values):
    return jnp.concatenate((values, jnp.ones_like(values)), axis=1)


def turned(block):
    return block.astype(F32).T.astype(BF16)


def turned_with_ones(values):
    return jnp.concatenate((turned(values), jnp.ones((16, values.shape[0]), BF16)), axis=0)


def softplus_and_slope(pre):
    scaled = pre * LOG2E
    decay = jnp.exp2(jnp.minimum(scaled, -scaled))
    small = decay * (LOG2E - (0.5 * LOG2E) * decay)
    log_term = jnp.where(decay < 0.01, small, jnp.log2(1.0 + decay))
    level = jnp.maximum(scaled, 0.0) + log_term
    return (level * LN2).astype(BF16), jnp.exp2(scaled - level)


def masked(mask, block, other):
    return block if mask is True else jnp.where(mask, block, other)


def columns(index, width):
    return slice(index * width, (index + 1) * width)


def causal_mask(rows):
    return lax.broadcasted_iota(jnp.int32, (rows, rows), 0) >= lax.broadcasted_iota(
        jnp.int32, (rows, rows), 1
    )


def interleave(tasks, window):
    waiting, active = list(tasks), []
    while waiting or active:
        if waiting and len(active) < window:
            active.append(waiting.pop(0))
        for task in active[::-1]:
            if next(task, active) is active:
                active.remove(task)


def mixture_task(scale, shifted, score_parts, values_t, unit, store):
    parts = score_parts(unit)
    yield
    peak = 0.0
    if shifted:
        peak = scale * functools.reduce(
            jnp.maximum,
            [jnp.max(masked(mask, part, MASKED_SCORE), axis=0, keepdims=True) for part, mask in parts],
        )
    weights = [
        masked(
            mask, jnp.exp2(part * scale - peak if shifted else part * scale), 0.0
        ).astype(BF16)
        for part, mask in parts
    ]
    weights = weights[0] if len(weights) == 1 else jnp.concatenate(weights, axis=0)
    mixed = dot(values_t[:, : weights.shape[0]], weights, NN)
    width = mixed.shape[0] - 16
    total = mixed[width : width + 1]
    store(unit, (mixed[:width] * (1.0 / total)).astype(BF16), total, peak + jnp.log2(total))


def attend(scale, units, score_parts, values_t, mix_ref, level_ref, tile, width, others, window):
    totals = []

    def store(unit, mixture, total, level):
        b, i = unit
        mix_ref[columns(b, width), columns(i, tile)] = mixture
        level_ref[0, b : b + 1, columns(i, tile)] = level
        totals.append(total)

    def tasks(shifted):
        return [
            mixture_task(scale, shifted, score_parts, values_t, unit, store) for unit in units
        ]

    first, spread = tasks(False), []
    for place, task in enumerate(first):
        spread += others[place * len(others) // len(first) : (place + 1) * len(others) // len(first)]
        spread.append(task)
    interleave(spread, window)
    low = jnp.min(functools.reduce(jnp.minimum, totals))
    high = jnp.max(functools.reduce(jnp.maximum, totals))

    @pl.when(jnp.logical_not((low > SAFE_LOW) & (high < SAFE_HIGH)))
    def _():
        interleave(tasks(True), window)


def local_attention(
    scale, place_ref, own_ref, other_ref, k_ref, v_ref, q_ref, mix_ref, level_ref, turned_ref
):
    rows, width = k_ref.shape
    heads = q_ref.shape[1] // width
    part = own_ref.shape[0]
    core = place_ref[1]
    q_ref[pl.ds(pl.multiple_of(core * part, part), part), :] = own_ref[...]
    q_ref[pl.ds(pl.multiple_of((1 - core) * part, part), part), :] = other_ref[...]
    @pl.when(pl.program_id(0) == 0)
    def _():
        turned_ref[...] = turned_with_ones(v_ref[...])

    tile = tile_of(rows)
    mask = lax.broadcasted_iota(jnp.int32, (tile, tile), 0) <= lax.broadcasted_iota(
        jnp.int32, (tile, tile), 1
    )

    def score_parts(unit):
        b, i = unit
        query = q_ref[columns(i, tile), columns(b, width)]
        last = (dot(k_ref[columns(i, tile), :], query, NT), mask)
        return [last] if i == 0 else [(dot(k_ref[: i * tile, :], query, NT), True), last]

    units = [(b, i) for i in range(rows // tile) for b in range(heads)]
    attend(
        scale, units, score_parts, turned_ref, mix_ref, level_ref, tile, width, [], LOCAL_WINDOW
    )


def chunk_attention(
    scale,
    distance,
    place_ref,
    q_ref,
    k_ref,
    v_ref,
    wk_ref,
    state_in,
    mix_ref,
    level_ref,
    slope_ref,
    state_ref,
    turned_ref,
):
    rows, width = k_ref.shape
    heads = q_ref.shape[1] // width
    pairs = heads // 2

    @pl.when(place_ref[0] < distance)
    def _():
        mix_ref[...] = jnp.zeros_like(mix_ref)
        slope_ref[...] = jnp.zeros_like(slope_ref)
        level_ref[...] = jnp.full_like(level_ref, MASKED_SCORE)
        state_ref[...] = state_in[...]

    @pl.when(place_ref[0] >= distance)
    def _():
        @pl.when(pl.program_id(0) == 0)
        def _():
            turned_ref[...] = turned_with_ones(v_ref[...])

        tile = tile_of(rows)
        tiles = rows // tile
        keys = k_ref[...]
        weights = [
            jnp.concatenate((wk_ref[2 * pair], wk_ref[2 * pair + 1]), axis=1)
            for pair in range(pairs)
        ]
        states = [state_in[pair] for pair in range(pairs)]

        def feature_task(pair, i):
            pre = dot(keys[columns(i, tile)], weights[pair], NN)
            yield
            feat, slope = softplus_and_slope(pre)
            slope_ref[columns(i, tile), columns(pair, 2 * width)] = slope.astype(BF16)
            states[pair] = states[pair] + dot(turned_ref[:, columns(i, tile)], feat, NN)
            if i == tiles - 1:
                state_ref[pair] = states[pair]

        def score_parts(unit):
            b, i = unit
            return [(dot(keys, q_ref[columns(i, tile), columns(b, width)], NT), True)]

        units = [(b, i) for i in range(tiles) for b in range(heads)]
        features = [feature_task(pair, i) for i in range(tiles) for pair in range(pairs)]
        attend(
            scale,
            units,
            score_parts,
            turned_ref,
            mix_ref,
            level_ref,
            tile,
            width,
            features,
            CHUNK_WINDOW,
        )


def student(total_tokens, chunk_count, place_ref, q_ref, k_ref, v_ref, *refs):
    refs = list(refs)
    chunk_keys = [refs.pop(0) for _ in range(chunk_count)]
    chunk_values = [refs.pop(0) for _ in range(chunk_count)]
    mix_refs = [refs.pop(0) for _ in range(chunk_count + 1)]
    level_refs = [refs.pop(0) for _ in range(chunk_count + 1)]
    slope_refs = [refs.pop(0) for _ in range(chunk_count)]
    wq_ref, wk_ref, state_ref, out_ref, wide_t, keys_t, chunk_t, wk_acc = refs
    rows, width = k_ref.shape
    heads = q_ref.shape[1] // width
    pairs = heads // 2
    tile = tile_of(rows)
    tiles = rows // tile
    mask = causal_mask(tile)

    @pl.when(pl.program_id(0) == 0)
    def _():
        wide_t[...] = turned_with_ones(v_ref[...])
        keys_t[...] = turned(k_ref[...])
        for c in range(chunk_count):

            @pl.when(place_ref[0] >= c + 1)
            def _(c=c):
                chunk_t[c] = turned(chunk_keys[c][...])

    head_list = range(heads)
    tile_list = range(tiles)
    wide = [with_ones(v_ref[columns(i, tile), :]) for i in tile_list]
    key_feat, key_slope, states, shares = {}, {}, {}, {}

    def key_task(pair):
        weight = jnp.concatenate((wk_ref[2 * pair], wk_ref[2 * pair + 1]), axis=1)
        running = state_ref[pair]
        pre = dot(k_ref[columns(0, tile), :], weight, NN)
        for i in tile_list:
            yield
            later = dot(k_ref[columns(i + 1, tile), :], weight, NN) if i + 1 < tiles else None
            feat, slope = softplus_and_slope(pre)
            pre = later
            key_slope[pair, i] = slope
            for side in range(2):
                here = columns(side, width)
                key_feat[2 * pair + side, i] = feat[:, here]
                norm = jnp.broadcast_to(running[width : width + 1, here], (width, width))
                states[2 * pair + side, i] = jnp.concatenate(
                    (running[:width, here], norm), axis=0
                ).astype(BF16)
            if i + 1 < tiles:
                running = running + dot(wide_t[:, columns(i, tile)], feat, NN)

    def share_task(i):
        levels = [ref[0, :, columns(i, tile)] for ref in level_refs]
        peak = functools.reduce(jnp.maximum, levels)
        parts = [jnp.exp2(level - peak) for level in levels]
        inverse = 1.0 / functools.reduce(jnp.add, parts)
        shares[i] = [part * inverse for part in parts]
        yield

    interleave([key_task(pair) for pair in range(pairs)] + [share_task(i) for i in tile_list], 4)

    backs, query_change, key_change = {}, {}, {}

    def unit_task(b, i):
        here, head = columns(i, tile), columns(b, width)
        pre = dot(q_ref[here, head], wq_ref[b], NN)
        yield
        feat, slope = softplus_and_slope(pre)
        affinity = dot(feat, key_feat[b, i], NT)
        mixed = dot(feat, states[b, i], NT)
        yield
        affinity = jnp.where(mask, affinity, 0.0).astype(BF16)
        mixed = mixed + dot(affinity, wide[i], NN)
        teacher = functools.reduce(
            jnp.add,
            [
                share[b : b + 1] * ref[head, here].astype(F32)
                for share, ref in zip(shares[i], mix_refs)
            ],
        )
        teacher = turned(teacher).astype(F32)
        yield
        inverse = 1.0 / mixed[:, width:]
        result = mixed[:, :width] * inverse
        grad_out = (result - teacher) * (2.0 / total_tokens)
        grad_denom = jnp.sum(grad_out * result, axis=1, keepdims=True) * inverse * (-1.0 / width)
        grads = jnp.concatenate((grad_out * inverse, grad_denom), axis=1).astype(BF16)
        grad_aff = dot(grads, wide[i], NT)
        backs[b, i] = dot(feat, grads, TN)
        grad_qfeat = dot(grads, states[b, i], NN)
        yield
        grad_aff = jnp.where(mask, grad_aff, 0.0).astype(BF16)
        grad_qfeat = grad_qfeat + dot(grad_aff, key_feat[b, i], NN)
        key_change[b, i] = dot(grad_aff, feat, TN)
        yield
        query_change[b, i] = (grad_qfeat * slope).astype(BF16)

    interleave([unit_task(b, i) for b in head_list for i in tile_list], UNIT_WINDOW)

    whole = [None] * pairs

    def query_weight_task(b):
        change = jnp.concatenate([query_change[b, i] for i in tile_list], axis=0)
        out_ref[b, 0] = dot(q_ref[:, columns(b, width)], change, TN).astype(out_ref.dtype)
        yield

    def key_weight_task(pair):
        sides = (2 * pair, 2 * pair + 1)
        running = [backs[b, tiles - 1] for b in sides]
        changes = [None] * tiles
        for i in reversed(tile_list):
            both = jnp.concatenate([key_change[b, i] for b in sides], axis=1)
            if i + 1 < tiles:
                later = jnp.concatenate(running, axis=0).astype(BF16)
                both = both + dot(wide[i], later, NT)
                running = [old + backs[b, i] for old, b in zip(running, sides)]
                yield
            changes[i] = (both * key_slope[pair, i]).astype(BF16)
        whole[pair] = jnp.concatenate(running, axis=0).astype(BF16)
        wk_acc[pair] = dot(keys_t[...], jnp.concatenate(changes, axis=0), NN)

    tasks = []
    for pair in range(pairs):
        tasks += [query_weight_task(2 * pair), query_weight_task(2 * pair + 1)]
        tasks.append(key_weight_task(pair))
    interleave(tasks, 3)

    for c in range(chunk_count):

        @pl.when(place_ref[0] >= c + 1)
        def _(c=c):
            values = with_ones(chunk_values[c][...])
            sums = [None] * pairs

            def chunk_task(pair, i):
                here = columns(i, tile)
                slope = slope_refs[c][here, columns(pair, 2 * width)]
                change = dot(values[here], whole[pair], NT)
                yield
                change = (change * slope.astype(F32)).astype(BF16)
                term = dot(chunk_t[c, :, here], change, NN)
                sums[pair] = term if i == 0 else sums[pair] + term
                if i == tiles - 1:
                    wk_acc[pair] += sums[pair]

            interleave([chunk_task(pair, i) for pair in range(pairs) for i in tile_list], 2)

    for b in head_list:
        out_ref[b, 1] = wk_acc[b // 2][:, columns(b % 2, width)].astype(out_ref.dtype)


def params():
    return pltpu.CompilerParams(
        vmem_limit_bytes=VMEM_BYTES, dimension_semantics=("arbitrary",)
    )


def cost(microseconds):
    return pl.CostEstimate(
        flops=int(microseconds * 1e9), bytes_accessed=int(microseconds * 3e6), transcendentals=0
    )


class Plan:
    def __init__(self, rows, half, groups, width, feats):
        self.rows, self.half, self.groups, self.width, self.feats = rows, half, groups, width, feats
        self.per_group = half // groups
        self.heads = math.gcd(self.per_group, BLOCK_HEADS)
        self.steps = half // self.heads
        self.mix_type = jax.ShapeDtypeStruct((half * width, rows), BF16)
        self.q_type = jax.ShapeDtypeStruct((rows, half * width), BF16)
        self.level_type = jax.ShapeDtypeStruct((self.steps, SUBLANES, rows), F32)
        self.state_type = jax.ShapeDtypeStruct((half // 2, width + 16, 2 * feats), F32)

    def specs(self, start=0):
        rows, width, heads, steps = self.rows, self.width, self.heads, self.steps
        groups, per_group = self.groups, self.per_group
        return dict(
            q=pl.BlockSpec((rows, heads * width), lambda h, *_: (0, start + h)),
            k=pl.BlockSpec((rows, width), lambda h, *_: (0, (start + h) * heads // per_group)),
            v=pl.BlockSpec(
                (rows, width), lambda h, *_: (0, groups + (start + h) * heads // per_group)
            ),
            mix=pl.BlockSpec((heads * width, rows), lambda h, *_: (start + h, 0)),
            level=pl.BlockSpec((1, SUBLANES, rows), lambda h, *_: (start + h, 0, 0)),
            w=pl.BlockSpec(
                (heads, width, self.feats),
                lambda h, place: (place[1] * steps + start + h, 0, 0),
            ),
            state=pl.BlockSpec(
                (heads // 2, width + 16, 2 * self.feats), lambda h, *_: (start + h, 0, 0)
            ),
        )

    def local(self, place, queries, other_q, kv):
        at, steps = self.specs(), self.steps
        part, block = queries.shape[0], self.heads * self.width
        return pl.pallas_call(
            functools.partial(local_attention, self.width ** (-0.5) * LOG2E),
            grid_spec=pltpu.PrefetchScalarGridSpec(
                num_scalar_prefetch=1,
                grid=(steps,),
                in_specs=[
                    pl.BlockSpec((part, block), lambda h, place: (0, place[1] * steps + h)),
                    pl.BlockSpec((part, block), lambda h, *_: (0, h)),
                    at["k"],
                    at["v"],
                ],
                out_specs=[at["q"], at["mix"], at["level"]],
                scratch_shapes=[pltpu.VMEM((self.width + 16, self.rows), BF16)],
            ),
            out_shape=[self.q_type, self.mix_type, self.level_type],
            compiler_params=params(),
            cost_estimate=cost(12),
            name="local_attention",
        )(place, queries, other_q, kv, kv)

    def chunk(self, distance, place, q, chunk, feat_k, state):
        at = self.specs()
        return pl.pallas_call(
            functools.partial(chunk_attention, self.width ** (-0.5) * LOG2E, distance),
            grid_spec=pltpu.PrefetchScalarGridSpec(
                num_scalar_prefetch=1,
                grid=(self.steps,),
                in_specs=[at["q"], at["k"], at["v"], at["w"], at["state"]],
                out_specs=[at["mix"], at["level"], at["q"], at["state"]],
                scratch_shapes=[pltpu.VMEM((self.width + 16, self.rows), BF16)],
            ),
            out_shape=[self.mix_type, self.level_type, self.q_type, self.state_type],
            compiler_params=params(),
            cost_estimate=cost(18),
            name="chunk_attention",
        )(place, q, chunk, chunk, feat_k, state)

    def student(
        self, start, steps, chips, place, q, kv, chunks, mixes, levels, slopes, wq, wk, state
    ):
        at = self.specs(start)
        count, width, rows = len(chunks), self.width, self.rows
        grad_shape = (self.heads, 2, width, self.feats)
        return pl.pallas_call(
            functools.partial(student, chips * rows, count),
            grid_spec=pltpu.PrefetchScalarGridSpec(
                num_scalar_prefetch=1,
                grid=(steps,),
                in_specs=[at["q"], at["k"], at["v"]]
                + [at["k"]] * count
                + [at["v"]] * count
                + [at["mix"]] * len(mixes)
                + [at["level"]] * len(levels)
                + [at["q"]] * count
                + [at["w"], at["w"], at["state"]],
                out_specs=pl.BlockSpec(grad_shape, lambda h, *_: (h, 0, 0, 0)),
                scratch_shapes=[
                    pltpu.VMEM((width + 16, rows), BF16),
                    pltpu.VMEM((width, rows), BF16),
                    pltpu.VMEM((max(1, count), width, rows), BF16),
                    pltpu.VMEM((self.heads // 2, width, 2 * self.feats), F32),
                ],
            ),
            out_shape=jax.ShapeDtypeStruct((steps * self.heads,) + grad_shape[1:], BF16),
            compiler_params=params(),
            cost_estimate=cost(12 * steps),
            name="student",
        )(place, q, kv, kv, *chunks, *chunks, *mixes, *levels, *slopes, wq, wk, state)


def body(queries, keys, values, feat_q, feat_k):
    row_count = queries.shape[0]
    heads_here, width, feat_count = feat_q.shape
    seq_count = lax.axis_size("seq")
    chips = seq_count // CORES
    seq_place = lax.axis_index("seq")
    core, chip = seq_place % CORES, seq_place // CORES
    head_place = lax.axis_index("head")
    spread = max(1, HEADS // KV_HEADS // heads_here)
    key_value = jnp.stack((keys, values))
    for bit_index in range(spread.bit_length() - 1):
        partner = from_partner(key_value, "head", bit_index)
        upper_half = head_place // (1 << bit_index) % 2 == 1
        key_value = jnp.where(
            upper_half,
            jnp.concatenate((partner, key_value), axis=2),
            jnp.concatenate((key_value, partner), axis=2),
        )
    groups = key_value.shape[2] // width
    half = heads_here // CORES
    core_route = [(i, i ^ 1) for i in range(seq_count)]
    first = core == 0

    if groups > 1:
        own_groups = groups // CORES
        split = own_groups * width
        low, high = key_value[:, :, :split], key_value[:, :, split:]
        kept, sent = jnp.where(first, low, high), jnp.where(first, high, low)
    else:
        own_groups = groups
        kept = sent = key_value
    got = lax.ppermute(sent, "seq", core_route)
    kv = jnp.where(
        first, jnp.concatenate((kept, got), axis=1), jnp.concatenate((got, kept), axis=1)
    )
    kv = jnp.concatenate((kv[0], kv[1]), axis=1)
    other_q = lax.ppermute(
        lax.dynamic_slice_in_dim(queries, (1 - core) * half * width, half * width, 1),
        "seq",
        core_route,
    )
    rows = CORES * row_count
    chunks = []
    for distance in range(1, chips):
        route = [(i, i + CORES * distance) for i in range(seq_count - CORES * distance)]
        chunks.append(lax.ppermute(kv, "seq", route))

    plan = Plan(rows, half, own_groups, width, feat_count)
    place = jnp.stack((chip, core)).astype(jnp.int32)
    q, mix, level = plan.local(place, queries, other_q, kv)
    state = jnp.zeros(plan.state_type.shape, F32)
    mixes, levels, slopes = [mix], [level], []
    for index, chunk in enumerate(chunks):
        mix, level, slope, state = plan.chunk(index + 1, place, q, chunk, feat_k, state)
        mixes.append(mix)
        levels.append(level)
        slopes.append(slope)
    total_parts = sum(STUDENT_PARTS)
    parts = STUDENT_PARTS if plan.steps % total_parts == 0 else (1,)
    unit = plan.steps // sum(parts)
    network = Reduction(chip, chips, seq_count)
    wholes, start, total, sent, count = [], 0, None, None, 0
    for index, part in enumerate(parts):
        steps = part * unit
        grads = plan.student(
            start, steps, chips, place, q, kv, chunks, mixes, levels, slopes, feat_q, feat_k, state
        )
        start += steps
        grads, sent = lax.optimization_barrier((grads, sent))
        if sent is not None:
            total = network.received(sent, count, wholes)
        if index + 1 < len(parts):
            place, grads, total = lax.optimization_barrier((place, grads, total))
        sent, count = network.send(grads, total), 0 if total is None else total.shape[0]
    total = network.received(sent, count, wholes)
    network.received(network.send(None, total), total.shape[0], wholes)
    results = []
    for whole in wholes:
        whole = whole.reshape((-1,) + grads.shape[1:])
        results.append((whole, lax.ppermute(whole, "seq", core_route)))
    own = jnp.concatenate([pair[0] for pair in results], axis=0)
    other = jnp.concatenate([pair[1] for pair in results], axis=0)
    both = jnp.where(
        first, jnp.concatenate((own, other), axis=0), jnp.concatenate((other, own), axis=0)
    ).astype(F32)
    return both[:, 0], both[:, 1]


class Reduction:
    def __init__(self, chip, chips, seq_count):
        self.chip, self.chips, self.seq_count = chip, chips, seq_count

    def route(self, distance):
        count = self.seq_count
        return [(i, (i + CORES * distance) % count) for i in range(count)]

    def send(self, grads, total):
        sent = []
        for distance in range(self.chips):
            part = None
            if grads is not None:
                flat = grads.reshape(-1, grads.shape[-1])
                share = flat.shape[0] // self.chips
                place = (self.chip + distance) % self.chips
                part = lax.dynamic_slice_in_dim(flat, place * share, share, 0)
            block = jnp.concatenate([x for x in (total, part) if x is not None], axis=0)
            if distance:
                block = lax.ppermute(block, "seq", self.route(distance))
            sent.append(block)
        return sent

    def received(self, sent, count, wholes):
        if count:
            parts = [block[:count] for block in sent]
            order = jnp.concatenate(parts[::-1] + parts[:0:-1], axis=0)
            first = (self.chips - 1 - self.chip) * count
            wholes.append(lax.dynamic_slice_in_dim(order, first, self.chips * count, 0))
        if sent[0].shape[0] == count:
            return None
        return functools.reduce(
            jnp.add, [block[count:].astype(F32) for block in sent]
        ).astype(BF16)


def solution(mesh):
    return jax.shard_map(
        body,
        mesh=mesh,
        in_specs=(
            P("seq", "head"),
            P("seq", "head"),
            P("seq", "head"),
            P("head", None, None),
            P("head", None, None),
        ),
        out_specs=(P("head", None, None), P("head", None, None)),
        check_vma=False,
    )
```

```python
import functools
import math

import jax
import jax.numpy as jnp
from jax import lax
from jax.experimental import pallas as pl
from jax.experimental.pallas import tpu as pltpu
from jax.sharding import PartitionSpec as P

HEADS = 128
KV_HEADS = 8
CORES = 2
SUBLANES = 8
BLOCK_HEADS = 4
STUDENT_PARTS = (2, 1, 1)
LOCAL_WINDOW = 2
CHUNK_WINDOW = 2
UNIT_WINDOW = 8
LOG2E = math.log2(math.e)
MASKED_SCORE = -1e30
TINY_DECAY = 2.0**-11
SAFE_LOW = 2.0**-100
SAFE_HIGH = 2.0**120
VMEM_BYTES = 56 * 1024 * 1024
F32 = jnp.float32
BF16 = jnp.bfloat16

NN = (((1,), (0,)), ((), ()))
NT = (((1,), (1,)), ((), ()))
TN = (((0,), (0,)), ((), ()))


def dot(a, b, form):
    return lax.dot_general(a, b, form, preferred_element_type=F32)


def from_partner(block, axis, stride):
    count = lax.axis_size(axis)
    route = []
    for low in range(count):
        high = low | 1 << stride
        if high != low and high < count:
            route += [(low, high), (high, low)]
    return lax.ppermute(block, axis, route)


def tile_of(rows):
    return 256 if rows % 256 == 0 else rows


def with_ones(values):
    return jnp.concatenate((values, jnp.ones_like(values)), axis=1)


def turned(block):
    return block.astype(F32).T.astype(BF16)


def turned_with_ones(values):
    return jnp.concatenate((turned(values), jnp.ones((16, values.shape[0]), BF16)), axis=0)


def softplus_and_slope(pre):
    above, below = jnp.maximum(pre, 0.0), jnp.minimum(pre, 0.0)
    decay = jnp.exp(below - above)
    log_term = jnp.where(decay < TINY_DECAY, decay, jnp.log(1.0 + decay))
    return (above + log_term).astype(BF16), jnp.exp(below - log_term).astype(BF16)


def masked(mask, block, other):
    return block if mask is True else jnp.where(mask, block, other)


def columns(index, width):
    return slice(index * width, (index + 1) * width)


def causal_mask(rows):
    return lax.broadcasted_iota(jnp.int32, (rows, rows), 0) >= lax.broadcasted_iota(
        jnp.int32, (rows, rows), 1
    )


def interleave(tasks, window):
    waiting, active = list(tasks), []
    while waiting or active:
        if waiting and len(active) < window:
            active.append(waiting.pop(0))
        for task in active[::-1]:
            if next(task, active) is active:
                active.remove(task)


def mixture_task(scale, shifted, score_parts, values_t, unit, store):
    parts = score_parts(unit)
    yield
    peak = 0.0
    if shifted:
        peak = scale * functools.reduce(
            jnp.maximum,
            [jnp.max(masked(mask, part, MASKED_SCORE), axis=0, keepdims=True) for part, mask in parts],
        )
    weights = [
        masked(
            mask, jnp.exp2(part * scale - peak if shifted else part * scale), 0.0
        ).astype(BF16)
        for part, mask in parts
    ]
    weights = weights[0] if len(weights) == 1 else jnp.concatenate(weights, axis=0)
    mixed = dot(values_t[:, : weights.shape[0]], weights, NN)
    width = mixed.shape[0] - 16
    total = mixed[width : width + 1]
    store(unit, (mixed[:width] * (1.0 / total)).astype(BF16), total, peak + jnp.log2(total))


def attend(scale, units, score_parts, values_t, mix_ref, level_ref, tile, width, others, window):
    totals = []

    def store(unit, mixture, total, level):
        b, i = unit
        mix_ref[columns(b, width), columns(i, tile)] = mixture
        level_ref[0, b : b + 1, columns(i, tile)] = level
        totals.append(total)

    def tasks(shifted):
        return [
            mixture_task(scale, shifted, score_parts, values_t, unit, store) for unit in units
        ]

    first, spread = tasks(False), []
    for place, task in enumerate(first):
        spread += others[place * len(others) // len(first) : (place + 1) * len(others) // len(first)]
        spread.append(task)
    interleave(spread, window)
    low = jnp.min(functools.reduce(jnp.minimum, totals))
    high = jnp.max(functools.reduce(jnp.maximum, totals))

    @pl.when(jnp.logical_not((low > SAFE_LOW) & (high < SAFE_HIGH)))
    def _():
        interleave(tasks(True), window)


def local_attention(
    scale, group_steps, place_ref, own_ref, other_ref, k_ref, v_ref, q_ref, mix_ref, level_ref, turned_ref, keys_t
):
    rows, width = k_ref.shape
    heads = q_ref.shape[1] // width
    part = own_ref.shape[0]
    core = place_ref[1]
    q_ref[pl.ds(pl.multiple_of(core * part, part), part), :] = own_ref[...]
    q_ref[pl.ds(pl.multiple_of((1 - core) * part, part), part), :] = other_ref[...]
    @pl.when(pl.program_id(0) % group_steps == 0)
    def _():
        turned_ref[...] = turned_with_ones(v_ref[...])
        keys_t[...] = turned(k_ref[...])

    tile = tile_of(rows)
    mask = lax.broadcasted_iota(jnp.int32, (tile, tile), 0) <= lax.broadcasted_iota(
        jnp.int32, (tile, tile), 1
    )

    def score_parts(unit):
        b, i = unit
        query = q_ref[columns(i, tile), columns(b, width)]
        last = (dot(k_ref[columns(i, tile), :], query, NT), mask)
        return [last] if i == 0 else [(dot(k_ref[: i * tile, :], query, NT), True), last]

    units = [(b, i) for i in range(rows // tile) for b in range(heads)]
    attend(
        scale, units, score_parts, turned_ref, mix_ref, level_ref, tile, width, [], LOCAL_WINDOW
    )


def chunk_block(
    scale, group_steps, q_ref, k_ref, v_ref, wk_ref, state_of, outs
):
    mix_ref, level_ref, slope_ref, state_ref, keys_t, turned_ref = outs
    rows, width = k_ref.shape
    heads = q_ref.shape[1] // width
    pairs = heads // 2

    @pl.when(pl.program_id(0) % group_steps == 0)
    def _():
        turned_ref[...] = turned_with_ones(v_ref[...])
        keys_t[...] = turned(k_ref[...])

    tile = tile_of(rows)
    tiles = rows // tile
    keys = k_ref[...]

    def feature_task(pair):
        weight = jnp.concatenate((wk_ref[2 * pair], wk_ref[2 * pair + 1]), axis=1)
        pre = dot(keys, weight, NN)
        yield
        feat, slope = softplus_and_slope(pre)
        slope_ref[:, columns(pair, 2 * width)] = slope
        state_ref[pair] = state_of(pair) + dot(turned_ref[...], feat, NN)

    def score_parts(unit):
        b, i = unit
        return [(dot(keys, q_ref[columns(i, tile), columns(b, width)], NT), True)]

    units = [(b, i) for i in range(tiles) for b in range(heads)]
    features = [feature_task(pair) for pair in range(pairs)]
    attend(
        scale,
        units,
        score_parts,
        turned_ref,
        mix_ref,
        level_ref,
        tile,
        width,
        features,
        CHUNK_WINDOW,
    )


def chunk_attention(scale, group_steps, place_ref, q_ref, k_ref, v_ref, wk_ref, *outs):
    mix_ref, level_ref, slope_ref, state_ref, keys_t, _ = outs

    @pl.when(place_ref[0] < 1)
    def _():
        mix_ref[...] = jnp.zeros_like(mix_ref)
        slope_ref[...] = jnp.zeros_like(slope_ref)
        level_ref[...] = jnp.full_like(level_ref, MASKED_SCORE)
        state_ref[...] = jnp.zeros_like(state_ref)
        keys_t[...] = jnp.zeros_like(keys_t)

    @pl.when(place_ref[0] >= 1)
    def _():
        chunk_block(scale, group_steps, q_ref, k_ref, v_ref, wk_ref, lambda pair: 0.0, outs)


def student(scale, group_steps, total_tokens, chunk_count, place_ref, q_ref, k_ref, v_ref, *refs):
    refs = list(refs)
    done = min(chunk_count, 1)
    chunk_keys = [refs.pop(0) for _ in range(chunk_count - done)]
    chunk_values = [refs.pop(0) for _ in range(chunk_count)]
    mix_refs = [refs.pop(0) for _ in range(done + 1)]
    level_refs = [refs.pop(0) for _ in range(done + 1)]
    slope_refs = [refs.pop(0) for _ in range(done)]
    chunk_keys_t = [refs.pop(0) for _ in range(done)]
    wide_t, keys_t, wq_ref, wk_ref, state_in, out_ref, wk_acc, state_ref = refs[:8]
    refs = refs[8:]
    state_ref[...] = state_in[...]
    for c in range(done, chunk_count):
        own = [refs.pop(0) for _ in range(5)]
        mix, level, slope, turned_keys, turned_values = own
        mix_refs.append(mix)
        level_refs.append(level)
        slope_refs.append(slope)
        chunk_keys_t.append(turned_keys)

        @pl.when(place_ref[0] < c + 1)
        def _(mix=mix, level=level):
            mix[...] = jnp.zeros_like(mix)
            level[...] = jnp.full_like(level, MASKED_SCORE)

        @pl.when(place_ref[0] >= c + 1)
        def _(c=c, own=own):
            chunk_block(
                scale,
                group_steps,
                q_ref,
                chunk_keys[c - done],
                chunk_values[c],
                wk_ref,
                lambda pair: state_ref[pair],
                (*own[:3], state_ref, *own[3:]),
            )

    rows, width = k_ref.shape
    heads = q_ref.shape[1] // width
    pairs = heads // 2
    tile = tile_of(rows)
    tiles = rows // tile
    mask = causal_mask(tile).astype(F32).astype(BF16)

    head_list = range(heads)
    tile_list = range(tiles)
    wide = [with_ones(v_ref[columns(i, tile), :]) for i in tile_list]
    key_feat, key_slope, states, shares = {}, {}, {}, {}

    def key_task(pair):
        weight = jnp.concatenate((wk_ref[2 * pair], wk_ref[2 * pair + 1]), axis=1)
        running = state_ref[pair]
        pre = dot(k_ref[columns(0, tile), :], weight, NN)
        for i in tile_list:
            yield
            later = dot(k_ref[columns(i + 1, tile), :], weight, NN) if i + 1 < tiles else None
            feat, slope = softplus_and_slope(pre)
            pre = later
            key_slope[pair, i] = slope
            for side in range(2):
                here = columns(side, width)
                key_feat[2 * pair + side, i] = feat[:, here]
                norm = jnp.broadcast_to(running[width : width + 1, here], (width, width))
                states[2 * pair + side, i] = jnp.concatenate(
                    (running[:width, here], norm), axis=0
                ).astype(BF16)
            if i + 1 < tiles:
                running = running + dot(wide_t[:, columns(i, tile)], feat, NN)

    def share_task(i):
        levels = [ref[0, :, columns(i, tile)] for ref in level_refs]
        peak = functools.reduce(jnp.maximum, levels)
        parts = [jnp.exp2(level - peak) for level in levels]
        inverse = 1.0 / functools.reduce(jnp.add, parts)
        shares[i] = [part * inverse for part in parts]
        yield

    interleave([key_task(pair) for pair in range(pairs)] + [share_task(i) for i in tile_list], 4)

    backs, query_change, key_change = {}, {}, {}

    def unit_task(b, i):
        here, head = columns(i, tile), columns(b, width)
        pre = dot(q_ref[here, head], wq_ref[b], NN)
        yield
        feat, slope = softplus_and_slope(pre)
        affinity = dot(feat, key_feat[b, i], NT)
        mixed = dot(feat, states[b, i], NT)
        yield
        affinity = affinity.astype(BF16) * mask
        mixed = mixed + dot(affinity, wide[i], NN)
        teacher = functools.reduce(
            jnp.add,
            [
                share[b : b + 1] * ref[head, here].astype(F32)
                for share, ref in zip(shares[i], mix_refs)
            ],
        )
        teacher = turned(teacher).astype(F32)
        yield
        inverse = 1.0 / mixed[:, width:]
        result = mixed[:, :width] * inverse
        grad_out = (result - teacher) * (2.0 / total_tokens)
        grad_denom = jnp.sum(grad_out * result, axis=1, keepdims=True) * inverse * (-1.0 / width)
        grads = jnp.concatenate((grad_out * inverse, grad_denom), axis=1).astype(BF16)
        grad_aff = dot(grads, wide[i], NT)
        backs[b, i] = dot(feat, grads, TN)
        yield
        grad_aff = grad_aff.astype(BF16) * mask
        grad_qfeat = dot(
            jnp.concatenate((grads, grad_aff), axis=1),
            jnp.concatenate((states[b, i], key_feat[b, i]), axis=0),
            NN,
        )
        key_change[b, i] = dot(grad_aff, feat, TN)
        yield
        query_change[b, i] = grad_qfeat.astype(BF16) * slope

    interleave([unit_task(b, i) for b in head_list for i in tile_list], UNIT_WINDOW)

    whole = [None] * pairs

    def query_weight_task(b):
        change = jnp.concatenate([query_change[b, i] for i in tile_list], axis=0)
        out_ref[b, 0] = dot(q_ref[:, columns(b, width)], change, TN).astype(out_ref.dtype)
        yield

    def key_weight_task(pair):
        sides = (2 * pair, 2 * pair + 1)
        running = [backs[b, tiles - 1] for b in sides]
        changes = [None] * tiles
        for i in reversed(tile_list):
            both = jnp.concatenate([key_change[b, i] for b in sides], axis=1)
            if i + 1 < tiles:
                later = jnp.concatenate(running, axis=0).astype(BF16)
                both = both + dot(wide[i], later, NT)
                running = [old + backs[b, i] for old, b in zip(running, sides)]
                yield
            changes[i] = both.astype(BF16) * key_slope[pair, i]
        whole[pair] = jnp.concatenate(running, axis=0).astype(BF16)
        wk_acc[pair] = dot(keys_t[...], jnp.concatenate(changes, axis=0), NN)

    tasks = []
    for pair in range(pairs):
        tasks += [query_weight_task(2 * pair), query_weight_task(2 * pair + 1)]
        tasks.append(key_weight_task(pair))
    interleave(tasks, 3)

    for c in range(chunk_count):

        @pl.when(place_ref[0] >= c + 1)
        def _(c=c):
            values = with_ones(chunk_values[c][...])
            sums = [None] * pairs

            def chunk_task(pair, i):
                here = columns(i, tile)
                slope = slope_refs[c][here, columns(pair, 2 * width)]
                change = dot(values[here], whole[pair], NT)
                yield
                change = change.astype(BF16) * slope
                term = dot(chunk_keys_t[c][:, here], change, NN)
                sums[pair] = term if i == 0 else sums[pair] + term
                if i == tiles - 1:
                    wk_acc[pair] += sums[pair]

            interleave([chunk_task(pair, i) for pair in range(pairs) for i in tile_list], 2)

    for b in head_list:
        out_ref[b, 1] = wk_acc[b // 2][:, columns(b % 2, width)].astype(out_ref.dtype)


def params():
    return pltpu.CompilerParams(
        vmem_limit_bytes=VMEM_BYTES, dimension_semantics=("arbitrary",)
    )


def cost(microseconds):
    return pl.CostEstimate(
        flops=int(microseconds * 1e9), bytes_accessed=int(microseconds * 3e6), transcendentals=0
    )


class Plan:
    def __init__(self, rows, half, groups, width, feats):
        self.rows, self.half, self.groups, self.width, self.feats = rows, half, groups, width, feats
        self.per_group = half // groups
        self.heads = math.gcd(self.per_group, BLOCK_HEADS)
        self.steps = half // self.heads
        self.mix_type = jax.ShapeDtypeStruct((half * width, rows), BF16)
        self.q_type = jax.ShapeDtypeStruct((rows, half * width), BF16)
        self.level_type = jax.ShapeDtypeStruct((self.steps, SUBLANES, rows), F32)
        self.state_type = jax.ShapeDtypeStruct((half // 2, width + 16, 2 * feats), F32)

    def turned_type(self, height):
        return jax.ShapeDtypeStruct((height * self.groups, self.rows), BF16)

    def specs(self, start=0):
        rows, width, heads, steps = self.rows, self.width, self.heads, self.steps
        groups, per_group = self.groups, self.per_group
        return dict(
            q=pl.BlockSpec((rows, heads * width), lambda h, *_: (0, start + h)),
            k=pl.BlockSpec((rows, width), lambda h, *_: (0, (start + h) * heads // per_group)),
            v=pl.BlockSpec(
                (rows, width), lambda h, *_: (0, groups + (start + h) * heads // per_group)
            ),
            mix=pl.BlockSpec((heads * width, rows), lambda h, *_: (start + h, 0)),
            wide_t=pl.BlockSpec((width + 16, rows), lambda h, *_: ((start + h) * heads // per_group, 0)),
            keys_t=pl.BlockSpec((width, rows), lambda h, *_: ((start + h) * heads // per_group, 0)),
            level=pl.BlockSpec((1, SUBLANES, rows), lambda h, *_: (start + h, 0, 0)),
            w=pl.BlockSpec(
                (heads, width, self.feats),
                lambda h, place: (place[1] * steps + start + h, 0, 0),
            ),
            state=pl.BlockSpec(
                (heads // 2, width + 16, 2 * self.feats), lambda h, *_: (start + h, 0, 0)
            ),
        )

    def local(self, place, queries, other_q, kv):
        at, steps = self.specs(), self.steps
        part, block = queries.shape[0], self.heads * self.width
        return pl.pallas_call(
            functools.partial(
                local_attention, self.width ** (-0.5) * LOG2E, self.per_group // self.heads
            ),
            grid_spec=pltpu.PrefetchScalarGridSpec(
                num_scalar_prefetch=1,
                grid=(steps,),
                in_specs=[
                    pl.BlockSpec((part, block), lambda h, place: (0, place[1] * steps + h)),
                    pl.BlockSpec((part, block), lambda h, *_: (0, h)),
                    at["k"],
                    at["v"],
                ],
                out_specs=[at["q"], at["mix"], at["level"], at["wide_t"], at["keys_t"]],
            ),
            out_shape=[
                self.q_type,
                self.mix_type,
                self.level_type,
                self.turned_type(self.width + 16),
                self.turned_type(self.width),
            ],
            compiler_params=params(),
            cost_estimate=cost(12),
            name="local_attention",
        )(place, queries, other_q, kv, kv)

    def chunk(self, place, q, chunk, feat_k):
        at = self.specs()
        return pl.pallas_call(
            functools.partial(
                chunk_attention,
                self.width ** (-0.5) * LOG2E,
                self.per_group // self.heads,
            ),
            grid_spec=pltpu.PrefetchScalarGridSpec(
                num_scalar_prefetch=1,
                grid=(self.steps,),
                in_specs=[at["q"], at["k"], at["v"], at["w"]],
                out_specs=[at["mix"], at["level"], at["q"], at["state"], at["keys_t"]],
                scratch_shapes=[pltpu.VMEM((self.width + 16, self.rows), BF16)],
            ),
            out_shape=[
                self.mix_type,
                self.level_type,
                self.q_type,
                self.state_type,
                self.turned_type(self.width),
            ],
            compiler_params=params(),
            cost_estimate=cost(18),
            name="chunk_attention",
        )(place, q, chunk, chunk, feat_k)

    def student(
        self,
        start,
        steps,
        chips,
        place,
        q,
        kv,
        chunk_keys,
        chunks,
        mixes,
        levels,
        slopes,
        wide_t,
        keys_t,
        wq,
        wk,
        state,
    ):
        at = self.specs(start)
        count, width, rows = len(chunks), self.width, self.rows
        grad_shape = (self.heads, 2, width, self.feats)
        done = len(slopes)
        return pl.pallas_call(
            functools.partial(
                student,
                width ** (-0.5) * LOG2E,
                self.per_group // self.heads,
                chips * rows,
                count,
            ),
            grid_spec=pltpu.PrefetchScalarGridSpec(
                num_scalar_prefetch=1,
                grid=(steps,),
                in_specs=[at["q"], at["k"], at["v"]]
                + [at["k"]] * (count - done)
                + [at["v"]] * count
                + [at["mix"]] * len(mixes)
                + [at["level"]] * len(levels)
                + [at["q"]] * done
                + [at["keys_t"]] * done
                + [at["wide_t"], at["keys_t"], at["w"], at["w"], at["state"]],
                out_specs=pl.BlockSpec(grad_shape, lambda h, *_: (h, 0, 0, 0)),
                scratch_shapes=[
                    pltpu.VMEM((self.heads // 2, width, 2 * self.feats), F32),
                    pltpu.VMEM((self.heads // 2, width + 16, 2 * self.feats), F32),
                ]
                + [
                    pltpu.VMEM((self.heads * width, rows), BF16),
                    pltpu.VMEM((1, SUBLANES, rows), F32),
                    pltpu.VMEM((rows, self.heads * width), BF16),
                    pltpu.VMEM((width, rows), BF16),
                    pltpu.VMEM((width + 16, rows), BF16),
                ]
                * (count - done),
            ),
            out_shape=jax.ShapeDtypeStruct((steps * self.heads,) + grad_shape[1:], BF16),
            compiler_params=params(),
            cost_estimate=cost(20 * steps),
            name="student",
        )(
            place, q, kv, kv, *chunks[done:], *chunks, *mixes, *levels, *slopes, *chunk_keys, wide_t, keys_t, wq, wk, state
        )


def body(queries, keys, values, feat_q, feat_k):
    row_count = queries.shape[0]
    heads_here, width, feat_count = feat_q.shape
    seq_count = lax.axis_size("seq")
    chips = seq_count // CORES
    seq_place = lax.axis_index("seq")
    core, chip = seq_place % CORES, seq_place // CORES
    head_place = lax.axis_index("head")
    spread = max(1, HEADS // KV_HEADS // heads_here)
    key_value = jnp.stack((keys, values))
    for bit_index in range(spread.bit_length() - 1):
        partner = from_partner(key_value, "head", bit_index)
        upper_half = head_place // (1 << bit_index) % 2 == 1
        key_value = jnp.where(
            upper_half,
            jnp.concatenate((partner, key_value), axis=2),
            jnp.concatenate((key_value, partner), axis=2),
        )
    groups = key_value.shape[2] // width
    half = heads_here // CORES
    core_route = [(i, i ^ 1) for i in range(seq_count)]
    first = core == 0

    if groups > 1:
        own_groups = groups // CORES
        split = own_groups * width
        low, high = key_value[:, :, :split], key_value[:, :, split:]
        kept, sent = jnp.where(first, low, high), jnp.where(first, high, low)
    else:
        own_groups = groups
        kept = sent = key_value
    got = lax.ppermute(sent, "seq", core_route)
    kv = jnp.where(
        first, jnp.concatenate((kept, got), axis=1), jnp.concatenate((got, kept), axis=1)
    )
    kv = jnp.concatenate((kv[0], kv[1]), axis=1)
    other_q = lax.ppermute(
        lax.dynamic_slice_in_dim(queries, (1 - core) * half * width, half * width, 1),
        "seq",
        core_route,
    )
    rows = CORES * row_count
    chunks = []
    for distance in range(1, chips):
        route = [(i, i + CORES * distance) for i in range(seq_count - CORES * distance)]
        chunks.append(lax.ppermute(kv, "seq", route))

    plan = Plan(rows, half, own_groups, width, feat_count)
    place = jnp.stack((chip, core)).astype(jnp.int32)
    q, mix, level, wide_t, keys_t = plan.local(place, queries, other_q, kv)
    mixes, levels, slopes, chunk_keys = [mix], [level], [], []
    for chunk in chunks[:1]:
        mix, level, slope, state, turned_keys = plan.chunk(place, q, chunk, feat_k)
        mixes.append(mix)
        levels.append(level)
        slopes.append(slope)
        chunk_keys.append(turned_keys)
    if not chunks:
        state = jnp.zeros(plan.state_type.shape, F32)
    total_parts = sum(STUDENT_PARTS)
    parts = STUDENT_PARTS if plan.steps % total_parts == 0 else (1,)
    unit = plan.steps // sum(parts)
    network = Reduction(chip, chips, seq_count)
    wholes, start, total, sent, count = [], 0, None, None, 0
    for index, part in enumerate(parts):
        steps = part * unit
        grads = plan.student(
            start, steps, chips, place, q, kv, chunk_keys, chunks, mixes, levels, slopes, wide_t, keys_t, feat_q, feat_k, state
        )
        start += steps
        grads, sent = lax.optimization_barrier((grads, sent))
        if sent is not None:
            total = network.received(sent, count, wholes)
        if index + 1 < len(parts):
            place, grads, total = lax.optimization_barrier((place, grads, total))
        sent, count = network.send(grads, total), 0 if total is None else total.shape[0]
    total = network.received(sent, count, wholes)
    network.received(network.send(None, total), total.shape[0], wholes)
    results = []
    for whole in wholes:
        whole = whole.reshape((-1,) + grads.shape[1:])
        results.append((whole, lax.ppermute(whole, "seq", core_route)))
    own = jnp.concatenate([pair[0] for pair in results], axis=0)
    other = jnp.concatenate([pair[1] for pair in results], axis=0)
    both = jnp.where(
        first, jnp.concatenate((own, other), axis=0), jnp.concatenate((other, own), axis=0)
    ).astype(F32)
    return both[:, 0], both[:, 1]


class Reduction:
    def __init__(self, chip, chips, seq_count):
        self.chip, self.chips, self.seq_count = chip, chips, seq_count

    def route(self, distance):
        count = self.seq_count
        return [(i, (i + CORES * distance) % count) for i in range(count)]

    def send(self, grads, total):
        sent = []
        for distance in range(self.chips):
            part = None
            if grads is not None:
                flat = grads.reshape(-1, grads.shape[-1])
                share = flat.shape[0] // self.chips
                place = (self.chip + distance) % self.chips
                part = lax.dynamic_slice_in_dim(flat, place * share, share, 0)
            block = jnp.concatenate([x for x in (total, part) if x is not None], axis=0)
            if distance:
                block = lax.ppermute(block, "seq", self.route(distance))
            sent.append(block)
        return sent

    def received(self, sent, count, wholes):
        if count:
            parts = [block[:count] for block in sent]
            order = jnp.concatenate(parts[::-1] + parts[:0:-1], axis=0)
            first = (self.chips - 1 - self.chip) * count
            wholes.append(lax.dynamic_slice_in_dim(order, first, self.chips * count, 0))
        if sent[0].shape[0] == count:
            return None
        return functools.reduce(
            jnp.add, [block[count:].astype(F32) for block in sent]
        ).astype(BF16)


def solution(mesh):
    return jax.shard_map(
        body,
        mesh=mesh,
        in_specs=(
            P("seq", "head"),
            P("seq", "head"),
            P("seq", "head"),
            P("head", None, None),
            P("head", None, None),
        ),
        out_specs=(P("head", None, None), P("head", None, None)),
        check_vma=False,
    )
```

```python
import functools
import math

import jax
import jax.numpy as jnp
from jax import lax
from jax.experimental import pallas as pl
from jax.experimental.pallas import tpu as pltpu
from jax.sharding import PartitionSpec as P

HEADS = 128
KV_HEADS = 8
CORES = 2
SUBLANES = 8
BLOCK_HEADS = 4
STUDENT_PARTS = (2, 1, 1)
LOCAL_WINDOW = 2
CHUNK_WINDOW = 2
UNIT_WINDOW = 8
LOG2E = math.log2(math.e)
MASKED_SCORE = -1e30
TINY_DECAY = 2.0**-11
SAFE_LOW = 2.0**-100
SAFE_HIGH = 2.0**120
VMEM_BYTES = 56 * 1024 * 1024
F32 = jnp.float32
BF16 = jnp.bfloat16

NN = (((1,), (0,)), ((), ()))
NT = (((1,), (1,)), ((), ()))
TN = (((0,), (0,)), ((), ()))


def dot(a, b, form):
    return lax.dot_general(a, b, form, preferred_element_type=F32)


def from_partner(block, axis, stride):
    count = lax.axis_size(axis)
    route = []
    for low in range(count):
        high = low | 1 << stride
        if high != low and high < count:
            route += [(low, high), (high, low)]
    return lax.ppermute(block, axis, route)


def tile_of(rows):
    return 256 if rows % 256 == 0 else rows


def with_ones(values):
    return jnp.concatenate((values, jnp.ones_like(values)), axis=1)


def turned(block):
    return block.astype(F32).T.astype(BF16)


def turned_with_ones(values):
    return jnp.concatenate((turned(values), jnp.ones((16, values.shape[0]), BF16)), axis=0)


def softplus_and_slope(pre):
    above, below = jnp.maximum(pre, 0.0), jnp.minimum(pre, 0.0)
    decay = jnp.exp(below - above)
    log_term = jnp.where(decay < TINY_DECAY, decay, jnp.log(1.0 + decay))
    return (above + log_term).astype(BF16), jnp.exp(below - log_term).astype(BF16)


def masked(mask, block, other):
    return block if mask is True else jnp.where(mask, block, other)


def columns(index, width):
    return slice(index * width, (index + 1) * width)


def causal_mask(rows):
    return lax.broadcasted_iota(jnp.int32, (rows, rows), 0) >= lax.broadcasted_iota(
        jnp.int32, (rows, rows), 1
    )


def interleave(tasks, window):
    waiting, active = list(tasks), []
    while waiting or active:
        if waiting and len(active) < window:
            active.append(waiting.pop(0))
        for task in active[::-1]:
            if next(task, active) is active:
                active.remove(task)


def mixture_task(scale, score_parts, values_t, unit, store):
    parts = score_parts(unit)
    yield
    weights = [masked(mask, jnp.exp2(part * scale), 0.0).astype(BF16) for part, mask in parts]
    weights = weights[0] if len(weights) == 1 else jnp.concatenate(weights, axis=0)
    store(unit, dot(values_t[:, : weights.shape[0]], weights, NN))


def attend(scale, causal, q_ref, k_ref, score_parts, values_t, mix_ref, level_ref, others, window):
    rows, width = k_ref.shape
    heads = q_ref.shape[1] // width
    tile = tile_of(rows)
    units = [(b, i) for i in range(rows // tile) for b in range(heads)]
    totals = []

    def store(unit, mixed):
        b, i = unit
        total = mixed[width : width + 1]
        mix_ref[columns(b, width), columns(i, tile)] = (mixed[:width] * (1.0 / total)).astype(BF16)
        level_ref[0, b : b + 1, columns(i, tile)] = jnp.log2(total)
        totals.append(total)

    spread, count = [], len(units)
    for place, unit in enumerate(units):
        spread += others[place * len(others) // count : (place + 1) * len(others) // count]
        spread.append(mixture_task(scale, score_parts, values_t, unit, store))
    interleave(spread, window)
    low = jnp.min(functools.reduce(jnp.minimum, totals))
    high = jnp.max(functools.reduce(jnp.maximum, totals))

    def shifted(index, carry):
        b, i = index % heads, index // heads
        here = pl.ds(pl.multiple_of(i * tile, tile), tile)
        head = pl.ds(pl.multiple_of(b * width, width), width)
        scores = dot(k_ref[...], q_ref[here, head], NT) * scale
        mask = True
        if causal:
            mask = lax.broadcasted_iota(jnp.int32, scores.shape, 0) <= i * tile + (
                lax.broadcasted_iota(jnp.int32, scores.shape, 1)
            )
        peak = jnp.max(masked(mask, scores, MASKED_SCORE), axis=0, keepdims=True)
        weights = masked(mask, jnp.exp2(scores - peak), 0.0).astype(BF16)
        mixed = dot(values_t[...], weights, NN)
        total = mixed[width : width + 1]
        mix_ref[head, here] = (mixed[:width] * (1.0 / total)).astype(BF16)
        level_ref[0, pl.ds(b, 1), here] = peak + jnp.log2(total)
        return carry

    @pl.when(jnp.logical_not((low > SAFE_LOW) & (high < SAFE_HIGH)))
    def _():
        lax.fori_loop(0, count, shifted, 0)


def local_attention(
    scale, group_steps, place_ref, own_ref, other_ref, k_ref, v_ref, q_ref, mix_ref, level_ref, turned_ref, keys_t
):
    rows, width = k_ref.shape
    heads = q_ref.shape[1] // width
    part = own_ref.shape[0]
    core = place_ref[1]
    q_ref[pl.ds(pl.multiple_of(core * part, part), part), :] = own_ref[...]
    q_ref[pl.ds(pl.multiple_of((1 - core) * part, part), part), :] = other_ref[...]
    @pl.when(pl.program_id(0) % group_steps == 0)
    def _():
        turned_ref[...] = turned_with_ones(v_ref[...])
        keys_t[...] = turned(k_ref[...])

    tile = tile_of(rows)
    mask = lax.broadcasted_iota(jnp.int32, (tile, tile), 0) <= lax.broadcasted_iota(
        jnp.int32, (tile, tile), 1
    )

    def score_parts(unit):
        b, i = unit
        query = q_ref[columns(i, tile), columns(b, width)]
        last = (dot(k_ref[columns(i, tile), :], query, NT), mask)
        return [last] if i == 0 else [(dot(k_ref[: i * tile, :], query, NT), True), last]

    attend(
        scale, True, q_ref, k_ref, score_parts, turned_ref, mix_ref, level_ref, [], LOCAL_WINDOW
    )


def chunk_block(
    scale, group_steps, q_ref, k_ref, v_ref, wk_ref, state_of, outs
):
    mix_ref, level_ref, slope_ref, state_ref, keys_t, turned_ref = outs
    rows, width = k_ref.shape
    heads = q_ref.shape[1] // width
    pairs = heads // 2

    @pl.when(pl.program_id(0) % group_steps == 0)
    def _():
        turned_ref[...] = turned_with_ones(v_ref[...])
        keys_t[...] = turned(k_ref[...])

    tile = tile_of(rows)
    keys = k_ref[...]

    def feature_task(pair):
        weight = jnp.concatenate((wk_ref[2 * pair], wk_ref[2 * pair + 1]), axis=1)
        pre = dot(keys, weight, NN)
        yield
        feat, slope = softplus_and_slope(pre)
        slope_ref[:, columns(pair, 2 * width)] = slope
        state_ref[pair] = state_of(pair) + dot(turned_ref[...], feat, NN)

    def score_parts(unit):
        b, i = unit
        return [(dot(keys, q_ref[columns(i, tile), columns(b, width)], NT), True)]

    features = [feature_task(pair) for pair in range(pairs)]
    attend(
        scale,
        False,
        q_ref,
        k_ref,
        score_parts,
        turned_ref,
        mix_ref,
        level_ref,
        features,
        CHUNK_WINDOW,
    )


def chunk_attention(scale, group_steps, place_ref, q_ref, k_ref, v_ref, wk_ref, *outs):
    mix_ref, level_ref, slope_ref, state_ref, keys_t, _ = outs

    @pl.when(place_ref[0] < 1)
    def _():
        mix_ref[...] = jnp.zeros_like(mix_ref)
        slope_ref[...] = jnp.zeros_like(slope_ref)
        level_ref[...] = jnp.full_like(level_ref, MASKED_SCORE)
        state_ref[...] = jnp.zeros_like(state_ref)
        keys_t[...] = jnp.zeros_like(keys_t)

    @pl.when(place_ref[0] >= 1)
    def _():
        chunk_block(scale, group_steps, q_ref, k_ref, v_ref, wk_ref, lambda pair: 0.0, outs)


def student(scale, group_steps, total_tokens, chunk_count, place_ref, q_ref, k_ref, v_ref, *refs):
    refs = list(refs)
    done = min(chunk_count, 1)
    chunk_keys = [refs.pop(0) for _ in range(chunk_count - done)]
    chunk_values = [refs.pop(0) for _ in range(chunk_count)]
    mix_refs = [refs.pop(0) for _ in range(done + 1)]
    level_refs = [refs.pop(0) for _ in range(done + 1)]
    slope_refs = [refs.pop(0) for _ in range(done)]
    chunk_keys_t = [refs.pop(0) for _ in range(done)]
    wide_t, keys_t, wq_ref, wk_ref, state_in, out_ref, wk_acc, state_ref = refs[:8]
    refs = refs[8:]
    state_ref[...] = state_in[...]
    for c in range(done, chunk_count):
        own = [refs.pop(0) for _ in range(5)]
        mix, level, slope, turned_keys, turned_values = own
        mix_refs.append(mix)
        level_refs.append(level)
        slope_refs.append(slope)
        chunk_keys_t.append(turned_keys)

        @pl.when(place_ref[0] < c + 1)
        def _(mix=mix, level=level):
            mix[...] = jnp.zeros_like(mix)
            level[...] = jnp.full_like(level, MASKED_SCORE)

        @pl.when(place_ref[0] >= c + 1)
        def _(c=c, own=own):
            chunk_block(
                scale,
                group_steps,
                q_ref,
                chunk_keys[c - done],
                chunk_values[c],
                wk_ref,
                lambda pair: state_ref[pair],
                (*own[:3], state_ref, *own[3:]),
            )

    rows, width = k_ref.shape
    heads = q_ref.shape[1] // width
    pairs = heads // 2
    tile = tile_of(rows)
    tiles = rows // tile
    mask = causal_mask(tile).astype(F32).astype(BF16)

    head_list = range(heads)
    tile_list = range(tiles)
    wide = [with_ones(v_ref[columns(i, tile), :]) for i in tile_list]
    key_feat, key_slope, states, shares = {}, {}, {}, {}

    def key_task(pair):
        weight = jnp.concatenate((wk_ref[2 * pair], wk_ref[2 * pair + 1]), axis=1)
        running = state_ref[pair]
        pre = dot(k_ref[columns(0, tile), :], weight, NN)
        for i in tile_list:
            yield
            later = dot(k_ref[columns(i + 1, tile), :], weight, NN) if i + 1 < tiles else None
            feat, slope = softplus_and_slope(pre)
            pre = later
            key_slope[pair, i] = slope
            for side in range(2):
                here = columns(side, width)
                key_feat[2 * pair + side, i] = feat[:, here]
                norm = jnp.broadcast_to(running[width : width + 1, here], (width, width))
                states[2 * pair + side, i] = jnp.concatenate(
                    (running[:width, here], norm), axis=0
                ).astype(BF16)
            if i + 1 < tiles:
                running = running + dot(wide_t[:, columns(i, tile)], feat, NN)

    def share_task(i):
        levels = [ref[0, :, columns(i, tile)] for ref in level_refs]
        peak = functools.reduce(jnp.maximum, levels)
        parts = [jnp.exp2(level - peak) for level in levels]
        inverse = 1.0 / functools.reduce(jnp.add, parts)
        shares[i] = [part * inverse for part in parts]
        yield

    interleave([key_task(pair) for pair in range(pairs)] + [share_task(i) for i in tile_list], 4)

    backs, query_change, key_change = {}, {}, {}

    def unit_task(b, i):
        here, head = columns(i, tile), columns(b, width)
        pre = dot(q_ref[here, head], wq_ref[b], NN)
        yield
        feat, slope = softplus_and_slope(pre)
        affinity = dot(feat, key_feat[b, i], NT)
        mixed = dot(feat, states[b, i], NT)
        yield
        affinity = affinity.astype(BF16) * mask
        mixed = mixed + dot(affinity, wide[i], NN)
        teacher = functools.reduce(
            jnp.add,
            [
                share[b : b + 1] * ref[head, here].astype(F32)
                for share, ref in zip(shares[i], mix_refs)
            ],
        )
        teacher = turned(teacher).astype(F32)
        yield
        inverse = 1.0 / mixed[:, width:]
        result = mixed[:, :width] * inverse
        grad_out = (result - teacher) * (2.0 / total_tokens)
        grad_denom = jnp.sum(grad_out * result, axis=1, keepdims=True) * inverse * (-1.0 / width)
        grads = jnp.concatenate((grad_out * inverse, grad_denom), axis=1).astype(BF16)
        grad_aff = dot(grads, wide[i], NT)
        backs[b, i] = dot(feat, grads, TN)
        yield
        grad_aff = grad_aff.astype(BF16) * mask
        grad_qfeat = dot(
            jnp.concatenate((grads, grad_aff), axis=1),
            jnp.concatenate((states[b, i], key_feat[b, i]), axis=0),
            NN,
        )
        key_change[b, i] = dot(grad_aff, feat, TN)
        yield
        query_change[b, i] = grad_qfeat.astype(BF16) * slope

    interleave([unit_task(b, i) for b in head_list for i in tile_list], UNIT_WINDOW)

    whole = [None] * pairs

    def query_weight_task(b):
        change = jnp.concatenate([query_change[b, i] for i in tile_list], axis=0)
        out_ref[b, 0] = dot(q_ref[:, columns(b, width)], change, TN).astype(out_ref.dtype)
        yield

    def key_weight_task(pair):
        sides = (2 * pair, 2 * pair + 1)
        running = [backs[b, tiles - 1] for b in sides]
        changes = [None] * tiles
        for i in reversed(tile_list):
            both = jnp.concatenate([key_change[b, i] for b in sides], axis=1)
            if i + 1 < tiles:
                later = jnp.concatenate(running, axis=0).astype(BF16)
                both = both + dot(wide[i], later, NT)
                running = [old + backs[b, i] for old, b in zip(running, sides)]
                yield
            changes[i] = both.astype(BF16) * key_slope[pair, i]
        whole[pair] = jnp.concatenate(running, axis=0).astype(BF16)
        wk_acc[pair] = dot(keys_t[...], jnp.concatenate(changes, axis=0), NN)

    tasks = []
    for pair in range(pairs):
        tasks += [query_weight_task(2 * pair), query_weight_task(2 * pair + 1)]
        tasks.append(key_weight_task(pair))
    interleave(tasks, 3)

    for c in range(chunk_count):

        @pl.when(place_ref[0] >= c + 1)
        def _(c=c):
            values = with_ones(chunk_values[c][...])
            sums = [None] * pairs

            def chunk_task(pair, i):
                here = columns(i, tile)
                slope = slope_refs[c][here, columns(pair, 2 * width)]
                change = dot(values[here], whole[pair], NT)
                yield
                change = change.astype(BF16) * slope
                term = dot(chunk_keys_t[c][:, here], change, NN)
                sums[pair] = term if i == 0 else sums[pair] + term
                if i == tiles - 1:
                    wk_acc[pair] += sums[pair]

            interleave([chunk_task(pair, i) for pair in range(pairs) for i in tile_list], 2)

    for b in head_list:
        out_ref[b, 1] = wk_acc[b // 2][:, columns(b % 2, width)].astype(out_ref.dtype)


def params():
    return pltpu.CompilerParams(
        vmem_limit_bytes=VMEM_BYTES, dimension_semantics=("arbitrary",)
    )


def cost(microseconds):
    return pl.CostEstimate(
        flops=int(microseconds * 1e9), bytes_accessed=int(microseconds * 3e6), transcendentals=0
    )


class Plan:
    def __init__(self, rows, half, groups, width, feats):
        self.rows, self.half, self.groups, self.width, self.feats = rows, half, groups, width, feats
        self.per_group = half // groups
        self.heads = math.gcd(self.per_group, BLOCK_HEADS)
        self.steps = half // self.heads
        self.mix_type = jax.ShapeDtypeStruct((half * width, rows), BF16)
        self.q_type = jax.ShapeDtypeStruct((rows, half * width), BF16)
        self.level_type = jax.ShapeDtypeStruct((self.steps, SUBLANES, rows), F32)
        self.state_type = jax.ShapeDtypeStruct((half // 2, width + 16, 2 * feats), F32)

    def turned_type(self, height):
        return jax.ShapeDtypeStruct((height * self.groups, self.rows), BF16)

    def specs(self, start=0):
        rows, width, heads, steps = self.rows, self.width, self.heads, self.steps
        groups, per_group = self.groups, self.per_group
        return dict(
            q=pl.BlockSpec((rows, heads * width), lambda h, *_: (0, start + h)),
            k=pl.BlockSpec((rows, width), lambda h, *_: (0, (start + h) * heads // per_group)),
            v=pl.BlockSpec(
                (rows, width), lambda h, *_: (0, groups + (start + h) * heads // per_group)
            ),
            mix=pl.BlockSpec((heads * width, rows), lambda h, *_: (start + h, 0)),
            wide_t=pl.BlockSpec((width + 16, rows), lambda h, *_: ((start + h) * heads // per_group, 0)),
            keys_t=pl.BlockSpec((width, rows), lambda h, *_: ((start + h) * heads // per_group, 0)),
            level=pl.BlockSpec((1, SUBLANES, rows), lambda h, *_: (start + h, 0, 0)),
            w=pl.BlockSpec(
                (heads, width, self.feats),
                lambda h, place: (place[1] * steps + start + h, 0, 0),
            ),
            state=pl.BlockSpec(
                (heads // 2, width + 16, 2 * self.feats), lambda h, *_: (start + h, 0, 0)
            ),
        )

    def local(self, place, queries, other_q, kv):
        at, steps = self.specs(), self.steps
        part, block = queries.shape[0], self.heads * self.width
        return pl.pallas_call(
            functools.partial(
                local_attention, self.width ** (-0.5) * LOG2E, self.per_group // self.heads
            ),
            grid_spec=pltpu.PrefetchScalarGridSpec(
                num_scalar_prefetch=1,
                grid=(steps,),
                in_specs=[
                    pl.BlockSpec((part, block), lambda h, place: (0, place[1] * steps + h)),
                    pl.BlockSpec((part, block), lambda h, *_: (0, h)),
                    at["k"],
                    at["v"],
                ],
                out_specs=[at["q"], at["mix"], at["level"], at["wide_t"], at["keys_t"]],
            ),
            out_shape=[
                self.q_type,
                self.mix_type,
                self.level_type,
                self.turned_type(self.width + 16),
                self.turned_type(self.width),
            ],
            compiler_params=params(),
            cost_estimate=cost(12),
            name="local_attention",
        )(place, queries, other_q, kv, kv)

    def chunk(self, place, q, chunk, feat_k):
        at = self.specs()
        return pl.pallas_call(
            functools.partial(
                chunk_attention,
                self.width ** (-0.5) * LOG2E,
                self.per_group // self.heads,
            ),
            grid_spec=pltpu.PrefetchScalarGridSpec(
                num_scalar_prefetch=1,
                grid=(self.steps,),
                in_specs=[at["q"], at["k"], at["v"], at["w"]],
                out_specs=[at["mix"], at["level"], at["q"], at["state"], at["keys_t"]],
                scratch_shapes=[pltpu.VMEM((self.width + 16, self.rows), BF16)],
            ),
            out_shape=[
                self.mix_type,
                self.level_type,
                self.q_type,
                self.state_type,
                self.turned_type(self.width),
            ],
            compiler_params=params(),
            cost_estimate=cost(18),
            name="chunk_attention",
        )(place, q, chunk, chunk, feat_k)

    def student(
        self,
        start,
        steps,
        chips,
        place,
        q,
        kv,
        chunk_keys,
        chunks,
        mixes,
        levels,
        slopes,
        wide_t,
        keys_t,
        wq,
        wk,
        state,
    ):
        at = self.specs(start)
        count, width, rows = len(chunks), self.width, self.rows
        grad_shape = (self.heads, 2, width, self.feats)
        done = len(slopes)
        return pl.pallas_call(
            functools.partial(
                student,
                width ** (-0.5) * LOG2E,
                self.per_group // self.heads,
                chips * rows,
                count,
            ),
            grid_spec=pltpu.PrefetchScalarGridSpec(
                num_scalar_prefetch=1,
                grid=(steps,),
                in_specs=[at["q"], at["k"], at["v"]]
                + [at["k"]] * (count - done)
                + [at["v"]] * count
                + [at["mix"]] * len(mixes)
                + [at["level"]] * len(levels)
                + [at["q"]] * done
                + [at["keys_t"]] * done
                + [at["wide_t"], at["keys_t"], at["w"], at["w"], at["state"]],
                out_specs=pl.BlockSpec(grad_shape, lambda h, *_: (h, 0, 0, 0)),
                scratch_shapes=[
                    pltpu.VMEM((self.heads // 2, width, 2 * self.feats), F32),
                    pltpu.VMEM((self.heads // 2, width + 16, 2 * self.feats), F32),
                ]
                + [
                    pltpu.VMEM((self.heads * width, rows), BF16),
                    pltpu.VMEM((1, SUBLANES, rows), F32),
                    pltpu.VMEM((rows, self.heads * width), BF16),
                    pltpu.VMEM((width, rows), BF16),
                    pltpu.VMEM((width + 16, rows), BF16),
                ]
                * (count - done),
            ),
            out_shape=jax.ShapeDtypeStruct((steps * self.heads,) + grad_shape[1:], BF16),
            compiler_params=params(),
            cost_estimate=cost(20 * steps),
            name="student",
        )(
            place, q, kv, kv, *chunks[done:], *chunks, *mixes, *levels, *slopes, *chunk_keys, wide_t, keys_t, wq, wk, state
        )


def body(queries, keys, values, feat_q, feat_k):
    row_count = queries.shape[0]
    heads_here, width, feat_count = feat_q.shape
    seq_count = lax.axis_size("seq")
    chips = seq_count // CORES
    seq_place = lax.axis_index("seq")
    core, chip = seq_place % CORES, seq_place // CORES
    head_place = lax.axis_index("head")
    spread = max(1, HEADS // KV_HEADS // heads_here)
    key_value = jnp.stack((keys, values))
    for bit_index in range(spread.bit_length() - 1):
        partner = from_partner(key_value, "head", bit_index)
        upper_half = head_place // (1 << bit_index) % 2 == 1
        key_value = jnp.where(
            upper_half,
            jnp.concatenate((partner, key_value), axis=2),
            jnp.concatenate((key_value, partner), axis=2),
        )
    groups = key_value.shape[2] // width
    half = heads_here // CORES
    core_route = [(i, i ^ 1) for i in range(seq_count)]
    first = core == 0

    if groups > 1:
        own_groups = groups // CORES
        split = own_groups * width
        low, high = key_value[:, :, :split], key_value[:, :, split:]
        kept, sent = jnp.where(first, low, high), jnp.where(first, high, low)
    else:
        own_groups = groups
        kept = sent = key_value
    got = lax.ppermute(sent, "seq", core_route)
    kv = jnp.where(
        first, jnp.concatenate((kept, got), axis=1), jnp.concatenate((got, kept), axis=1)
    )
    kv = jnp.concatenate((kv[0], kv[1]), axis=1)
    other_q = lax.ppermute(
        lax.dynamic_slice_in_dim(queries, (1 - core) * half * width, half * width, 1),
        "seq",
        core_route,
    )
    rows = CORES * row_count
    chunks = []
    for distance in range(1, chips):
        route = [(i, i + CORES * distance) for i in range(seq_count - CORES * distance)]
        chunks.append(lax.ppermute(kv, "seq", route))

    plan = Plan(rows, half, own_groups, width, feat_count)
    place = jnp.stack((chip, core)).astype(jnp.int32)
    q, mix, level, wide_t, keys_t = plan.local(place, queries, other_q, kv)
    mixes, levels, slopes, chunk_keys = [mix], [level], [], []
    for chunk in chunks[:1]:
        mix, level, slope, state, turned_keys = plan.chunk(place, q, chunk, feat_k)
        mixes.append(mix)
        levels.append(level)
        slopes.append(slope)
        chunk_keys.append(turned_keys)
    if not chunks:
        state = jnp.zeros(plan.state_type.shape, F32)
    total_parts = sum(STUDENT_PARTS)
    parts = STUDENT_PARTS if plan.steps % total_parts == 0 else (1,)
    unit = plan.steps // sum(parts)
    network = Reduction(chip, chips, seq_count)
    wholes, start, total, sent, count = [], 0, None, None, 0
    for index, part in enumerate(parts):
        steps = part * unit
        grads = plan.student(
            start, steps, chips, place, q, kv, chunk_keys, chunks, mixes, levels, slopes, wide_t, keys_t, feat_q, feat_k, state
        )
        start += steps
        grads, sent = lax.optimization_barrier((grads, sent))
        if sent is not None:
            total = network.received(sent, count, wholes)
        if index + 1 < len(parts):
            place, grads, total = lax.optimization_barrier((place, grads, total))
        sent, count = network.send(grads, total), 0 if total is None else total.shape[0]
    total = network.received(sent, count, wholes)
    network.received(network.send(None, total), total.shape[0], wholes)
    results = []
    for whole in wholes:
        whole = whole.reshape((-1,) + grads.shape[1:])
        results.append((whole, lax.ppermute(whole, "seq", core_route)))
    own = jnp.concatenate([pair[0] for pair in results], axis=0)
    other = jnp.concatenate([pair[1] for pair in results], axis=0)
    both = jnp.where(
        first, jnp.concatenate((own, other), axis=0), jnp.concatenate((other, own), axis=0)
    ).astype(F32)
    return both[:, 0], both[:, 1]


class Reduction:
    def __init__(self, chip, chips, seq_count):
        self.chip, self.chips, self.seq_count = chip, chips, seq_count

    def route(self, distance):
        count = self.seq_count
        return [(i, (i + CORES * distance) % count) for i in range(count)]

    def send(self, grads, total):
        sent = []
        for distance in range(self.chips):
            part = None
            if grads is not None:
                flat = grads.reshape(-1, grads.shape[-1])
                share = flat.shape[0] // self.chips
                place = (self.chip + distance) % self.chips
                part = lax.dynamic_slice_in_dim(flat, place * share, share, 0)
            block = jnp.concatenate([x for x in (total, part) if x is not None], axis=0)
            if distance:
                block = lax.ppermute(block, "seq", self.route(distance))
            sent.append(block)
        return sent

    def received(self, sent, count, wholes):
        if count:
            parts = [block[:count] for block in sent]
            order = jnp.concatenate(parts[::-1] + parts[:0:-1], axis=0)
            first = (self.chips - 1 - self.chip) * count
            wholes.append(lax.dynamic_slice_in_dim(order, first, self.chips * count, 0))
        if sent[0].shape[0] == count:
            return None
        return functools.reduce(
            jnp.add, [block[count:].astype(F32) for block in sent]
        ).astype(BF16)


def solution(mesh):
    return jax.shard_map(
        body,
        mesh=mesh,
        in_specs=(
            P("seq", "head"),
            P("seq", "head"),
            P("seq", "head"),
            P("head", None, None),
            P("head", None, None),
        ),
        out_specs=(P("head", None, None), P("head", None, None)),
        check_vma=False,
    )
```

```python
import functools
import math

import jax
import jax.numpy as jnp
from jax import lax
from jax.experimental import pallas as pl
from jax.experimental.pallas import tpu as pltpu
from jax.sharding import PartitionSpec as P

HEADS = 128
KV_HEADS = 8
CORES = 2
SUBLANES = 8
BLOCK_HEADS = 4
STUDENT_PARTS = (2, 1, 1)
LOCAL_WINDOW = 2
CHUNK_WINDOW = 2
UNIT_WINDOW = 8
LOG2E = math.log2(math.e)
MASKED_SCORE = -1e30
TINY_DECAY = 2.0**-11
SAFE_LOW = 2.0**-100
SAFE_HIGH = 2.0**120
VMEM_BYTES = 56 * 1024 * 1024
F32 = jnp.float32
BF16 = jnp.bfloat16

NN = (((1,), (0,)), ((), ()))
NT = (((1,), (1,)), ((), ()))
TN = (((0,), (0,)), ((), ()))


def dot(a, b, form):
    return lax.dot_general(a, b, form, preferred_element_type=F32)


def from_partner(block, axis, stride):
    count = lax.axis_size(axis)
    route = []
    for low in range(count):
        high = low | 1 << stride
        if high != low and high < count:
            route += [(low, high), (high, low)]
    return lax.ppermute(block, axis, route)


def tile_of(rows):
    return 256 if rows % 256 == 0 else rows


def with_ones(values):
    return jnp.concatenate((values, jnp.ones_like(values)), axis=1)


def turned(block):
    return block.astype(F32).T.astype(BF16)


def turned_with_ones(values):
    return jnp.concatenate((turned(values), jnp.ones((16, values.shape[0]), BF16)), axis=0)


def softplus_and_slope(pre):
    above, below = jnp.maximum(pre, 0.0), jnp.minimum(pre, 0.0)
    decay = jnp.exp(below - above)
    log_term = jnp.where(decay < TINY_DECAY, decay, jnp.log(1.0 + decay))
    return (above + log_term).astype(BF16), jnp.exp(below - log_term).astype(BF16)


def masked(mask, block, other):
    return block if mask is True else jnp.where(mask, block, other)


def columns(index, width):
    return slice(index * width, (index + 1) * width)


def causal_mask(rows):
    return lax.broadcasted_iota(jnp.int32, (rows, rows), 0) >= lax.broadcasted_iota(
        jnp.int32, (rows, rows), 1
    )


def interleave(tasks, window):
    waiting, active = list(tasks), []
    while waiting or active:
        if waiting and len(active) < window:
            active.append(waiting.pop(0))
        for task in active[::-1]:
            if next(task, active) is active:
                active.remove(task)


def mixture_task(scale, score_parts, values_t, unit, store):
    parts = score_parts(unit)
    yield
    weights = [masked(mask, jnp.exp2(part * scale), 0.0).astype(BF16) for part, mask in parts]
    weights = weights[0] if len(weights) == 1 else jnp.concatenate(weights, axis=0)
    store(unit, dot(values_t[:, : weights.shape[0]], weights, NN))


def attend(scale, causal, tile, q_ref, k_ref, score_parts, values_t, mix_ref, level_ref, others, window):
    rows, width = k_ref.shape
    heads = q_ref.shape[1] // width
    units = [(b, i) for i in range(rows // tile) for b in range(heads)]
    totals = []

    def store(unit, mixed):
        b, i = unit
        total = mixed[width : width + 1]
        mix_ref[columns(b, width), columns(i, tile)] = (mixed[:width] * (1.0 / total)).astype(BF16)
        level_ref[0, b : b + 1, columns(i, tile)] = jnp.log2(total)
        totals.append(total)

    spread, count = [], len(units)
    for place, unit in enumerate(units):
        spread += others[place * len(others) // count : (place + 1) * len(others) // count]
        spread.append(mixture_task(scale, score_parts, values_t, unit, store))
    interleave(spread, window)
    low = jnp.min(functools.reduce(jnp.minimum, totals))
    high = jnp.max(functools.reduce(jnp.maximum, totals))

    def shifted(index, carry):
        b, i = index % heads, index // heads
        here = pl.ds(pl.multiple_of(i * tile, tile), tile)
        head = pl.ds(pl.multiple_of(b * width, width), width)
        scores = dot(k_ref[...], q_ref[here, head], NT) * scale
        mask = True
        if causal:
            mask = lax.broadcasted_iota(jnp.int32, scores.shape, 0) <= i * tile + (
                lax.broadcasted_iota(jnp.int32, scores.shape, 1)
            )
        peak = jnp.max(masked(mask, scores, MASKED_SCORE), axis=0, keepdims=True)
        weights = masked(mask, jnp.exp2(scores - peak), 0.0).astype(BF16)
        mixed = dot(values_t[...], weights, NN)
        total = mixed[width : width + 1]
        mix_ref[head, here] = (mixed[:width] * (1.0 / total)).astype(BF16)
        level_ref[0, pl.ds(b, 1), here] = peak + jnp.log2(total)
        return carry

    @pl.when(jnp.logical_not((low > SAFE_LOW) & (high < SAFE_HIGH)))
    def _():
        lax.fori_loop(0, count, shifted, 0)


def local_attention(
    scale, group_steps, place_ref, own_ref, other_ref, k_ref, v_ref, q_ref, mix_ref, level_ref, turned_ref, keys_t
):
    rows, width = k_ref.shape
    heads = q_ref.shape[1] // width
    part = own_ref.shape[0]
    core = place_ref[1]
    q_ref[pl.ds(pl.multiple_of(core * part, part), part), :] = own_ref[...]
    q_ref[pl.ds(pl.multiple_of((1 - core) * part, part), part), :] = other_ref[...]
    @pl.when(pl.program_id(0) % group_steps == 0)
    def _():
        turned_ref[...] = turned_with_ones(v_ref[...])
        keys_t[...] = turned(k_ref[...])

    tile = tile_of(rows)
    mask = lax.broadcasted_iota(jnp.int32, (tile, tile), 0) <= lax.broadcasted_iota(
        jnp.int32, (tile, tile), 1
    )

    def score_parts(unit):
        b, i = unit
        query = q_ref[columns(i, tile), columns(b, width)]
        last = (dot(k_ref[columns(i, tile), :], query, NT), mask)
        return [last] if i == 0 else [(dot(k_ref[: i * tile, :], query, NT), True), last]

    attend(
        scale,
        True,
        tile,
        q_ref,
        k_ref,
        score_parts,
        turned_ref,
        mix_ref,
        level_ref,
        [],
        LOCAL_WINDOW,
    )


def chunk_block(
    scale, group_steps, q_ref, k_ref, v_ref, wk_ref, state_of, outs
):
    mix_ref, level_ref, slope_ref, state_ref, keys_t, turned_ref = outs
    rows, width = k_ref.shape
    heads = q_ref.shape[1] // width
    pairs = heads // 2

    @pl.when(pl.program_id(0) % group_steps == 0)
    def _():
        turned_ref[...] = turned_with_ones(v_ref[...])
        keys_t[...] = turned(k_ref[...])

    tile = rows
    keys = k_ref[...]

    def feature_task(pair):
        weight = jnp.concatenate((wk_ref[2 * pair], wk_ref[2 * pair + 1]), axis=1)
        pre = dot(keys, weight, NN)
        yield
        feat, slope = softplus_and_slope(pre)
        slope_ref[:, columns(pair, 2 * width)] = slope
        state_ref[pair] = state_of(pair) + dot(turned_ref[...], feat, NN)

    def score_parts(unit):
        b, i = unit
        return [(dot(keys, q_ref[columns(i, tile), columns(b, width)], NT), True)]

    features = [feature_task(pair) for pair in range(pairs)]
    attend(
        scale,
        False,
        tile,
        q_ref,
        k_ref,
        score_parts,
        turned_ref,
        mix_ref,
        level_ref,
        features,
        CHUNK_WINDOW,
    )


def chunk_attention(scale, group_steps, place_ref, q_ref, k_ref, v_ref, wk_ref, *outs):
    mix_ref, level_ref, slope_ref, state_ref, keys_t, _ = outs

    @pl.when(place_ref[0] < 1)
    def _():
        mix_ref[...] = jnp.zeros_like(mix_ref)
        slope_ref[...] = jnp.zeros_like(slope_ref)
        level_ref[...] = jnp.full_like(level_ref, MASKED_SCORE)
        state_ref[...] = jnp.zeros_like(state_ref)
        keys_t[...] = jnp.zeros_like(keys_t)

    @pl.when(place_ref[0] >= 1)
    def _():
        chunk_block(scale, group_steps, q_ref, k_ref, v_ref, wk_ref, lambda pair: 0.0, outs)


def student(scale, group_steps, total_tokens, chunk_count, place_ref, q_ref, k_ref, v_ref, *refs):
    refs = list(refs)
    done = min(chunk_count, 1)
    chunk_keys = [refs.pop(0) for _ in range(chunk_count - done)]
    chunk_values = [refs.pop(0) for _ in range(chunk_count)]
    mix_refs = [refs.pop(0) for _ in range(done + 1)]
    level_refs = [refs.pop(0) for _ in range(done + 1)]
    slope_refs = [refs.pop(0) for _ in range(done)]
    chunk_keys_t = [refs.pop(0) for _ in range(done)]
    wide_t, keys_t, wq_ref, wk_ref, state_in, out_ref, wk_acc, state_ref = refs[:8]
    refs = refs[8:]
    state_ref[...] = state_in[...]
    for c in range(done, chunk_count):
        own = [refs.pop(0) for _ in range(5)]
        mix, level, slope, turned_keys, turned_values = own
        mix_refs.append(mix)
        level_refs.append(level)
        slope_refs.append(slope)
        chunk_keys_t.append(turned_keys)

        @pl.when(place_ref[0] < c + 1)
        def _(mix=mix, level=level):
            mix[...] = jnp.zeros_like(mix)
            level[...] = jnp.full_like(level, MASKED_SCORE)

        @pl.when(place_ref[0] >= c + 1)
        def _(c=c, own=own):
            chunk_block(
                scale,
                group_steps,
                q_ref,
                chunk_keys[c - done],
                chunk_values[c],
                wk_ref,
                lambda pair: state_ref[pair],
                (*own[:3], state_ref, *own[3:]),
            )

    rows, width = k_ref.shape
    heads = q_ref.shape[1] // width
    pairs = heads // 2
    tile = tile_of(rows)
    tiles = rows // tile
    mask = causal_mask(tile).astype(F32).astype(BF16)

    head_list = range(heads)
    tile_list = range(tiles)
    wide = [with_ones(v_ref[columns(i, tile), :]) for i in tile_list]
    key_feat, key_slope, states, shares = {}, {}, {}, {}

    def key_task(pair):
        weight = jnp.concatenate((wk_ref[2 * pair], wk_ref[2 * pair + 1]), axis=1)
        running = state_ref[pair]
        pre = dot(k_ref[columns(0, tile), :], weight, NN)
        for i in tile_list:
            yield
            later = dot(k_ref[columns(i + 1, tile), :], weight, NN) if i + 1 < tiles else None
            feat, slope = softplus_and_slope(pre)
            pre = later
            key_slope[pair, i] = slope
            for side in range(2):
                here = columns(side, width)
                key_feat[2 * pair + side, i] = feat[:, here]
                norm = jnp.broadcast_to(running[width : width + 1, here], (width, width))
                states[2 * pair + side, i] = jnp.concatenate(
                    (running[:width, here], norm), axis=0
                ).astype(BF16)
            if i + 1 < tiles:
                running = running + dot(wide_t[:, columns(i, tile)], feat, NN)

    def share_task(i):
        levels = [ref[0, :, columns(i, tile)] for ref in level_refs]
        peak = functools.reduce(jnp.maximum, levels)
        parts = [jnp.exp2(level - peak) for level in levels]
        inverse = 1.0 / functools.reduce(jnp.add, parts)
        shares[i] = [part * inverse for part in parts]
        yield

    interleave([key_task(pair) for pair in range(pairs)] + [share_task(i) for i in tile_list], 4)

    backs, query_change, key_change = {}, {}, {}

    def unit_task(b, i):
        here, head = columns(i, tile), columns(b, width)
        pre = dot(q_ref[here, head], wq_ref[b], NN)
        yield
        feat, slope = softplus_and_slope(pre)
        affinity = dot(feat, key_feat[b, i], NT)
        mixed = dot(feat, states[b, i], NT)
        yield
        affinity = affinity.astype(BF16) * mask
        mixed = mixed + dot(affinity, wide[i], NN)
        teacher = functools.reduce(
            jnp.add,
            [
                share[b : b + 1] * ref[head, here].astype(F32)
                for share, ref in zip(shares[i], mix_refs)
            ],
        )
        teacher = turned(teacher).astype(F32)
        yield
        inverse = 1.0 / mixed[:, width:]
        result = mixed[:, :width] * inverse
        grad_out = (result - teacher) * (2.0 / total_tokens)
        grad_denom = jnp.sum(grad_out * result, axis=1, keepdims=True) * inverse * (-1.0 / width)
        grads = jnp.concatenate((grad_out * inverse, grad_denom), axis=1).astype(BF16)
        grad_aff = dot(grads, wide[i], NT)
        backs[b, i] = dot(feat, grads, TN)
        yield
        grad_aff = grad_aff.astype(BF16) * mask
        grad_qfeat = dot(
            jnp.concatenate((grads, grad_aff), axis=1),
            jnp.concatenate((states[b, i], key_feat[b, i]), axis=0),
            NN,
        )
        key_change[b, i] = dot(grad_aff, feat, TN)
        yield
        query_change[b, i] = grad_qfeat.astype(BF16) * slope

    interleave([unit_task(b, i) for b in head_list for i in tile_list], UNIT_WINDOW)

    whole = [None] * pairs

    def query_weight_task(b):
        change = jnp.concatenate([query_change[b, i] for i in tile_list], axis=0)
        out_ref[b, 0] = dot(q_ref[:, columns(b, width)], change, TN).astype(out_ref.dtype)
        yield

    def key_weight_task(pair):
        sides = (2 * pair, 2 * pair + 1)
        running = [backs[b, tiles - 1] for b in sides]
        changes = [None] * tiles
        for i in reversed(tile_list):
            both = jnp.concatenate([key_change[b, i] for b in sides], axis=1)
            if i + 1 < tiles:
                later = jnp.concatenate(running, axis=0).astype(BF16)
                both = both + dot(wide[i], later, NT)
                running = [old + backs[b, i] for old, b in zip(running, sides)]
                yield
            changes[i] = both.astype(BF16) * key_slope[pair, i]
        whole[pair] = jnp.concatenate(running, axis=0).astype(BF16)
        wk_acc[pair] = dot(keys_t[...], jnp.concatenate(changes, axis=0), NN)

    tasks = []
    for pair in range(pairs):
        tasks += [query_weight_task(2 * pair), query_weight_task(2 * pair + 1)]
        tasks.append(key_weight_task(pair))
    interleave(tasks, 3)

    for c in range(chunk_count):

        @pl.when(place_ref[0] >= c + 1)
        def _(c=c):
            values = with_ones(chunk_values[c][...])
            sums = [None] * pairs

            def chunk_task(pair, i):
                here = columns(i, tile)
                slope = slope_refs[c][here, columns(pair, 2 * width)]
                change = dot(values[here], whole[pair], NT)
                yield
                change = change.astype(BF16) * slope
                term = dot(chunk_keys_t[c][:, here], change, NN)
                sums[pair] = term if i == 0 else sums[pair] + term
                if i == tiles - 1:
                    wk_acc[pair] += sums[pair]

            interleave([chunk_task(pair, i) for pair in range(pairs) for i in tile_list], 2)

    for b in head_list:
        out_ref[b, 1] = wk_acc[b // 2][:, columns(b % 2, width)].astype(out_ref.dtype)


def params():
    return pltpu.CompilerParams(
        vmem_limit_bytes=VMEM_BYTES, dimension_semantics=("arbitrary",)
    )


def cost(microseconds):
    return pl.CostEstimate(
        flops=int(microseconds * 1e9), bytes_accessed=int(microseconds * 3e6), transcendentals=0
    )


class Plan:
    def __init__(self, rows, half, groups, width, feats):
        self.rows, self.half, self.groups, self.width, self.feats = rows, half, groups, width, feats
        self.per_group = half // groups
        self.heads = math.gcd(self.per_group, BLOCK_HEADS)
        self.steps = half // self.heads
        self.mix_type = jax.ShapeDtypeStruct((half * width, rows), BF16)
        self.q_type = jax.ShapeDtypeStruct((rows, half * width), BF16)
        self.level_type = jax.ShapeDtypeStruct((self.steps, SUBLANES, rows), F32)
        self.state_type = jax.ShapeDtypeStruct((half // 2, width + 16, 2 * feats), F32)

    def turned_type(self, height):
        return jax.ShapeDtypeStruct((height * self.groups, self.rows), BF16)

    def specs(self, start=0):
        rows, width, heads, steps = self.rows, self.width, self.heads, self.steps
        groups, per_group = self.groups, self.per_group
        return dict(
            q=pl.BlockSpec((rows, heads * width), lambda h, *_: (0, start + h)),
            k=pl.BlockSpec((rows, width), lambda h, *_: (0, (start + h) * heads // per_group)),
            v=pl.BlockSpec(
                (rows, width), lambda h, *_: (0, groups + (start + h) * heads // per_group)
            ),
            mix=pl.BlockSpec((heads * width, rows), lambda h, *_: (start + h, 0)),
            wide_t=pl.BlockSpec((width + 16, rows), lambda h, *_: ((start + h) * heads // per_group, 0)),
            keys_t=pl.BlockSpec((width, rows), lambda h, *_: ((start + h) * heads // per_group, 0)),
            level=pl.BlockSpec((1, SUBLANES, rows), lambda h, *_: (start + h, 0, 0)),
            w=pl.BlockSpec(
                (heads, width, self.feats),
                lambda h, place: (place[1] * steps + start + h, 0, 0),
            ),
            state=pl.BlockSpec(
                (heads // 2, width + 16, 2 * self.feats), lambda h, *_: (start + h, 0, 0)
            ),
        )

    def local(self, place, queries, other_q, kv):
        at, steps = self.specs(), self.steps
        part, block = queries.shape[0], self.heads * self.width
        return pl.pallas_call(
            functools.partial(
                local_attention, self.width ** (-0.5) * LOG2E, self.per_group // self.heads
            ),
            grid_spec=pltpu.PrefetchScalarGridSpec(
                num_scalar_prefetch=1,
                grid=(steps,),
                in_specs=[
                    pl.BlockSpec((part, block), lambda h, place: (0, place[1] * steps + h)),
                    pl.BlockSpec((part, block), lambda h, *_: (0, h)),
                    at["k"],
                    at["v"],
                ],
                out_specs=[at["q"], at["mix"], at["level"], at["wide_t"], at["keys_t"]],
            ),
            out_shape=[
                self.q_type,
                self.mix_type,
                self.level_type,
                self.turned_type(self.width + 16),
                self.turned_type(self.width),
            ],
            compiler_params=params(),
            cost_estimate=cost(12),
            name="local_attention",
        )(place, queries, other_q, kv, kv)

    def chunk(self, place, q, chunk, feat_k):
        at = self.specs()
        return pl.pallas_call(
            functools.partial(
                chunk_attention,
                self.width ** (-0.5) * LOG2E,
                self.per_group // self.heads,
            ),
            grid_spec=pltpu.PrefetchScalarGridSpec(
                num_scalar_prefetch=1,
                grid=(self.steps,),
                in_specs=[at["q"], at["k"], at["v"], at["w"]],
                out_specs=[at["mix"], at["level"], at["q"], at["state"], at["keys_t"]],
                scratch_shapes=[pltpu.VMEM((self.width + 16, self.rows), BF16)],
            ),
            out_shape=[
                self.mix_type,
                self.level_type,
                self.q_type,
                self.state_type,
                self.turned_type(self.width),
            ],
            compiler_params=params(),
            cost_estimate=cost(18),
            name="chunk_attention",
        )(place, q, chunk, chunk, feat_k)

    def student(
        self,
        start,
        steps,
        chips,
        place,
        q,
        kv,
        chunk_keys,
        chunks,
        mixes,
        levels,
        slopes,
        wide_t,
        keys_t,
        wq,
        wk,
        state,
    ):
        at = self.specs(start)
        count, width, rows = len(chunks), self.width, self.rows
        grad_shape = (self.heads, 2, width, self.feats)
        done = len(slopes)
        return pl.pallas_call(
            functools.partial(
                student,
                width ** (-0.5) * LOG2E,
                self.per_group // self.heads,
                chips * rows,
                count,
            ),
            grid_spec=pltpu.PrefetchScalarGridSpec(
                num_scalar_prefetch=1,
                grid=(steps,),
                in_specs=[at["q"], at["k"], at["v"]]
                + [at["k"]] * (count - done)
                + [at["v"]] * count
                + [at["mix"]] * len(mixes)
                + [at["level"]] * len(levels)
                + [at["q"]] * done
                + [at["keys_t"]] * done
                + [at["wide_t"], at["keys_t"], at["w"], at["w"], at["state"]],
                out_specs=pl.BlockSpec(grad_shape, lambda h, *_: (h, 0, 0, 0)),
                scratch_shapes=[
                    pltpu.VMEM((self.heads // 2, width, 2 * self.feats), F32),
                    pltpu.VMEM((self.heads // 2, width + 16, 2 * self.feats), F32),
                ]
                + [
                    pltpu.VMEM((self.heads * width, rows), BF16),
                    pltpu.VMEM((1, SUBLANES, rows), F32),
                    pltpu.VMEM((rows, self.heads * width), BF16),
                    pltpu.VMEM((width, rows), BF16),
                    pltpu.VMEM((width + 16, rows), BF16),
                ]
                * (count - done),
            ),
            out_shape=jax.ShapeDtypeStruct((steps * self.heads,) + grad_shape[1:], BF16),
            compiler_params=params(),
            cost_estimate=cost(20 * steps),
            name="student",
        )(
            place, q, kv, kv, *chunks[done:], *chunks, *mixes, *levels, *slopes, *chunk_keys, wide_t, keys_t, wq, wk, state
        )


def body(queries, keys, values, feat_q, feat_k):
    row_count = queries.shape[0]
    heads_here, width, feat_count = feat_q.shape
    seq_count = lax.axis_size("seq")
    chips = seq_count // CORES
    seq_place = lax.axis_index("seq")
    core, chip = seq_place % CORES, seq_place // CORES
    head_place = lax.axis_index("head")
    spread = max(1, HEADS // KV_HEADS // heads_here)
    key_value = jnp.stack((keys, values))
    for bit_index in range(spread.bit_length() - 1):
        partner = from_partner(key_value, "head", bit_index)
        upper_half = head_place // (1 << bit_index) % 2 == 1
        key_value = jnp.where(
            upper_half,
            jnp.concatenate((partner, key_value), axis=2),
            jnp.concatenate((key_value, partner), axis=2),
        )
    groups = key_value.shape[2] // width
    half = heads_here // CORES
    core_route = [(i, i ^ 1) for i in range(seq_count)]
    first = core == 0

    if groups > 1:
        own_groups = groups // CORES
        split = own_groups * width
        low, high = key_value[:, :, :split], key_value[:, :, split:]
        kept, sent = jnp.where(first, low, high), jnp.where(first, high, low)
    else:
        own_groups = groups
        kept = sent = key_value
    got = lax.ppermute(sent, "seq", core_route)
    kv = jnp.where(
        first, jnp.concatenate((kept, got), axis=1), jnp.concatenate((got, kept), axis=1)
    )
    kv = jnp.concatenate((kv[0], kv[1]), axis=1)
    other_q = lax.ppermute(
        lax.dynamic_slice_in_dim(queries, (1 - core) * half * width, half * width, 1),
        "seq",
        core_route,
    )
    rows = CORES * row_count
    chunks = []
    for distance in range(1, chips):
        route = [(i, i + CORES * distance) for i in range(seq_count - CORES * distance)]
        chunks.append(lax.ppermute(kv, "seq", route))

    plan = Plan(rows, half, own_groups, width, feat_count)
    place = jnp.stack((chip, core)).astype(jnp.int32)
    q, mix, level, wide_t, keys_t = plan.local(place, queries, other_q, kv)
    mixes, levels, slopes, chunk_keys = [mix], [level], [], []
    for chunk in chunks[:1]:
        mix, level, slope, state, turned_keys = plan.chunk(place, q, chunk, feat_k)
        mixes.append(mix)
        levels.append(level)
        slopes.append(slope)
        chunk_keys.append(turned_keys)
    if not chunks:
        state = jnp.zeros(plan.state_type.shape, F32)
    total_parts = sum(STUDENT_PARTS)
    parts = STUDENT_PARTS if plan.steps % total_parts == 0 else (1,)
    unit = plan.steps // sum(parts)
    network = Reduction(chip, chips, seq_count)
    wholes, start, total, sent, count = [], 0, None, None, 0
    for index, part in enumerate(parts):
        steps = part * unit
        grads = plan.student(
            start, steps, chips, place, q, kv, chunk_keys, chunks, mixes, levels, slopes, wide_t, keys_t, feat_q, feat_k, state
        )
        start += steps
        grads, sent = lax.optimization_barrier((grads, sent))
        if sent is not None:
            total = network.received(sent, count, wholes)
        if index + 1 < len(parts):
            place, grads, total = lax.optimization_barrier((place, grads, total))
        sent, count = network.send(grads, total), 0 if total is None else total.shape[0]
    total = network.received(sent, count, wholes)
    network.received(network.send(None, total), total.shape[0], wholes)
    results = []
    for whole in wholes:
        whole = whole.reshape((-1,) + grads.shape[1:])
        results.append((whole, lax.ppermute(whole, "seq", core_route)))
    own = jnp.concatenate([pair[0] for pair in results], axis=0)
    other = jnp.concatenate([pair[1] for pair in results], axis=0)
    both = jnp.where(
        first, jnp.concatenate((own, other), axis=0), jnp.concatenate((other, own), axis=0)
    ).astype(F32)
    return both[:, 0], both[:, 1]


class Reduction:
    def __init__(self, chip, chips, seq_count):
        self.chip, self.chips, self.seq_count = chip, chips, seq_count

    def route(self, distance):
        count = self.seq_count
        return [(i, (i + CORES * distance) % count) for i in range(count)]

    def send(self, grads, total):
        sent = []
        for distance in range(self.chips):
            part = None
            if grads is not None:
                flat = grads.reshape(-1, grads.shape[-1])
                share = flat.shape[0] // self.chips
                place = (self.chip + distance) % self.chips
                part = lax.dynamic_slice_in_dim(flat, place * share, share, 0)
            block = jnp.concatenate([x for x in (total, part) if x is not None], axis=0)
            if distance:
                block = lax.ppermute(block, "seq", self.route(distance))
            sent.append(block)
        return sent

    def received(self, sent, count, wholes):
        if count:
            parts = [block[:count] for block in sent]
            order = jnp.concatenate(parts[::-1] + parts[:0:-1], axis=0)
            first = (self.chips - 1 - self.chip) * count
            wholes.append(lax.dynamic_slice_in_dim(order, first, self.chips * count, 0))
        if sent[0].shape[0] == count:
            return None
        return functools.reduce(
            jnp.add, [block[count:].astype(F32) for block in sent]
        ).astype(BF16)


def solution(mesh):
    return jax.shard_map(
        body,
        mesh=mesh,
        in_specs=(
            P("seq", "head"),
            P("seq", "head"),
            P("seq", "head"),
            P("head", None, None),
            P("head", None, None),
        ),
        out_specs=(P("head", None, None), P("head", None, None)),
        check_vma=False,
    )
```

```python
import functools
import math

import jax
import jax.numpy as jnp
from jax import lax
from jax.experimental import pallas as pl
from jax.experimental.pallas import tpu as pltpu
from jax.sharding import PartitionSpec as P

HEADS = 128
KV_HEADS = 8
CORES = 2
SUBLANES = 8
BLOCK_HEADS = 4
STUDENT_PARTS = (2, 1, 1)
LOCAL_WINDOW = 2
CHUNK_WINDOW = 2
UNIT_WINDOW = 8
LOG2E = math.log2(math.e)
MASKED_SCORE = -1e30
TINY_DECAY = 2.0**-11
SAFE_LOW = 2.0**-100
SAFE_HIGH = 2.0**120
VMEM_BYTES = 56 * 1024 * 1024
F32 = jnp.float32
BF16 = jnp.bfloat16

NN = (((1,), (0,)), ((), ()))
NT = (((1,), (1,)), ((), ()))
TN = (((0,), (0,)), ((), ()))


def dot(a, b, form):
    return lax.dot_general(a, b, form, preferred_element_type=F32)


def from_partner(block, axis, stride):
    count = lax.axis_size(axis)
    route = []
    for low in range(count):
        high = low | 1 << stride
        if high != low and high < count:
            route += [(low, high), (high, low)]
    return lax.ppermute(block, axis, route)


def tile_of(rows):
    return 256 if rows % 256 == 0 else rows


def with_ones(values):
    return jnp.concatenate((values, jnp.ones_like(values)), axis=1)


def turned(block):
    return block.astype(F32).T.astype(BF16)


def turned_with_ones(values):
    return jnp.concatenate((turned(values), jnp.ones((16, values.shape[0]), BF16)), axis=0)


def softplus_and_slope(pre):
    above, below = jnp.maximum(pre, 0.0), jnp.minimum(pre, 0.0)
    decay = jnp.exp(below - above)
    log_term = jnp.where(decay < TINY_DECAY, decay, jnp.log(1.0 + decay))
    return (above + log_term).astype(BF16), jnp.exp(below - log_term).astype(BF16)


def masked(mask, block, other):
    return block if mask is True else jnp.where(mask, block, other)


def columns(index, width):
    return slice(index * width, (index + 1) * width)


def causal_mask(rows):
    return lax.broadcasted_iota(jnp.int32, (rows, rows), 0) >= lax.broadcasted_iota(
        jnp.int32, (rows, rows), 1
    )


def interleave(tasks, window):
    waiting, active = list(tasks), []
    while waiting or active:
        if waiting and len(active) < window:
            active.append(waiting.pop(0))
        for task in active[::-1]:
            if next(task, active) is active:
                active.remove(task)


def mixture_task(scale, score_parts, values_t, unit, store):
    parts = score_parts(unit)
    yield
    weights = [masked(mask, jnp.exp2(part * scale), 0.0).astype(BF16) for part, mask in parts]
    weights = weights[0] if len(weights) == 1 else jnp.concatenate(weights, axis=0)
    store(unit, dot(values_t[:, : weights.shape[0]], weights, NN))


def attend(scale, causal, tile, q_ref, k_ref, score_parts, values_t, mix_ref, level_ref, others, window):
    rows, width = k_ref.shape
    heads = q_ref.shape[1] // width
    units = [(b, i) for i in range(rows // tile) for b in range(heads)]
    totals = []

    def store(unit, mixed):
        b, i = unit
        total = mixed[width : width + 1]
        mix_ref[columns(b, width), columns(i, tile)] = (mixed[:width] * (1.0 / total)).astype(BF16)
        level_ref[0, b : b + 1, columns(i, tile)] = jnp.log2(total)
        totals.append(total)

    spread, count = [], len(units)
    for place, unit in enumerate(units):
        spread += others[place * len(others) // count : (place + 1) * len(others) // count]
        spread.append(mixture_task(scale, score_parts, values_t, unit, store))
    interleave(spread, window)
    low = jnp.min(functools.reduce(jnp.minimum, totals))
    high = jnp.max(functools.reduce(jnp.maximum, totals))

    def shifted(index, carry):
        b, i = index % heads, index // heads
        here = pl.ds(pl.multiple_of(i * tile, tile), tile)
        head = pl.ds(pl.multiple_of(b * width, width), width)
        scores = dot(k_ref[...], q_ref[here, head], NT) * scale
        mask = True
        if causal:
            mask = lax.broadcasted_iota(jnp.int32, scores.shape, 0) <= i * tile + (
                lax.broadcasted_iota(jnp.int32, scores.shape, 1)
            )
        peak = jnp.max(masked(mask, scores, MASKED_SCORE), axis=0, keepdims=True)
        weights = masked(mask, jnp.exp2(scores - peak), 0.0).astype(BF16)
        mixed = dot(values_t[...], weights, NN)
        total = mixed[width : width + 1]
        mix_ref[head, here] = (mixed[:width] * (1.0 / total)).astype(BF16)
        level_ref[0, pl.ds(b, 1), here] = peak + jnp.log2(total)
        return carry

    @pl.when(jnp.logical_not((low > SAFE_LOW) & (high < SAFE_HIGH)))
    def _():
        lax.fori_loop(0, count, shifted, 0)


def local_attention(
    scale, group_steps, place_ref, own_ref, other_ref, k_ref, v_ref, q_ref, mix_ref, level_ref, turned_ref, keys_t
):
    rows, width = k_ref.shape
    heads = q_ref.shape[1] // width
    part = own_ref.shape[0]
    core = place_ref[1]
    q_ref[pl.ds(pl.multiple_of(core * part, part), part), :] = own_ref[...]
    q_ref[pl.ds(pl.multiple_of((1 - core) * part, part), part), :] = other_ref[...]
    @pl.when(pl.program_id(0) % group_steps == 0)
    def _():
        turned_ref[...] = turned_with_ones(v_ref[...])
        keys_t[...] = turned(k_ref[...])

    tile = tile_of(rows)
    mask = lax.broadcasted_iota(jnp.int32, (tile, tile), 0) <= lax.broadcasted_iota(
        jnp.int32, (tile, tile), 1
    )

    def score_parts(unit):
        b, i = unit
        query = q_ref[columns(i, tile), columns(b, width)]
        last = (dot(k_ref[columns(i, tile), :], query, NT), mask)
        return [last] if i == 0 else [(dot(k_ref[: i * tile, :], query, NT), True), last]

    attend(
        scale,
        True,
        tile,
        q_ref,
        k_ref,
        score_parts,
        turned_ref,
        mix_ref,
        level_ref,
        [],
        LOCAL_WINDOW,
    )


def chunk_block(
    scale, group_steps, q_ref, k_ref, v_ref, wk_ref, state_of, outs
):
    mix_ref, level_ref, slope_ref, state_ref, keys_t, turned_ref = outs
    rows, width = k_ref.shape
    heads = q_ref.shape[1] // width
    pairs = heads // 2

    @pl.when(pl.program_id(0) % group_steps == 0)
    def _():
        turned_ref[...] = turned_with_ones(v_ref[...])
        keys_t[...] = turned(k_ref[...])

    tile = rows
    keys = k_ref[...]

    def feature_task(pair):
        weight = jnp.concatenate((wk_ref[2 * pair], wk_ref[2 * pair + 1]), axis=1)
        pre = dot(keys, weight, NN)
        yield
        feat, slope = softplus_and_slope(pre)
        slope_ref[:, columns(pair, 2 * width)] = slope
        state_ref[pair] = state_of(pair) + dot(turned_ref[...], feat, NN)

    def score_parts(unit):
        b, i = unit
        return [(dot(keys, q_ref[columns(i, tile), columns(b, width)], NT), True)]

    features = [feature_task(pair) for pair in range(pairs)]
    attend(
        scale,
        False,
        tile,
        q_ref,
        k_ref,
        score_parts,
        turned_ref,
        mix_ref,
        level_ref,
        features,
        CHUNK_WINDOW,
    )


def chunk_attention(scale, group_steps, place_ref, q_ref, k_ref, v_ref, wk_ref, *outs):
    mix_ref, level_ref, slope_ref, state_ref, keys_t, _ = outs

    @pl.when(place_ref[0] < 1)
    def _():
        mix_ref[...] = jnp.zeros_like(mix_ref)
        slope_ref[...] = jnp.zeros_like(slope_ref)
        level_ref[...] = jnp.full_like(level_ref, MASKED_SCORE)
        state_ref[...] = jnp.zeros_like(state_ref)
        keys_t[...] = jnp.zeros_like(keys_t)

    @pl.when(place_ref[0] >= 1)
    def _():
        chunk_block(scale, group_steps, q_ref, k_ref, v_ref, wk_ref, lambda pair: 0.0, outs)


def student(scale, group_steps, total_tokens, chunk_count, place_ref, q_ref, k_ref, v_ref, *refs):
    refs = list(refs)
    done = min(chunk_count, 1)
    chunk_keys = [refs.pop(0) for _ in range(chunk_count - done)]
    chunk_values = [refs.pop(0) for _ in range(chunk_count)]
    mix_refs = [refs.pop(0) for _ in range(done + 1)]
    level_refs = [refs.pop(0) for _ in range(done + 1)]
    slope_refs = [refs.pop(0) for _ in range(done)]
    chunk_keys_t = [refs.pop(0) for _ in range(done)]
    wide_t, keys_t, wq_ref, wk_ref, state_in, out_ref, wk_acc, state_ref = refs[:8]
    refs = refs[8:]
    state_ref[...] = state_in[...]
    for c in range(done, chunk_count):
        own = [refs.pop(0) for _ in range(5)]
        mix, level, slope, turned_keys, turned_values = own
        mix_refs.append(mix)
        level_refs.append(level)
        slope_refs.append(slope)
        chunk_keys_t.append(turned_keys)

        @pl.when(place_ref[0] < c + 1)
        def _(mix=mix, level=level):
            mix[...] = jnp.zeros_like(mix)
            level[...] = jnp.full_like(level, MASKED_SCORE)

        @pl.when(place_ref[0] >= c + 1)
        def _(c=c, own=own):
            chunk_block(
                scale,
                group_steps,
                q_ref,
                chunk_keys[c - done],
                chunk_values[c],
                wk_ref,
                lambda pair: state_ref[pair],
                (*own[:3], state_ref, *own[3:]),
            )

    rows, width = k_ref.shape
    heads = q_ref.shape[1] // width
    pairs = heads // 2
    tile = tile_of(rows)
    tiles = rows // tile
    mask = causal_mask(tile).astype(F32).astype(BF16)

    head_list = range(heads)
    tile_list = range(tiles)
    wide = [with_ones(v_ref[columns(i, tile), :]) for i in tile_list]
    key_feat, key_slope, states, shares = {}, {}, {}, {}

    def key_task(pair):
        weight = jnp.concatenate((wk_ref[2 * pair], wk_ref[2 * pair + 1]), axis=1)
        running = state_ref[pair]
        pre = dot(k_ref[columns(0, tile), :], weight, NN)
        for i in tile_list:
            yield
            later = dot(k_ref[columns(i + 1, tile), :], weight, NN) if i + 1 < tiles else None
            feat, slope = softplus_and_slope(pre)
            pre = later
            key_slope[pair, i] = slope
            for side in range(2):
                here = columns(side, width)
                key_feat[2 * pair + side, i] = feat[:, here]
                norm = jnp.broadcast_to(running[width : width + 1, here], (width, width))
                states[2 * pair + side, i] = jnp.concatenate(
                    (running[:width, here], norm), axis=0
                ).astype(BF16)
            if i + 1 < tiles:
                running = running + dot(wide_t[:, columns(i, tile)], feat, NN)

    def share_task(i):
        levels = [ref[0, :, columns(i, tile)] for ref in level_refs]
        peak = functools.reduce(jnp.maximum, levels)
        parts = [jnp.exp2(level - peak) for level in levels]
        inverse = 1.0 / functools.reduce(jnp.add, parts)
        shares[i] = [part * inverse for part in parts]
        yield

    interleave([key_task(pair) for pair in range(pairs)] + [share_task(i) for i in tile_list], 4)

    backs, query_change, key_change = {}, {}, {}

    def unit_task(b, i):
        here, head = columns(i, tile), columns(b, width)
        pre = dot(q_ref[here, head], wq_ref[b], NN)
        yield
        feat, slope = softplus_and_slope(pre)
        affinity = dot(feat, key_feat[b, i], NT)
        mixed = dot(feat, states[b, i], NT)
        yield
        affinity = affinity.astype(BF16) * mask
        mixed = mixed + dot(affinity, wide[i], NN)
        teacher = functools.reduce(
            jnp.add,
            [
                share[b : b + 1] * ref[head, here].astype(F32)
                for share, ref in zip(shares[i], mix_refs)
            ],
        )
        teacher = turned(teacher).astype(F32)
        yield
        inverse = 1.0 / mixed[:, width:]
        result = mixed[:, :width] * inverse
        grad_out = (result - teacher) * (2.0 / total_tokens)
        grad_denom = jnp.sum(grad_out * result, axis=1, keepdims=True) * inverse * (-1.0 / width)
        grads = jnp.concatenate((grad_out * inverse, grad_denom), axis=1).astype(BF16)
        grad_aff = dot(grads, wide[i], NT)
        backs[b, i] = dot(feat, grads, TN)
        yield
        grad_aff = grad_aff.astype(BF16) * mask
        grad_qfeat = dot(
            jnp.concatenate((grads, grad_aff), axis=1),
            jnp.concatenate((states[b, i], key_feat[b, i]), axis=0),
            NN,
        )
        key_change[b, i] = dot(grad_aff, feat, TN)
        yield
        query_change[b, i] = grad_qfeat.astype(BF16) * slope

    interleave([unit_task(b, i) for b in head_list for i in tile_list], UNIT_WINDOW)

    whole = [None] * pairs

    def query_weight_task(b):
        change = jnp.concatenate([query_change[b, i] for i in tile_list], axis=0)
        out_ref[b, 0] = dot(q_ref[:, columns(b, width)], change, TN).astype(out_ref.dtype)
        yield

    def key_weight_task(pair):
        sides = (2 * pair, 2 * pair + 1)
        running = [backs[b, tiles - 1] for b in sides]
        changes = [None] * tiles
        for i in reversed(tile_list):
            both = jnp.concatenate([key_change[b, i] for b in sides], axis=1)
            if i + 1 < tiles:
                later = jnp.concatenate(running, axis=0).astype(BF16)
                both = both + dot(wide[i], later, NT)
                running = [old + backs[b, i] for old, b in zip(running, sides)]
                yield
            changes[i] = both.astype(BF16) * key_slope[pair, i]
        whole[pair] = jnp.concatenate(running, axis=0).astype(BF16)
        wk_acc[pair] = dot(keys_t[...], jnp.concatenate(changes, axis=0), NN)

    tasks = []
    for pair in range(pairs):
        tasks += [query_weight_task(2 * pair), query_weight_task(2 * pair + 1)]
        tasks.append(key_weight_task(pair))
    interleave(tasks, 3)

    for c in range(chunk_count):

        @pl.when(place_ref[0] >= c + 1)
        def _(c=c):
            values = with_ones(chunk_values[c][...])
            sums = [None] * pairs

            def chunk_task(pair, i):
                here = columns(i, tile)
                slope = slope_refs[c][here, columns(pair, 2 * width)]
                change = dot(values[here], whole[pair], NT)
                yield
                change = change.astype(BF16) * slope
                term = dot(chunk_keys_t[c][:, here], change, NN)
                sums[pair] = term if i == 0 else sums[pair] + term
                if i == tiles - 1:
                    wk_acc[pair] += sums[pair]

            interleave([chunk_task(pair, i) for pair in range(pairs) for i in tile_list], 2)

    for b in head_list:
        out_ref[b, 1] = wk_acc[b // 2][:, columns(b % 2, width)].astype(out_ref.dtype)


def params():
    return pltpu.CompilerParams(
        vmem_limit_bytes=VMEM_BYTES, dimension_semantics=("arbitrary",)
    )


def cost(microseconds):
    return pl.CostEstimate(
        flops=int(microseconds * 1e9), bytes_accessed=int(microseconds * 3e6), transcendentals=0
    )


class Plan:
    def __init__(self, rows, half, groups, width, feats):
        self.rows, self.half, self.groups, self.width, self.feats = rows, half, groups, width, feats
        self.per_group = half // groups
        self.heads = math.gcd(self.per_group, BLOCK_HEADS)
        self.steps = half // self.heads
        self.mix_type = jax.ShapeDtypeStruct((half * width, rows), BF16)
        self.q_type = jax.ShapeDtypeStruct((rows, half * width), BF16)
        self.level_type = jax.ShapeDtypeStruct((self.steps, SUBLANES, rows), F32)
        self.state_type = jax.ShapeDtypeStruct((half // 2, width + 16, 2 * feats), F32)

    def turned_type(self, height):
        return jax.ShapeDtypeStruct((height * self.groups, self.rows), BF16)

    def specs(self, start=0):
        rows, width, heads, steps = self.rows, self.width, self.heads, self.steps
        groups, per_group = self.groups, self.per_group
        return dict(
            q=pl.BlockSpec((rows, heads * width), lambda h, *_: (0, start + h)),
            k=pl.BlockSpec((rows, width), lambda h, *_: (0, (start + h) * heads // per_group)),
            v=pl.BlockSpec(
                (rows, width), lambda h, *_: (0, groups + (start + h) * heads // per_group)
            ),
            mix=pl.BlockSpec((heads * width, rows), lambda h, *_: (start + h, 0)),
            wide_t=pl.BlockSpec((width + 16, rows), lambda h, *_: ((start + h) * heads // per_group, 0)),
            keys_t=pl.BlockSpec((width, rows), lambda h, *_: ((start + h) * heads // per_group, 0)),
            level=pl.BlockSpec((1, SUBLANES, rows), lambda h, *_: (start + h, 0, 0)),
            w=pl.BlockSpec(
                (heads, width, self.feats),
                lambda h, place: (place[1] * steps + start + h, 0, 0),
            ),
            state=pl.BlockSpec(
                (heads // 2, width + 16, 2 * self.feats), lambda h, *_: (start + h, 0, 0)
            ),
        )

    def local(self, place, queries, other_q, kv):
        at, steps = self.specs(), self.steps
        part, block = queries.shape[0], self.heads * self.width
        return pl.pallas_call(
            functools.partial(
                local_attention, self.width ** (-0.5) * LOG2E, self.per_group // self.heads
            ),
            grid_spec=pltpu.PrefetchScalarGridSpec(
                num_scalar_prefetch=1,
                grid=(steps,),
                in_specs=[
                    pl.BlockSpec((part, block), lambda h, place: (0, place[1] * steps + h)),
                    pl.BlockSpec((part, block), lambda h, *_: (0, h)),
                    at["k"],
                    at["v"],
                ],
                out_specs=[at["q"], at["mix"], at["level"], at["wide_t"], at["keys_t"]],
            ),
            out_shape=[
                self.q_type,
                self.mix_type,
                self.level_type,
                self.turned_type(self.width + 16),
                self.turned_type(self.width),
            ],
            compiler_params=params(),
            cost_estimate=cost(12),
            name="local_attention",
        )(place, queries, other_q, kv, kv)

    def chunk(self, place, q, chunk, feat_k):
        at = self.specs()
        return pl.pallas_call(
            functools.partial(
                chunk_attention,
                self.width ** (-0.5) * LOG2E,
                self.per_group // self.heads,
            ),
            grid_spec=pltpu.PrefetchScalarGridSpec(
                num_scalar_prefetch=1,
                grid=(self.steps,),
                in_specs=[at["q"], at["k"], at["v"], at["w"]],
                out_specs=[at["mix"], at["level"], at["q"], at["state"], at["keys_t"]],
                scratch_shapes=[pltpu.VMEM((self.width + 16, self.rows), BF16)],
            ),
            out_shape=[
                self.mix_type,
                self.level_type,
                self.q_type,
                self.state_type,
                self.turned_type(self.width),
            ],
            compiler_params=params(),
            cost_estimate=cost(18),
            name="chunk_attention",
        )(place, q, chunk, chunk, feat_k)

    def student(
        self,
        start,
        steps,
        chips,
        place,
        q,
        kv,
        chunk_keys,
        chunks,
        mixes,
        levels,
        slopes,
        wide_t,
        keys_t,
        wq,
        wk,
        state,
    ):
        at = self.specs(start)
        count, width, rows = len(chunks), self.width, self.rows
        grad_shape = (self.heads, 2, width, self.feats)
        done = len(slopes)
        return pl.pallas_call(
            functools.partial(
                student,
                width ** (-0.5) * LOG2E,
                self.per_group // self.heads,
                chips * rows,
                count,
            ),
            grid_spec=pltpu.PrefetchScalarGridSpec(
                num_scalar_prefetch=1,
                grid=(steps,),
                in_specs=[at["q"], at["k"], at["v"]]
                + [at["k"]] * (count - done)
                + [at["v"]] * count
                + [at["mix"]] * len(mixes)
                + [at["level"]] * len(levels)
                + [at["q"]] * done
                + [at["keys_t"]] * done
                + [at["wide_t"], at["keys_t"], at["w"], at["w"], at["state"]],
                out_specs=pl.BlockSpec(grad_shape, lambda h, *_: (h, 0, 0, 0)),
                scratch_shapes=[
                    pltpu.VMEM((self.heads // 2, width, 2 * self.feats), F32),
                    pltpu.VMEM((self.heads // 2, width + 16, 2 * self.feats), F32),
                ]
                + [
                    pltpu.VMEM((self.heads * width, rows), BF16),
                    pltpu.VMEM((1, SUBLANES, rows), F32),
                    pltpu.VMEM((rows, self.heads * width), BF16),
                    pltpu.VMEM((width, rows), BF16),
                    pltpu.VMEM((width + 16, rows), BF16),
                ]
                * (count - done),
            ),
            out_shape=jax.ShapeDtypeStruct((steps * self.heads,) + grad_shape[1:], BF16),
            compiler_params=params(),
            cost_estimate=cost(20 * steps),
            name="student",
        )(
            place, q, kv, kv, *chunks[done:], *chunks, *mixes, *levels, *slopes, *chunk_keys, wide_t, keys_t, wq, wk, state
        )


def body(queries, keys, values, feat_q, feat_k):
    row_count = queries.shape[0]
    heads_here, width, feat_count = feat_q.shape
    seq_count = lax.axis_size("seq")
    chips = seq_count // CORES
    seq_place = lax.axis_index("seq")
    core, chip = seq_place % CORES, seq_place // CORES
    head_place = lax.axis_index("head")
    spread = max(1, HEADS // KV_HEADS // heads_here)
    key_value = jnp.stack((keys, values))
    for bit_index in range(spread.bit_length() - 1):
        partner = from_partner(key_value, "head", bit_index)
        upper_half = head_place // (1 << bit_index) % 2 == 1
        key_value = jnp.where(
            upper_half,
            jnp.concatenate((partner, key_value), axis=2),
            jnp.concatenate((key_value, partner), axis=2),
        )
    groups = key_value.shape[2] // width
    half = heads_here // CORES
    core_route = [(i, i ^ 1) for i in range(seq_count)]
    first = core == 0

    if groups > 1:
        own_groups = groups // CORES
        split = own_groups * width
        low, high = key_value[:, :, :split], key_value[:, :, split:]
        kept, sent = jnp.where(first, low, high), jnp.where(first, high, low)
    else:
        own_groups = groups
        kept = sent = key_value
    got = lax.ppermute(sent, "seq", core_route)
    sent_q = lax.dynamic_slice_in_dim(queries, (1 - core) * half * width, half * width, 1)
    sent_q, got = lax.optimization_barrier((sent_q, got))
    other_q = lax.ppermute(sent_q, "seq", core_route)
    kv = jnp.where(
        first, jnp.concatenate((kept, got), axis=1), jnp.concatenate((got, kept), axis=1)
    )
    kv = jnp.concatenate((kv[0], kv[1]), axis=1)
    rows = CORES * row_count
    chunks = []
    for distance in range(1, chips):
        route = [(i, i + CORES * distance) for i in range(seq_count - CORES * distance)]
        chunks.append(lax.ppermute(kv, "seq", route))

    plan = Plan(rows, half, own_groups, width, feat_count)
    place = jnp.stack((chip, core)).astype(jnp.int32)
    q, mix, level, wide_t, keys_t = plan.local(place, queries, other_q, kv)
    mixes, levels, slopes, chunk_keys = [mix], [level], [], []
    for chunk in chunks[:1]:
        mix, level, slope, state, turned_keys = plan.chunk(place, q, chunk, feat_k)
        mixes.append(mix)
        levels.append(level)
        slopes.append(slope)
        chunk_keys.append(turned_keys)
    if not chunks:
        state = jnp.zeros(plan.state_type.shape, F32)
    total_parts = sum(STUDENT_PARTS)
    parts = STUDENT_PARTS if plan.steps % total_parts == 0 else (1,)
    unit = plan.steps // sum(parts)
    network = Reduction(chip, chips, seq_count)
    wholes, start, total, sent, count = [], 0, None, None, 0
    for index, part in enumerate(parts):
        steps = part * unit
        grads = plan.student(
            start, steps, chips, place, q, kv, chunk_keys, chunks, mixes, levels, slopes, wide_t, keys_t, feat_q, feat_k, state
        )
        start += steps
        grads, sent = lax.optimization_barrier((grads, sent))
        if sent is not None:
            total = network.received(sent, count, wholes)
        if index + 1 < len(parts):
            place, grads, total = lax.optimization_barrier((place, grads, total))
        sent, count = network.send(grads, total), 0 if total is None else total.shape[0]
    total = network.received(sent, count, wholes)
    network.received(network.send(None, total), total.shape[0], wholes)
    results = []
    for whole in wholes:
        whole = whole.reshape((-1,) + grads.shape[1:])
        results.append((whole, lax.ppermute(whole, "seq", core_route)))
    own = jnp.concatenate([pair[0] for pair in results], axis=0)
    other = jnp.concatenate([pair[1] for pair in results], axis=0)
    both = jnp.where(
        first, jnp.concatenate((own, other), axis=0), jnp.concatenate((other, own), axis=0)
    ).astype(F32)
    return both[:, 0], both[:, 1]


class Reduction:
    def __init__(self, chip, chips, seq_count):
        self.chip, self.chips, self.seq_count = chip, chips, seq_count

    def route(self, distance):
        count = self.seq_count
        return [(i, (i + CORES * distance) % count) for i in range(count)]

    def send(self, grads, total):
        sent = []
        for distance in range(self.chips):
            part = None
            if grads is not None:
                flat = grads.reshape(-1, grads.shape[-1])
                share = flat.shape[0] // self.chips
                place = (self.chip + distance) % self.chips
                part = lax.dynamic_slice_in_dim(flat, place * share, share, 0)
            block = jnp.concatenate([x for x in (total, part) if x is not None], axis=0)
            if distance:
                block = lax.ppermute(block, "seq", self.route(distance))
            sent.append(block)
        return sent

    def received(self, sent, count, wholes):
        if count:
            parts = [block[:count] for block in sent]
            order = jnp.concatenate(parts[::-1] + parts[:0:-1], axis=0)
            first = (self.chips - 1 - self.chip) * count
            wholes.append(lax.dynamic_slice_in_dim(order, first, self.chips * count, 0))
        if sent[0].shape[0] == count:
            return None
        return functools.reduce(
            jnp.add, [block[count:].astype(F32) for block in sent]
        ).astype(BF16)


def solution(mesh):
    return jax.shard_map(
        body,
        mesh=mesh,
        in_specs=(
            P("seq", "head"),
            P("seq", "head"),
            P("seq", "head"),
            P("head", None, None),
            P("head", None, None),
        ),
        out_specs=(P("head", None, None), P("head", None, None)),
        check_vma=False,
    )
```
